128 devices in a mesh: grp: 8 (over z, core), rep: 16 (over x, y).
Axes of the slice: x: 4, y: 4, z: 4, core: 2. Of those that a mesh axis runs over, the one named last changes fastest.
Arguments:
- queries: bfloat16 [32768, 1024], P(('grp', 'rep')), may hold values from -24 to 24
- passages: bfloat16 [32768, 1024], P(('grp', 'rep')), may hold values from -24 to 24
- neg_device: int32 [32768, 7], P(('grp', 'rep')), may hold values from 0 to 127, as said below
- neg_row: int32 [32768, 7], P(('grp', 'rep')), may hold values from 0 to 255
Outputs:
- losses: float32 [32768], P(('grp', 'rep'))
- grad_queries: bfloat16 [32768, 1024], P(('grp', 'rep'))
- grad_passages: bfloat16 [32768, 1024], P(('grp', 'rep'))
The draws below stay inside these ranges and needn't reach their ends.
Inputs may be any that keep to these rules, and one draw needn't show every extreme that they name: `neg_device`: the 7 hard negatives of one query lie on different devices. The 256 queries of one device name any one device at most 16 times (some devices not at all); there is one device that the queries of every device name exactly 16 times.
All inputs are finite; a program needn't handle non-finite values.
Results may differ from the reference program's by a relative error of at most 0.015.
Values may be sent and summed in bfloat16 or wider, within the bound.
No kernel may reach another device: no remote copies, remote signals or barrier semaphores. Data moves between devices by JAX's collectives and lax.ppermute only.
A program may use at most 128 MiB of HBM per device.

```python
import math
import jax
import jax.numpy as jnp
from jax import lax

E = 1024
NEG = 7
TOK_DEV = 256
TOKENS = 32768
CAP = 16
N_GRP = 8
N_REP = 16
DEVICES = 128


passage_scale = 0.5


positive_logit = 9.0


hard_logit = 7.0


copy_logit = 7.5


noise_level = 0.05


def shared_base(key):
    return jax.random.normal(jax.random.fold_in(key, 101), (TOKENS, E), jnp.float32)


def passage_field(base_rows, copy_weight):
    near_step = N_REP * TOK_DEV
    far_step = N_GRP // 2 * N_REP * TOK_DEV
    copies = jnp.roll(base_rows, -near_step, axis=0) + jnp.roll(base_rows, near_step, axis=0) + jnp.roll(base_rows, -far_step, axis=0)
    return passage_scale * (base_rows + copy_weight * copies)


def hard_pairs(key):
    slot_total = DEVICES * CAP
    request_total = TOK_DEV * NEG
    device_rank = jax.random.permutation(jax.random.fold_in(key, 201), DEVICES).astype(jnp.int32)
    jitter = jax.random.randint(jax.random.fold_in(key, 202), (DEVICES, DEVICES, 1), 0, max(2, DEVICES // 4)).astype(jnp.int32)
    slot_number = jnp.arange(CAP, dtype=jnp.int32)[None, None, :]
    rank_cube = device_rank[None, :, None]
    weight = rank_cube + DEVICES // 2 + jitter
    priority = (slot_number + 1) * weight
    priority = jnp.where(rank_cube == 0, -1, priority)
    order_key = (priority * slot_total + rank_cube * CAP + slot_number).reshape(DEVICES, slot_total)
    ordering = jnp.argsort(order_key, axis=1)
    chosen = jnp.sort(ordering[:, :request_total], axis=1).astype(jnp.int32)
    owners = chosen // CAP
    dev_table = jnp.transpose(owners.reshape(DEVICES, NEG, TOK_DEV), (0, 2, 1))
    shuffle_keys = jax.random.split(jax.random.fold_in(key, 203), DEVICES)
    row_order = jax.vmap(lambda single: jax.random.permutation(single, TOK_DEV))(shuffle_keys).astype(jnp.int32)
    dev_table = jnp.take_along_axis(dev_table, row_order[:, :, None], axis=1)
    rotation = (jnp.arange(TOK_DEV, dtype=jnp.int32)[:, None] + jnp.arange(NEG, dtype=jnp.int32)[None, :]) % NEG
    rotation = jnp.broadcast_to(rotation[None, :, :], (DEVICES, TOK_DEV, NEG))
    dev_table = jnp.take_along_axis(dev_table, rotation, axis=2).reshape(TOKENS, NEG).astype(jnp.int32)
    first_pick = jax.random.randint(jax.random.fold_in(key, 204), (TOKENS, NEG), 0, TOK_DEV)
    second_pick = jax.random.randint(jax.random.fold_in(key, 205), (TOKENS, NEG), 0, TOK_DEV)
    third_pick = jax.random.randint(jax.random.fold_in(key, 206), (TOKENS, NEG), 0, TOK_DEV)
    row_picks = jnp.minimum(jnp.minimum(first_pick, second_pick), third_pick).astype(jnp.int32)
    perm_keys = jax.random.split(jax.random.fold_in(key, 207), DEVICES)
    row_perm = jax.vmap(lambda single: jax.random.permutation(single, TOK_DEV))(perm_keys).astype(jnp.int32)
    row_table = row_perm[dev_table, row_picks].astype(jnp.int32)
    return (dev_table, row_table)


def draw_queries(key, part):
    base_rows = shared_base(key)
    dev_table, row_table = hard_pairs(key)
    key = jax.random.fold_in(key, 7)
    noise_rows = jax.random.normal(jax.random.fold_in(key, 104), (TOKENS, E), jnp.float32)
    flat_index = (dev_table * TOK_DEV + row_table).astype(jnp.int32)
    neg_sum = jnp.zeros((TOKENS, E), jnp.float32)
    for column in range(NEG):
        neg_sum = neg_sum + jnp.take(base_rows, flat_index[:, column], axis=0)
    logit_unit = 3.0 * math.sqrt(E)
    mixture = (positive_logit / logit_unit * base_rows + hard_logit / logit_unit * neg_sum + noise_level * noise_rows) / passage_scale
    return jnp.clip(mixture, -24.0, 24.0).astype(jnp.bfloat16)


def draw_passages(key, part):
    base_rows = shared_base(key)
    full_rows = passage_field(base_rows, copy_logit / positive_logit)
    return jnp.clip(full_rows, -24.0, 24.0).astype(jnp.bfloat16)


def draw_neg_device(key, part):
    dev_table, row_table = hard_pairs(key)
    return dev_table


def draw_neg_row(key, part):
    dev_table, row_table = hard_pairs(key)
    return row_table


def setup_inputs(seed: int = 0) -> dict:
    arg_keys = jax.random.split(jax.random.key(seed), 5)
    return {
        "queries": draw_queries(jax.random.fold_in(arg_keys[4], 71), 0),
        "passages": draw_passages(jax.random.fold_in(arg_keys[4], 71), 0),
        "neg_device": draw_neg_device(jax.random.fold_in(arg_keys[4], 71), 0),
        "neg_row": draw_neg_row(jax.random.fold_in(arg_keys[4], 71), 0),
    }


def reference(queries, passages, neg_device, neg_row):
    tok_rows = TOK_DEV
    groups = N_GRP
    replicas = N_REP
    emb_width = E
    neg_count = NEG
    group_rows = groups * tok_rows
    temper = 3.0 / math.sqrt(emb_width)
    global_index = (neg_device * tok_rows + neg_row).astype(jnp.int32)

    def regroup(array):
        tail = array.shape[1:]
        shaped = array.reshape((groups, replicas, tok_rows) + tail)
        shaped = jnp.swapaxes(shaped, 0, 1)
        return shaped.reshape((replicas, group_rows) + tail)

    def ungroup(array):
        tail = array.shape[2:]
        shaped = array.reshape((replicas, groups, tok_rows) + tail)
        shaped = jnp.swapaxes(shaped, 0, 1)
        return shaped.reshape((TOKENS,) + tail)

    def one_group(hard_sum, inputs):
        query_block, passage_block, index_block = inputs
        negatives = jnp.take(passages, index_block.reshape(-1), axis=0).reshape(group_rows, neg_count, emb_width)
        scores = temper * jnp.dot(query_block, passage_block.T, preferred_element_type=jnp.float32)
        hard_scores = temper * jnp.einsum('qe,qke->qk', query_block.astype(jnp.float32), negatives.astype(jnp.float32))
        row_top = jnp.maximum(lax.optimization_barrier(jnp.max(scores, axis=1)), lax.optimization_barrier(jnp.max(hard_scores, axis=1)))
        row_total = lax.optimization_barrier(jnp.sum(jnp.exp(scores - row_top[:, None]), axis=1)) + lax.optimization_barrier(jnp.sum(jnp.exp(hard_scores - row_top[:, None]), axis=1))
        log_total = row_top + jnp.log(row_total)
        group_losses = log_total - jnp.diagonal(scores)
        identity = jnp.eye(group_rows, dtype=jnp.float32)
        d_scores = (jnp.exp(scores - log_total[:, None]) - identity).astype(jnp.bfloat16)
        d_hard = jnp.exp(hard_scores - log_total[:, None]).astype(jnp.bfloat16)
        query_grads = temper * (jnp.dot(d_scores, passage_block, preferred_element_type=jnp.float32) + jnp.einsum('qk,qke->qe', d_hard.astype(jnp.float32), negatives.astype(jnp.float32)))
        query_grads = query_grads.astype(jnp.bfloat16)
        pieces = temper * jnp.einsum('gqp,gqe->gpe', d_scores.reshape(groups, tok_rows, group_rows).astype(jnp.float32), query_block.reshape(groups, tok_rows, emb_width).astype(jnp.float32))
        in_batch = lax.optimization_barrier(jnp.sum(pieces.astype(jnp.bfloat16).astype(jnp.float32), axis=0))
        hard_terms = (temper * d_hard.astype(jnp.float32)[:, :, None] * query_block.astype(jnp.float32)[:, None, :]).astype(jnp.bfloat16)
        hard_sum = hard_sum.at[index_block.reshape(-1)].add(hard_terms.reshape(-1, emb_width).astype(jnp.float32))
        return (hard_sum, (group_losses, query_grads, in_batch))
    start_sum = jnp.zeros((TOKENS, emb_width), jnp.float32)
    hard_sum, outputs = lax.scan(one_group, start_sum, (regroup(queries), regroup(passages), regroup(global_index)))
    group_losses, query_grads, in_batch = outputs
    losses = ungroup(group_losses)
    grad_queries = ungroup(query_grads)
    grad_passages = (ungroup(in_batch) + hard_sum).astype(jnp.bfloat16)
    return (losses, grad_queries, grad_passages)
```

```python
import functools
import math

import jax
import jax.numpy as jnp
from jax import lax
from jax.experimental import pallas as pl
from jax.experimental.pallas import tpu as pltpu
from jax.sharding import PartitionSpec as P

F32 = jnp.float32
BF16 = jnp.bfloat16
I32 = jnp.int32
LOW = -1e30
NT = (((1,), (1,)), ((), ()))
TN = (((0,), (0,)), ((), ()))
NN = (((1,), (0,)), ((), ()))
VMEM_LIMIT = 48 * 1024 * 1024


def mm(a, b, dims=NN, exact=False):
    return lax.dot_general(
        a, b, dims, precision=lax.Precision.HIGHEST if exact else None, preferred_element_type=F32
    )


def iota(shape, dim):
    return lax.broadcasted_iota(I32, shape, dim)


def slot_hits(v_ref, g, reps, cap, devices, toks):
    rows = reps * cap
    slot = iota((rows, devices), 0)
    pick = (iota((rows, devices), 1) == g * reps + slot // cap).astype(BF16)
    spread = mm(pick, v_ref[...])
    want = (iota((rows, toks), 0) % cap + 1).astype(F32)
    return pick, spread == want


def prep_kernel(reps, cap, nd_ref, nr_ref, q_ref, slots_ref, code_ref, v_ref, row_ref):
    g = pl.program_id(0)
    negs, toks = nd_ref.shape
    devices = v_ref.shape[0]

    @pl.when(g == 0)
    def _():
        dev = iota((devices, toks), 0)
        named = jnp.zeros((devices, toks), F32)
        rows = jnp.zeros((devices, toks), F32)
        for k in range(negs):
            hit = dev == nd_ref[k : k + 1, :]
            named = named + jnp.where(hit, 1.0, 0.0)
            rows = rows + jnp.where(hit, (nr_ref[k : k + 1, :] + 1).astype(F32), 0.0)
        before = (iota((toks, toks), 0) < iota((toks, toks), 1)).astype(BF16)
        rank = mm(named.astype(BF16), before)
        v_ref[...] = (named * (rank + 1.0)).astype(BF16)
        row_ref[...] = rows.astype(BF16)

    pick, hit = slot_hits(v_ref, g, reps, cap, devices, toks)
    wanted = mm(pick, row_ref[...])
    hot = hit.astype(BF16)
    slots_ref[...] = mm(hot, q_ref[...]).astype(BF16).reshape(slots_ref.shape)
    ids = mm(jnp.ones((8, toks), BF16), jnp.where(hit, wanted, 0.0).astype(BF16), NT)
    tok = mm(iota((8, toks), 1).astype(F32).astype(BF16), hot, NT)
    code = tok * 512.0 + ids
    code_ref[pl.ds(g, 1), :] = code[0:1, :].astype(I32)


def slot_codes(code_ref, g, reps, cap):
    code = code_ref[pl.ds(g, 1), :]
    ids = code & 511
    slots = code.shape[1]
    valid = ids > 0
    mine = iota((reps, slots), 1) // cap == iota((reps, slots), 0)
    return ids, code >> 9, valid, mine


def serve_kernel(
    reps, cap, temper, place_ref, code_ref, qr_ref, p_ref, q_ref,
    served_ref, hs_ref, part_ref, top, total, top_in, total_in,
):
    g = pl.program_id(0)
    groups = pl.num_programs(0)
    toks, width = q_ref.shape
    slots = reps * cap

    @pl.when(g == 0)
    def _():
        top[...] = jnp.full(top.shape, LOW, F32)
        total[...] = jnp.zeros(total.shape, F32)
        top_in[...] = jnp.full(top_in.shape, LOW, F32)
        total_in[...] = jnp.zeros(total_in.shape, F32)

    ids, tok, valid, mine = slot_codes(code_ref, g, reps, cap)
    passages = p_ref[...]
    asking = qr_ref[...].reshape(slots, width)
    hit = iota((toks, slots), 0) + 1 == ids
    served = mm(hit.astype(BF16), passages, TN).astype(BF16)
    served_ref[...] = served.reshape(served_ref.shape)
    cross = mm(passages, asking, NT)
    hs = temper * jnp.sum(jnp.where(hit, cross, 0.0), axis=0, keepdims=True)
    hs_ref[pl.ds(g, 1), :] = hs
    token = (iota((toks, slots), 0) == tok) & valid
    live = mine & valid
    value = mm(jnp.where(live, hs, 0.0), jnp.where(token, 1.0, 0.0), NT, exact=True)
    there = mm(live.astype(BF16), token.astype(BF16), NT) > 0.5
    value = jnp.where(there, value, LOW)
    new_top = jnp.maximum(top[...], value)
    total[...] = total[...] * jnp.exp(top[...] - new_top) + jnp.where(
        there, jnp.exp(value - new_top), 0.0
    )
    top[...] = new_top
    scores = temper * mm(passages, q_ref[...], NT)
    new_in = jnp.maximum(top_in[...], jnp.max(scores, axis=0, keepdims=True))
    total_in[...] = total_in[...] * jnp.exp(top_in[...] - new_in) + jnp.sum(
        jnp.exp(scores - new_in), axis=0, keepdims=True
    )
    top_in[...] = new_in

    @pl.when(g == groups - 1)
    def _():
        part = jnp.where(total[...] > 0.0, top[...] + jnp.log(total[...]), LOW)
        inside = top_in[...] + jnp.log(total_in[...])
        high = jnp.maximum(part, inside)
        both = high + jnp.log(jnp.exp(part - high) + jnp.exp(inside - high))
        own = iota(part.shape, 0) == place_ref[1]
        part_ref[...] = jnp.where(own, both, part)


def own_row(lt_ref, place_ref):
    lt = lt_ref[...]
    own = iota(lt.shape, 0) == place_ref[1]
    return jnp.sum(jnp.where(own, lt, 0.0), axis=0, keepdims=True)


def grad_kernel(
    reps, cap, temper, place_ref, code_ref, hs_ref, lt_ref, qr_ref, p_ref, q_ref,
    gp_ref, gq_ref, loss_ref,
):
    g = pl.program_id(0)
    toks, width = q_ref.shape
    slots = reps * cap
    ids, tok, valid, mine = slot_codes(code_ref, g, reps, cap)
    passages = p_ref[...]
    asking = qr_ref[...].reshape(slots, width)
    queries = q_ref[...]
    token = jnp.where((iota((toks, slots), 0) == tok) & valid, 1.0, 0.0)
    found = mm(lt_ref[...], token, exact=True)
    log_slot = jnp.sum(jnp.where(mine, found, 0.0), axis=0, keepdims=True)
    hs = hs_ref[pl.ds(g, 1), :]
    d_hard = jnp.where(valid, jnp.exp(hs - log_slot), 0.0)
    hard = jnp.where(iota((toks, slots), 0) + 1 == ids, d_hard, 0.0).astype(BF16)
    lt_own = own_row(lt_ref, place_ref)
    scores = temper * mm(passages, queries, NT)
    eye = iota((toks, toks), 0) == iota((toks, toks), 1)
    here = g == place_ref[0]
    d_scores = jnp.exp(scores - lt_own) - jnp.where(eye & here, 1.0, 0.0)
    d_scores = d_scores.astype(BF16)
    gp_ref[...] = (temper * (mm(hard, asking) + mm(d_scores, queries))).astype(BF16)
    step = mm(d_scores, passages, TN)

    @pl.when(g == 0)
    def _():
        gq_ref[...] = step

    @pl.when(g > 0)
    def _():
        gq_ref[...] += step

    @pl.when(here)
    def _():
        loss_ref[...] = lt_own - jnp.sum(jnp.where(eye, scores, 0.0), axis=0, keepdims=True)


def final_kernel(reps, cap, temper, place_ref, v_ref, lt_ref, f_ref, q_ref, gq_ref, out_ref, acc):
    g = pl.program_id(0)
    toks, width = q_ref.shape
    slots = reps * cap
    _, hit = slot_hits(v_ref, g, reps, cap, v_ref.shape[0], toks)
    fetched = f_ref[...].reshape(slots, width)
    scores = temper * mm(fetched, q_ref[...], NT)
    d_hard = jnp.where(hit, jnp.exp(scores - own_row(lt_ref, place_ref)), 0.0).astype(BF16)
    step = mm(d_hard, fetched, TN)

    @pl.when(g == 0)
    def _():
        acc[...] = gq_ref[...] + step

    @pl.when(g > 0)
    def _():
        acc[...] += step

    @pl.when(g == pl.num_programs(0) - 1)
    def _():
        out_ref[...] = (temper * acc[...]).astype(BF16)


def full(shape):
    return pl.BlockSpec(shape, lambda g: (0,) * len(shape))


def log_add_over_rep(part, reps):
    step = 1
    while step < reps:
        other = lax.ppermute(part, "rep", [(i, i ^ step) for i in range(reps)])
        part = jnp.maximum(part, other) + jnp.log1p(jnp.exp(-jnp.abs(part - other)))
        step *= 2
    return part


def shards(queries, passages, neg_device, neg_row):
    toks, width = queries.shape
    negs = neg_device.shape[1]
    groups = lax.axis_size("grp")
    reps = lax.axis_size("rep")
    devices = groups * reps
    cap = 8 * toks // devices
    slots = reps * cap
    temper = 3.0 / math.sqrt(width)
    place = jnp.stack([lax.axis_index("grp"), lax.axis_index("rep")]).astype(I32)
    smem = pl.BlockSpec(memory_space=pltpu.SMEM)
    by_group = pl.BlockSpec((reps, cap, width), lambda g: (0, g, 0))
    block = pl.BlockSpec((toks, width), lambda g: (g, 0))
    params = pltpu.CompilerParams(
        dimension_semantics=("arbitrary",), vmem_limit_bytes=VMEM_LIMIT
    )
    unit = 2 * toks * width * groups * slots

    def cost(n, mib):
        return pl.CostEstimate(flops=n * unit, bytes_accessed=mib << 20, transcendentals=0)

    gathered = lax.all_gather(passages, "grp", axis=0, tiled=True)

    slot_queries, code, ranks = pl.pallas_call(
        functools.partial(prep_kernel, reps, cap),
        grid=(groups,),
        in_specs=[full((negs, toks)), full((negs, toks)), full((toks, width))],
        out_specs=[by_group, full((groups, slots)), full((devices, toks))],
        out_shape=[
            jax.ShapeDtypeStruct((reps, groups * cap, width), BF16),
            jax.ShapeDtypeStruct((groups, slots), I32),
            jax.ShapeDtypeStruct((devices, toks), BF16),
        ],
        scratch_shapes=[pltpu.VMEM((devices, toks), BF16)],
        compiler_params=params,
        cost_estimate=cost(1, 5),
        name="prep",
    )(neg_device.T, neg_row.T, queries)

    asked = lax.all_to_all(
        code.reshape(groups, reps, cap).transpose(1, 0, 2).reshape(reps, groups * cap),
        "rep", split_axis=0, concat_axis=0, tiled=True,
    )
    asked = asked.reshape(reps, groups, cap).transpose(1, 0, 2).reshape(groups, slots)
    asking = lax.all_to_all(slot_queries, "rep", split_axis=0, concat_axis=0, tiled=True)

    served, hard_scores, part = pl.pallas_call(
        functools.partial(serve_kernel, reps, cap, temper),
        grid=(groups,),
        in_specs=[smem, full((groups, slots)), by_group, block, full((toks, width))],
        out_specs=[by_group, full((groups, slots)), full((reps, toks))],
        out_shape=[
            jax.ShapeDtypeStruct((reps, groups * cap, width), BF16),
            jax.ShapeDtypeStruct((groups, slots), F32),
            jax.ShapeDtypeStruct((reps, toks), F32),
        ],
        scratch_shapes=[
            pltpu.VMEM((reps, toks), F32),
            pltpu.VMEM((reps, toks), F32),
            pltpu.VMEM((1, toks), F32),
            pltpu.VMEM((1, toks), F32),
        ],
        compiler_params=params,
        cost_estimate=cost(3, 13),
        name="serve",
    )(place, asked, asking, gathered, queries)

    fetched = lax.all_to_all(served, "rep", split_axis=0, concat_axis=0, tiled=True)
    log_total = log_add_over_rep(part, reps)

    partial_sum, inner, losses = pl.pallas_call(
        functools.partial(grad_kernel, reps, cap, temper),
        grid=(groups,),
        in_specs=[
            smem, full((groups, slots)), full((groups, slots)), full((reps, toks)),
            by_group, block, full((toks, width)),
        ],
        out_specs=[block, full((toks, width)), full((1, toks))],
        out_shape=[
            jax.ShapeDtypeStruct((groups * toks, width), BF16),
            jax.ShapeDtypeStruct((toks, width), F32),
            jax.ShapeDtypeStruct((1, toks), F32),
        ],
        compiler_params=params,
        cost_estimate=cost(4, 14),
        name="grads",
    )(place, asked, hard_scores, log_total, asking, gathered, queries)

    grad_passages = lax.psum_scatter(partial_sum, "grp", scatter_dimension=0, tiled=True)

    grad_queries = pl.pallas_call(
        functools.partial(final_kernel, reps, cap, temper),
        grid=(groups,),
        in_specs=[
            smem, full((devices, toks)), full((reps, toks)), by_group,
            full((toks, width)), full((toks, width)),
        ],
        out_specs=full((toks, width)),
        out_shape=jax.ShapeDtypeStruct((toks, width), BF16),
        scratch_shapes=[pltpu.VMEM((toks, width), F32)],
        compiler_params=params,
        cost_estimate=cost(2, 6),
        name="final",
    )(place, ranks, log_total, fetched, queries, inner)
    return (losses.reshape(toks), grad_queries, grad_passages)


def solution(mesh):
    in_specs = (
        P(("grp", "rep"), None),
        P(("grp", "rep"), None),
        P(("grp", "rep"), None),
        P(("grp", "rep"), None),
    )
    out_specs = (P(("grp", "rep")), P(("grp", "rep"), None), P(("grp", "rep"), None))
    return jax.shard_map(shards, mesh=mesh, in_specs=in_specs, out_specs=out_specs, check_vma=False)
```

```python
import functools
import math

import jax
import jax.numpy as jnp
from jax import lax
from jax.experimental import pallas as pl
from jax.experimental.pallas import tpu as pltpu
from jax.sharding import PartitionSpec as P

F32 = jnp.float32
BF16 = jnp.bfloat16
I32 = jnp.int32
LOW = -1e30
NT = (((1,), (1,)), ((), ()))
TN = (((0,), (0,)), ((), ()))
NN = (((1,), (0,)), ((), ()))
VMEM_LIMIT = 60 * 1024 * 1024


def mm(a, b, dims=NN):
    return lax.dot_general(a, b, dims, preferred_element_type=F32)


def iota(shape, dim):
    return lax.broadcasted_iota(I32, shape, dim)


def split3(x):
    a = x.astype(BF16)
    rest = x - a.astype(F32)
    b = rest.astype(BF16)
    c = (rest - b.astype(F32)).astype(BF16)
    return jnp.concatenate([a, b, c], axis=0)


def slot_hits(v_ref, step, reps, cap, toks):
    rows = reps * 2 * cap
    devices = v_ref.shape[0]
    slot = iota((rows, devices), 0)
    owner = (2 * step + slot // cap % 2) * reps + slot // (2 * cap)
    pick = (iota((rows, devices), 1) == owner).astype(BF16)
    spread = mm(pick, v_ref[...])
    want = (iota((rows, toks), 0) % cap + 1).astype(F32)
    return pick, spread == want


def prep_kernel(reps, cap, nd_ref, nr_ref, q_ref, slots_ref, code_ref, v_ref, row_ref):
    step = pl.program_id(0)
    negs, toks = nd_ref.shape
    devices = v_ref.shape[0]

    @pl.when(step == 0)
    def _():
        dev = iota((devices, toks), 0)
        named = jnp.zeros((devices, toks), F32)
        rows = jnp.zeros((devices, toks), F32)
        for k in range(negs):
            hit = dev == nd_ref[k : k + 1, :]
            named = named + jnp.where(hit, 1.0, 0.0)
            rows = rows + jnp.where(hit, (nr_ref[k : k + 1, :] + 1).astype(F32), 0.0)
        before = (iota((toks, toks), 0) < iota((toks, toks), 1)).astype(BF16)
        rank = mm(named.astype(BF16), before)
        v_ref[...] = (named * (rank + 1.0)).astype(BF16)
        row_ref[...] = rows.astype(BF16)

    pick, hit = slot_hits(v_ref, step, reps, cap, toks)
    wanted = mm(pick, row_ref[...])
    hot = hit.astype(BF16)
    slots_ref[...] = mm(hot, q_ref[...]).astype(BF16).reshape(slots_ref.shape)
    ids = mm(jnp.ones((8, toks), BF16), jnp.where(hit, wanted, 0.0).astype(BF16), NT)
    tok = mm(iota((8, toks), 1).astype(F32).astype(BF16), hot, NT)
    code = tok * 512.0 + ids
    code_ref[pl.ds(step, 1), :] = code[0:1, :].astype(I32)


def serve_kernel(reps, cap, place_ref, code_ref, p_ref, served_ref):
    toks, width = p_ref.shape[1:]
    level = (place_ref[0] + pl.program_id(0)) % pl.num_programs(0)
    for core in range(2):
        ids = code_ref[pl.ds(2 * level + core, 1), :] & 511
        hot = (iota((toks, reps * cap), 0) + 1 == ids).astype(BF16)
        rows = mm(hot, p_ref[core], TN).astype(BF16).reshape(reps, cap, width)
        served_ref[:, core * cap : (core + 1) * cap, :] = rows


def inside_kernel(temper, p_ref, q_ref, out_ref, top, total):
    step = pl.program_id(0)

    @pl.when(step == 0)
    def _():
        top[...] = jnp.full(top.shape, LOW, F32)
        total[...] = jnp.zeros(total.shape, F32)

    scores = temper * mm(p_ref[...], q_ref[...], NT)
    high = jnp.maximum(top[...], jnp.max(scores, axis=0, keepdims=True))
    total[...] = total[...] * jnp.exp(top[...] - high) + jnp.sum(
        jnp.exp(scores - high), axis=0, keepdims=True
    )
    top[...] = high

    @pl.when(step == pl.num_programs(0) - 1)
    def _():
        out_ref[...] = top[...] + jnp.log(total[...])


def hard_kernel(
    reps, cap, temper, place_ref, code_ref, qr_ref, p_ref, inside_ref,
    hs_ref, part_ref, top, total,
):
    step = pl.program_id(0)
    toks, width = p_ref.shape[1:]
    slots = reps * cap
    level = (place_ref[0] + step) % pl.num_programs(0)
    mine = iota((reps, slots), 1) // cap == iota((reps, slots), 0)

    @pl.when(step == 0)
    def _():
        top[...] = jnp.full(top.shape, LOW, F32)
        total[...] = jnp.zeros(total.shape, F32)

    for core in range(2):
        code = code_ref[pl.ds(2 * level + core, 1), :]
        ids = code & 511
        valid = ids > 0
        asking = qr_ref[:, core * cap : (core + 1) * cap, :].reshape(slots, width)
        cross = mm(p_ref[core], asking, NT)
        hit = iota((toks, slots), 0) + 1 == ids
        hs = temper * jnp.sum(jnp.where(hit, cross, 0.0), axis=0, keepdims=True)
        hs_ref[pl.ds(2 * level + core, 1), :] = hs
        token = ((iota((toks, slots), 0) == code >> 9) & valid).astype(BF16)
        live = mine & valid
        parts = jnp.concatenate([split3(jnp.where(live, hs, 0.0)), live.astype(BF16)], axis=0)
        laid = mm(parts, token, NT)
        there = laid[3 * reps :] > 0.5
        value = laid[:reps] + laid[reps : 2 * reps] + laid[2 * reps : 3 * reps]
        value = jnp.where(there, value, LOW)
        high = jnp.maximum(top[...], value)
        total[...] = total[...] * jnp.exp(top[...] - high) + jnp.where(
            there, jnp.exp(value - high), 0.0
        )
        top[...] = high

    @pl.when(step == pl.num_programs(0) - 1)
    def _():
        part = jnp.where(total[...] > 0.0, top[...] + jnp.log(total[...]), LOW)
        inside = inside_ref[...]
        high = jnp.maximum(part, inside)
        both = high + jnp.log(jnp.exp(part - high) + jnp.exp(inside - high))
        own = iota(part.shape, 0) == place_ref[2]
        part_ref[...] = jnp.where(own, both, part)


def own_row(lt_ref, place_ref):
    lt = lt_ref[...]
    own = iota(lt.shape, 0) == place_ref[2]
    return jnp.sum(jnp.where(own, lt, 0.0), axis=0, keepdims=True)


def grad_kernel(
    reps, cap, temper, own_core, place_ref, code_ref, hs_ref, lt_ref, qr_ref, p_ref, q_ref, gp_ref,
):
    step = pl.program_id(0)
    toks, width = q_ref.shape
    slots = reps * cap
    level = (place_ref[0] + step) % pl.num_programs(0)
    core = place_ref[1] if own_core else 1 - place_ref[1]
    code = code_ref[pl.ds(2 * level + core, 1), :]
    ids = code & 511
    valid = ids > 0
    mine = iota((reps, slots), 1) // cap == iota((reps, slots), 0)
    token = ((iota((toks, slots), 0) == code >> 9) & valid).astype(BF16)
    found = mm(split3(lt_ref[...]), token)
    found = found[:reps] + found[reps : 2 * reps] + found[2 * reps :]
    log_slot = jnp.sum(jnp.where(mine, found, 0.0), axis=0, keepdims=True)
    hs = hs_ref[pl.ds(2 * level + core, 1), :]
    d_hard = jnp.where(valid, jnp.exp(hs - log_slot), 0.0)
    hard = jnp.where(iota((toks, slots), 0) + 1 == ids, d_hard, 0.0).astype(BF16)
    queries = q_ref[...]
    scores = temper * mm(p_ref[0], queries, NT)
    d_scores = jnp.exp(scores - own_row(lt_ref, place_ref))
    if own_core:
        eye = (iota((toks, toks), 0) == iota((toks, toks), 1)) & (step == 0)
        d_scores = d_scores - jnp.where(eye, 1.0, 0.0)
    d_scores = d_scores.astype(BF16)
    asking = qr_ref[...].reshape(slots, width)
    gp_ref[0] = (temper * (mm(hard, asking) + mm(d_scores, queries))).astype(BF16)


def inner_kernel(temper, place_ref, lt_ref, p_ref, q_ref, gq_ref, loss_ref, acc):
    step = pl.program_id(0)
    toks, width = q_ref.shape
    lt_own = own_row(lt_ref, place_ref)
    passages = p_ref[...]
    scores = temper * mm(passages, q_ref[...], NT)
    row = iota(scores.shape, 0) - toks * place_ref[1]
    eye = (row == iota(scores.shape, 1)) & (step == 0)
    d_scores = (jnp.exp(scores - lt_own) - jnp.where(eye, 1.0, 0.0)).astype(BF16)
    new = mm(d_scores, passages, TN)

    @pl.when(step == 0)
    def _():
        acc[...] = new
        loss_ref[...] = lt_own - jnp.sum(jnp.where(eye, scores, 0.0), axis=0, keepdims=True)

    @pl.when(step > 0)
    def _():
        acc[...] += new

    @pl.when(step == pl.num_programs(0) - 1)
    def _():
        gq_ref[...] = acc[...]


def final_kernel(reps, cap, temper, place_ref, v_ref, lt_ref, f_ref, q_ref, gq_ref, out_ref, acc):
    step = pl.program_id(0)
    toks, width = q_ref.shape
    _, hit = slot_hits(v_ref, step, reps, cap, toks)
    fetched = f_ref[...].reshape(2 * reps * cap, width)
    scores = temper * mm(fetched, q_ref[...], NT)
    d_hard = jnp.where(hit, jnp.exp(scores - own_row(lt_ref, place_ref)), 0.0).astype(BF16)
    new = mm(d_hard, fetched, TN)

    @pl.when(step == 0)
    def _():
        acc[...] = gq_ref[...] + new

    @pl.when(step > 0)
    def _():
        acc[...] += new

    @pl.when(step == pl.num_programs(0) - 1)
    def _():
        out_ref[...] = (temper * acc[...]).astype(BF16)


def full(shape):
    return pl.BlockSpec(shape, lambda *_: (0,) * len(shape))


def log_add_over_rep(part, reps):
    step = 1
    while step < reps:
        other = lax.ppermute(part, "rep", [(i, i ^ step) for i in range(reps)])
        part = jnp.maximum(part, other) + jnp.log1p(jnp.exp(-jnp.abs(part - other)))
        step *= 2
    return part


def codes_over_rep(code, reps, me):
    table = code[None]
    step = 1
    while step < reps:
        other = lax.ppermute(table, "rep", [(i, i ^ step) for i in range(reps)])
        table = jnp.concatenate([table, other], axis=0)
        step *= 2
    meant = jnp.sum(jnp.where((jnp.arange(reps) == me)[None, :, None], table, 0), axis=1)
    order = (jnp.arange(reps)[None, :] ^ me) == jnp.arange(reps)[:, None]
    return jnp.sum(jnp.where(order[:, :, None], meant[None], 0), axis=1)


def along_z(x, shift, groups):
    return lax.ppermute(
        x, "grp", [(i, (i + 2 * shift) % groups) for i in range(groups)]
    )


def other_core(x, groups):
    return lax.ppermute(x, "grp", [(i, i ^ 1) for i in range(groups)])


def gather_group(block, core, groups):
    half = block.shape[0] // 2
    below = along_z(block, 1, groups)
    above = along_z(block, -1, groups)
    far = jnp.concatenate(
        [along_z(below[:half], 1, groups), along_z(above[half:], -1, groups)], axis=0
    )
    own = jnp.stack([block, above, far, below])
    theirs = other_core(own, groups)
    first = core == 0
    return jnp.stack([jnp.where(first, own, theirs), jnp.where(first, theirs, own)], axis=1)


def scatter_group(own, other, groups):
    half = own.shape[1] // 2
    whole = own.astype(F32) + other_core(other, groups).astype(F32)
    up = along_z(whole[2, :half].astype(BF16), 1, groups).astype(F32)
    down = along_z(whole[2, half:].astype(BF16), -1, groups).astype(F32)
    to_above = jnp.concatenate([whole[1, :half] + up, whole[1, half:]], axis=0)
    to_below = jnp.concatenate([whole[3, :half], whole[3, half:] + down], axis=0)
    from_below = along_z(to_above.astype(BF16), 1, groups).astype(F32)
    from_above = along_z(to_below.astype(BF16), -1, groups).astype(F32)
    return (whole[0] + from_below + from_above).astype(BF16)


def shards(queries, passages, neg_device, neg_row):
    toks, width = queries.shape
    negs = neg_device.shape[1]
    groups = lax.axis_size("grp")
    reps = lax.axis_size("rep")
    devices = groups * reps
    levels = groups // 2
    cap = 8 * toks // devices
    slots = reps * cap
    temper = 3.0 / math.sqrt(width)
    me = lax.axis_index("rep")
    core = lax.axis_index("grp") % 2
    place = jnp.stack([lax.axis_index("grp") // 2, core, me]).astype(I32)
    block = jax.ShapeDtypeStruct((toks, width), BF16)
    slot_shape = jax.ShapeDtypeStruct((reps, groups * cap, width), BF16)
    pair = (reps, 2 * cap, width)

    def rows(*shape):
        return jax.ShapeDtypeStruct(shape, F32)

    def call(kernel, name, ins, outs, shapes, scratch, weight, prefetch):
        return pl.pallas_call(
            kernel,
            grid_spec=pltpu.PrefetchScalarGridSpec(
                num_scalar_prefetch=int(prefetch),
                grid=(levels,),
                in_specs=ins,
                out_specs=outs,
                scratch_shapes=scratch,
            ),
            out_shape=shapes,
            compiler_params=pltpu.CompilerParams(
                dimension_semantics=("arbitrary",), vmem_limit_bytes=VMEM_LIMIT
            ),
            cost_estimate=pl.CostEstimate(
                flops=weight, bytes_accessed=1 << 16, transcendentals=0
            ),
            name=name,
        )

    light, heavy = 1 << 20, 1 << 39

    slot_queries, code, ranks = call(
        functools.partial(prep_kernel, reps, cap), "prep",
        [full((negs, toks)), full((negs, toks)), full((toks, width))],
        [pl.BlockSpec(pair, lambda s: (0, s, 0)), full((levels, 2 * slots)), full((devices, toks))],
        [slot_shape, jax.ShapeDtypeStruct((levels, 2 * slots), I32),
         jax.ShapeDtypeStruct((devices, toks), BF16)],
        [pltpu.VMEM((devices, toks), BF16)], light, False,
    )(neg_device.T, neg_row.T, queries)

    asking = lax.all_to_all(slot_queries, "rep", split_axis=0, concat_axis=0, tiled=True)

    code = code.reshape(levels, reps, 2 * cap).transpose(1, 0, 2).reshape(reps, groups * cap)
    asked = codes_over_rep(code, reps, me)
    asked = asked.reshape(reps, groups, cap).transpose(1, 0, 2).reshape(groups, slots)
    gathered = gather_group(passages, core, groups)

    by_level = pl.BlockSpec((1, 2, toks, width), lambda s, *_: (s, 0, 0, 0))
    pair_block = pl.BlockSpec((None, 2, toks, width), lambda s, *_: (s, 0, 0, 0))
    flat_pair = pl.BlockSpec((2 * toks, width), lambda s, *_: (s, 0))
    slot_pair = pl.BlockSpec(pair, lambda s, place: (0, (place[0] + s) % levels, 0))
    flat = gathered.reshape(groups * toks, width)

    served = call(
        functools.partial(serve_kernel, reps, cap), "serve",
        [full((groups, slots)), pair_block], slot_pair, slot_shape, [], light, True,
    )(place, asked, gathered)

    inside = call(
        functools.partial(inside_kernel, temper), "inside",
        [flat_pair, full((toks, width))], full((1, toks)), rows(1, toks),
        [pltpu.VMEM((1, toks), F32), pltpu.VMEM((1, toks), F32)], light, False,
    )(flat, queries)

    fetched = lax.all_to_all(served, "rep", split_axis=0, concat_axis=0, tiled=True)

    hard_scores, part = call(
        functools.partial(hard_kernel, reps, cap, temper), "hard",
        [full((groups, slots)), slot_pair, pair_block, full((1, toks))],
        [full((groups, slots)), full((reps, toks))],
        [rows(groups, slots), rows(reps, toks)],
        [pltpu.VMEM((reps, toks), F32), pltpu.VMEM((reps, toks), F32)], light, True,
    )(place, asked, asking, gathered, inside)

    log_total = log_add_over_rep(part, reps)

    def column(own_core):
        def which(place):
            return place[1] if own_core else 1 - place[1]

        return call(
            functools.partial(grad_kernel, reps, cap, temper, own_core),
            "own" if own_core else "other",
            [full((groups, slots)), full((groups, slots)), full((reps, toks)),
             pl.BlockSpec((reps, cap, width),
                          lambda s, place: (0, 2 * ((place[0] + s) % levels) + which(place), 0)),
             pl.BlockSpec((None, 1, toks, width), lambda s, place: (s, which(place), 0, 0)),
             full((toks, width))],
            pl.BlockSpec((1, toks, width), lambda s, place: (s, 0, 0)),
            jax.ShapeDtypeStruct((levels, toks, width), BF16), [], light, True,
        )(place, asked, hard_scores, log_total, asking, gathered, queries)

    other = column(False)
    own = column(True)
    grad_passages = scatter_group(own, other, groups)

    inner, losses = call(
        functools.partial(inner_kernel, temper), "inner",
        [full((reps, toks)), flat_pair, full((toks, width))],
        [full((toks, width)), full((1, toks))], [rows(toks, width), rows(1, toks)],
        [pltpu.VMEM((toks, width), F32)], light, True,
    )(place, log_total, flat, queries)

    grad_queries = call(
        functools.partial(final_kernel, reps, cap, temper), "final",
        [full((devices, toks)), full((reps, toks)),
         pl.BlockSpec(pair, lambda s, place: (0, s, 0)),
         full((toks, width)), full((toks, width))],
        full((toks, width)), block, [pltpu.VMEM((toks, width), F32)], heavy, True,
    )(place, ranks, log_total, fetched, queries, inner)
    return (losses.reshape(toks), grad_queries, grad_passages)


def solution(mesh):
    in_specs = (
        P(("grp", "rep"), None),
        P(("grp", "rep"), None),
        P(("grp", "rep"), None),
        P(("grp", "rep"), None),
    )
    out_specs = (P(("grp", "rep")), P(("grp", "rep"), None), P(("grp", "rep"), None))
    return jax.shard_map(shards, mesh=mesh, in_specs=in_specs, out_specs=out_specs, check_vma=False)
```

```python
import functools
import math

import jax
import jax.numpy as jnp
from jax import lax
from jax.experimental import pallas as pl
from jax.experimental.pallas import tpu as pltpu
from jax.sharding import PartitionSpec as P

F32 = jnp.float32
BF16 = jnp.bfloat16
I32 = jnp.int32
LOW = -1e30
NT = (((1,), (1,)), ((), ()))
TN = (((0,), (0,)), ((), ()))
NN = (((1,), (0,)), ((), ()))
VMEM_LIMIT = 60 * 1024 * 1024


def mm(a, b, dims=NN):
    return lax.dot_general(a, b, dims, preferred_element_type=F32)


def iota(shape, dim):
    return lax.broadcasted_iota(I32, shape, dim)


def split3(x):
    a = x.astype(BF16)
    rest = x - a.astype(F32)
    b = rest.astype(BF16)
    c = (rest - b.astype(F32)).astype(BF16)
    return jnp.concatenate([a, b, c], axis=0)


def slot_hits(v_ref, group, reps, cap, toks):
    rows = reps * cap
    devices = v_ref.shape[0]
    owner = group * reps + iota((rows, devices), 0) // cap
    pick = (iota((rows, devices), 1) == owner).astype(BF16)
    spread = mm(pick, v_ref[...])
    want = (iota((rows, toks), 0) % cap + 1).astype(F32)
    return pick, spread == want


def prep_kernel(reps, cap, groups, nd_ref, nr_ref, q_ref, slots_ref, v_ref, row_ref, code_ref):
    step = pl.program_id(0)
    negs, toks = nd_ref.shape
    devices = v_ref.shape[0]
    slots = reps * cap

    @pl.when(step == 0)
    def _():
        dev = iota((devices, toks), 0)
        named = jnp.zeros((devices, toks), F32)
        rows = jnp.zeros((devices, toks), F32)
        for k in range(negs):
            hit = dev == nd_ref[k : k + 1, :]
            named = named + jnp.where(hit, 1.0, 0.0)
            rows = rows + jnp.where(hit, (nr_ref[k : k + 1, :] + 1).astype(F32), 0.0)
        before = (iota((toks, toks), 0) < iota((toks, toks), 1)).astype(BF16)
        rank = mm(named.astype(BF16), before)
        v_ref[...] = (named * (rank + 1.0)).astype(BF16)
        row_ref[...] = rows.astype(BF16)
        code_ref[...] = jnp.zeros(code_ref.shape, F32)

    @pl.when(step < groups)
    def _():
        pick, hit = slot_hits(v_ref, step, reps, cap, toks)
        hot = hit.astype(BF16)
        slots_ref[...] = mm(hot, q_ref[...]).astype(BF16).reshape(slots_ref.shape)
        wanted = mm(pick, row_ref[...])
        row = mm(jnp.ones((8, toks), BF16), jnp.where(hit, wanted, 0.0).astype(BF16), NT)
        tok = mm(iota((8, toks), 1).astype(F32).astype(BF16), hot, NT)
        place = iota((slots, slots), 0)
        same = place // cap == iota((slots, slots), 1) // cap
        spread = jnp.where(same & (place % cap == 0), row[0:1], 0.0)
        spread = spread + jnp.where(same & (place % cap == 1), tok[0:1], 0.0)
        lane = iota((slots, groups * cap), 1)
        to_lane = lane == step * cap + iota((slots, groups * cap), 0) % cap
        code_ref[...] += mm(spread.astype(BF16), to_lane.astype(BF16))

    @pl.when(step == groups)
    def _():
        rest = jnp.zeros((slots, slots_ref.shape[2] - groups * cap), F32)
        wide = jnp.concatenate([code_ref[...], rest], axis=1)
        slots_ref[...] = wide.astype(BF16).reshape(slots_ref.shape)


def read_codes(ext_ref, group, reps, cap):
    slots = reps * cap
    lanes = ext_ref.shape[2]
    ext = ext_ref[...].reshape(slots, lanes)
    to_slot = iota((lanes, slots), 0) == group * cap + iota((lanes, slots), 1) % cap
    laid = mm(ext, to_slot.astype(BF16))
    place = iota((slots, slots), 0)
    same = place // cap == iota((slots, slots), 1) // cap
    ids = jnp.sum(jnp.where(same & (place % cap == 0), laid, 0.0), axis=0, keepdims=True)
    tok = jnp.sum(jnp.where(same & (place % cap == 1), laid, 0.0), axis=0, keepdims=True)
    return ids.astype(I32), tok.astype(I32)


def serve_kernel(reps, cap, place_ref, code_ref, p_ref, served_ref):
    toks, width = p_ref.shape[1:]
    level = (place_ref[0] + pl.program_id(0)) % pl.num_programs(0)
    for core in range(2):
        ids = code_ref[pl.ds(2 * level + core, 1), :] & 511
        hot = (iota((toks, reps * cap), 0) + 1 == ids).astype(BF16)
        rows = mm(hot, p_ref[core], TN).astype(BF16).reshape(reps, cap, width)
        served_ref[:, core * cap : (core + 1) * cap, :] = rows


def inside_kernel(temper, p_ref, q_ref, out_ref, top, total):
    step = pl.program_id(0)

    @pl.when(step == 0)
    def _():
        top[...] = jnp.full(top.shape, LOW, F32)
        total[...] = jnp.zeros(total.shape, F32)

    scores = temper * mm(p_ref[...], q_ref[...], NT)
    high = jnp.maximum(top[...], jnp.max(scores, axis=0, keepdims=True))
    total[...] = total[...] * jnp.exp(top[...] - high) + jnp.sum(
        jnp.exp(scores - high), axis=0, keepdims=True
    )
    top[...] = high

    @pl.when(step == pl.num_programs(0) - 1)
    def _():
        out_ref[...] = top[...] + jnp.log(total[...])


def hard_kernel(
    reps, cap, temper, place_ref, ext_ref, qr_ref, p_ref, inside_ref,
    hs_ref, code_ref, part_ref, top, total,
):
    step = pl.program_id(0)
    toks, width = p_ref.shape[1:]
    slots = reps * cap
    level = (place_ref[0] + step) % pl.num_programs(0)
    mine = iota((reps, slots), 1) // cap == iota((reps, slots), 0)

    @pl.when(step == 0)
    def _():
        top[...] = jnp.full(top.shape, LOW, F32)
        total[...] = jnp.zeros(total.shape, F32)

    for core in range(2):
        ids, tok = read_codes(ext_ref, 2 * level + core, reps, cap)
        code_ref[pl.ds(2 * level + core, 1), :] = tok * 512 + ids
        valid = ids > 0
        asking = qr_ref[:, core * cap : (core + 1) * cap, :].reshape(slots, width)
        cross = mm(p_ref[core], asking, NT)
        hit = iota((toks, slots), 0) + 1 == ids
        hs = temper * jnp.sum(jnp.where(hit, cross, 0.0), axis=0, keepdims=True)
        hs_ref[pl.ds(2 * level + core, 1), :] = hs
        token = ((iota((toks, slots), 0) == tok) & valid).astype(BF16)
        live = mine & valid
        parts = jnp.concatenate([split3(jnp.where(live, hs, 0.0)), live.astype(BF16)], axis=0)
        laid = mm(parts, token, NT)
        there = laid[3 * reps :] > 0.5
        value = laid[:reps] + laid[reps : 2 * reps] + laid[2 * reps : 3 * reps]
        value = jnp.where(there, value, LOW)
        high = jnp.maximum(top[...], value)
        total[...] = total[...] * jnp.exp(top[...] - high) + jnp.where(
            there, jnp.exp(value - high), 0.0
        )
        top[...] = high

    @pl.when(step == pl.num_programs(0) - 1)
    def _():
        part = jnp.where(total[...] > 0.0, top[...] + jnp.log(total[...]), LOW)
        inside = inside_ref[...]
        high = jnp.maximum(part, inside)
        both = high + jnp.log(jnp.exp(part - high) + jnp.exp(inside - high))
        own = iota(part.shape, 0) == place_ref[2]
        part_ref[...] = jnp.broadcast_to(jnp.where(own, both, part)[None], part_ref.shape)


def own_row(lt_ref, place_ref):
    lt = lt_ref[...]
    own = iota(lt.shape, 0) == place_ref[2]
    return jnp.sum(jnp.where(own, lt, 0.0), axis=0, keepdims=True)


def grad_kernel(
    reps, cap, temper, own_core, place_ref, code_ref, hs_ref, lt_ref, qr_ref, p_ref, q_ref, gp_ref,
):
    step = pl.program_id(0)
    toks, width = q_ref.shape
    slots = reps * cap
    level = (place_ref[0] + step) % pl.num_programs(0)
    core = place_ref[1] if own_core else 1 - place_ref[1]
    code = code_ref[pl.ds(2 * level + core, 1), :]
    ids = code & 511
    valid = ids > 0
    mine = iota((reps, slots), 1) // cap == iota((reps, slots), 0)
    token = ((iota((toks, slots), 0) == code >> 9) & valid).astype(BF16)
    found = mm(split3(lt_ref[...]), token)
    found = found[:reps] + found[reps : 2 * reps] + found[2 * reps :]
    log_slot = jnp.sum(jnp.where(mine, found, 0.0), axis=0, keepdims=True)
    hs = hs_ref[pl.ds(2 * level + core, 1), :]
    d_hard = jnp.where(valid, jnp.exp(hs - log_slot), 0.0)
    hard = jnp.where(iota((toks, slots), 0) + 1 == ids, d_hard, 0.0).astype(BF16)
    queries = q_ref[...]
    scores = temper * mm(p_ref[0], queries, NT)
    d_scores = jnp.exp(scores - own_row(lt_ref, place_ref))
    if own_core:
        eye = (iota((toks, toks), 0) == iota((toks, toks), 1)) & (step == 0)
        d_scores = d_scores - jnp.where(eye, 1.0, 0.0)
    d_scores = d_scores.astype(BF16)
    asking = qr_ref[...].reshape(slots, width)
    gp_ref[0] = (temper * (mm(hard, asking) + mm(d_scores, queries))).astype(BF16)


def inner_kernel(temper, place_ref, lt_ref, p_ref, q_ref, gq_ref, loss_ref, acc):
    step = pl.program_id(0)
    toks, width = q_ref.shape
    lt_own = own_row(lt_ref, place_ref)
    passages = p_ref[...]
    scores = temper * mm(passages, q_ref[...], NT)
    row = iota(scores.shape, 0) - toks * place_ref[1]
    eye = (row == iota(scores.shape, 1)) & (step == 0)
    d_scores = (jnp.exp(scores - lt_own) - jnp.where(eye, 1.0, 0.0)).astype(BF16)
    new = mm(d_scores, passages, TN)

    @pl.when(step == 0)
    def _():
        acc[...] = new
        loss_ref[...] = lt_own - jnp.sum(jnp.where(eye, scores, 0.0), axis=0, keepdims=True)

    @pl.when(step > 0)
    def _():
        acc[...] += new

    @pl.when(step == pl.num_programs(0) - 1)
    def _():
        gq_ref[...] = acc[...]


def final_kernel(reps, cap, temper, place_ref, v_ref, lt_ref, f_ref, q_ref, gq_ref, out_ref, acc):
    step = pl.program_id(0)
    toks, width = q_ref.shape
    new = jnp.zeros((toks, width), F32)
    for core in range(2):
        _, hit = slot_hits(v_ref, 2 * step + core, reps, cap, toks)
        fetched = f_ref[:, core * cap : (core + 1) * cap, :].reshape(reps * cap, width)
        scores = temper * mm(fetched, q_ref[...], NT)
        d_hard = jnp.where(hit, jnp.exp(scores - own_row(lt_ref, place_ref)), 0.0).astype(BF16)
        new = new + mm(d_hard, fetched, TN)

    @pl.when(step == 0)
    def _():
        acc[...] = gq_ref[...] + new

    @pl.when(step > 0)
    def _():
        acc[...] += new

    @pl.when(step == pl.num_programs(0) - 1)
    def _():
        out_ref[...] = (temper * acc[...]).astype(BF16)


def full(shape):
    return pl.BlockSpec(shape, lambda *_: (0,) * len(shape))


def along_z(x, shift, groups):
    return lax.ppermute(
        x, "grp", [(i, (i + 2 * shift) % groups) for i in range(groups)]
    )


def other_core(x, groups):
    return lax.ppermute(x, "grp", [(i, i ^ 1) for i in range(groups)])


def gather_group(block, core, groups):
    half = block.shape[0] // 2
    below = along_z(block, 1, groups)
    above = along_z(block, -1, groups)
    far = jnp.concatenate(
        [along_z(below[:half], 1, groups), along_z(above[half:], -1, groups)], axis=0
    )
    own = jnp.stack([block, above, far, below])
    theirs = other_core(own, groups)
    first = core == 0
    return jnp.stack([jnp.where(first, own, theirs), jnp.where(first, theirs, own)], axis=1)


def scatter_group(own, other, groups):
    half = own.shape[1] // 2
    whole = own.astype(F32) + other_core(other, groups).astype(F32)
    up = along_z(whole[2, :half].astype(BF16), 1, groups).astype(F32)
    down = along_z(whole[2, half:].astype(BF16), -1, groups).astype(F32)
    to_above = jnp.concatenate([whole[1, :half] + up, whole[1, half:]], axis=0)
    to_below = jnp.concatenate([whole[3, :half], whole[3, half:] + down], axis=0)
    from_below = along_z(to_above.astype(BF16), 1, groups).astype(F32)
    from_above = along_z(to_below.astype(BF16), -1, groups).astype(F32)
    return (whole[0] + from_below + from_above).astype(BF16)


def shards(queries, passages, neg_device, neg_row):
    toks, width = queries.shape
    negs = neg_device.shape[1]
    groups = lax.axis_size("grp")
    reps = lax.axis_size("rep")
    devices = groups * reps
    levels = groups // 2
    cap = 8 * toks // devices
    slots = reps * cap
    temper = 3.0 / math.sqrt(width)
    me = lax.axis_index("rep")
    core = lax.axis_index("grp") % 2
    place = jnp.stack([lax.axis_index("grp") // 2, core, me]).astype(I32)
    block = jax.ShapeDtypeStruct((toks, width), BF16)
    slot_shape = jax.ShapeDtypeStruct((reps, groups * cap, width), BF16)
    pair = (reps, 2 * cap, width)

    def rows(*shape):
        return jax.ShapeDtypeStruct(shape, F32)

    def call(kernel, name, ins, outs, shapes, scratch, weight, prefetch, steps=levels):
        return pl.pallas_call(
            kernel,
            grid_spec=pltpu.PrefetchScalarGridSpec(
                num_scalar_prefetch=int(prefetch),
                grid=(steps,),
                in_specs=ins,
                out_specs=outs,
                scratch_shapes=scratch,
            ),
            out_shape=shapes,
            compiler_params=pltpu.CompilerParams(
                dimension_semantics=("arbitrary",), vmem_limit_bytes=VMEM_LIMIT
            ),
            cost_estimate=pl.CostEstimate(
                flops=weight, bytes_accessed=1 << 16, transcendentals=0
            ),
            name=name,
        )

    light, heavy = 1 << 20, 1 << 39

    sent, ranks = call(
        functools.partial(prep_kernel, reps, cap, groups), "prep",
        [full((negs, toks)), full((negs, toks)), full((toks, width))],
        [pl.BlockSpec((reps, cap, width), lambda s: (0, s, 0)), full((devices, toks))],
        [jax.ShapeDtypeStruct((reps, (groups + 1) * cap, width), BF16),
         jax.ShapeDtypeStruct((devices, toks), BF16)],
        [pltpu.VMEM((devices, toks), BF16), pltpu.VMEM((slots, groups * cap), F32)],
        light, False, groups + 1,
    )(neg_device.T, neg_row.T, queries)

    asking = lax.all_to_all(sent, "rep", split_axis=0, concat_axis=0, tiled=True)
    gathered = gather_group(passages, core, groups)

    by_level = pl.BlockSpec((1, 2, toks, width), lambda s, *_: (s, 0, 0, 0))
    pair_block = pl.BlockSpec((None, 2, toks, width), lambda s, *_: (s, 0, 0, 0))
    flat_pair = pl.BlockSpec((2 * toks, width), lambda s, *_: (s, 0))
    slot_pair = pl.BlockSpec(pair, lambda s, place: (0, (place[0] + s) % levels, 0))
    flat = gathered.reshape(groups * toks, width)

    inside = call(
        functools.partial(inside_kernel, temper), "inside",
        [flat_pair, full((toks, width))], full((1, toks)), rows(1, toks),
        [pltpu.VMEM((1, toks), F32), pltpu.VMEM((1, toks), F32)], light, False,
    )(flat, queries)

    hard_scores, asked, part = call(
        functools.partial(hard_kernel, reps, cap, temper), "hard",
        [pl.BlockSpec((reps, cap, groups * cap), lambda s, place: (0, groups, 0)),
         slot_pair, pair_block, full((1, toks))],
        [full((groups, slots)), full((groups, slots)), full((reps, reps, toks))],
        [rows(groups, slots), jax.ShapeDtypeStruct((groups, slots), I32), rows(reps, reps, toks)],
        [pltpu.VMEM((reps, toks), F32), pltpu.VMEM((reps, toks), F32)], light, True,
    )(place, asking, asking, gathered, inside)

    parts = lax.all_to_all(part, "rep", split_axis=0, concat_axis=0, tiled=True)
    high = jnp.max(parts, axis=0)
    log_total = high + jnp.log(jnp.sum(jnp.exp(parts - high), axis=0))

    served = call(
        functools.partial(serve_kernel, reps, cap), "serve",
        [full((groups, slots)), pair_block], slot_pair, slot_shape, [], light, True,
    )(place, asked, gathered)

    fetched = lax.all_to_all(served, "rep", split_axis=0, concat_axis=0, tiled=True)

    def column(own_core):
        def which(place):
            return place[1] if own_core else 1 - place[1]

        return call(
            functools.partial(grad_kernel, reps, cap, temper, own_core),
            "own" if own_core else "other",
            [full((groups, slots)), full((groups, slots)), full((reps, toks)),
             pl.BlockSpec((reps, cap, width),
                          lambda s, place: (0, 2 * ((place[0] + s) % levels) + which(place), 0)),
             pl.BlockSpec((None, 1, toks, width), lambda s, place: (s, which(place), 0, 0)),
             full((toks, width))],
            pl.BlockSpec((1, toks, width), lambda s, place: (s, 0, 0)),
            jax.ShapeDtypeStruct((levels, toks, width), BF16), [], light, True,
        )(place, asked, hard_scores, log_total, asking, gathered, queries)

    other = column(False)
    own = column(True)
    grad_passages = scatter_group(own, other, groups)

    inner, losses = call(
        functools.partial(inner_kernel, temper), "inner",
        [full((reps, toks)), flat_pair, full((toks, width))],
        [full((toks, width)), full((1, toks))], [rows(toks, width), rows(1, toks)],
        [pltpu.VMEM((toks, width), F32)], light, True,
    )(place, log_total, flat, queries)

    grad_queries = call(
        functools.partial(final_kernel, reps, cap, temper), "final",
        [full((devices, toks)), full((reps, toks)),
         pl.BlockSpec(pair, lambda s, place: (0, s, 0)),
         full((toks, width)), full((toks, width))],
        full((toks, width)), block, [pltpu.VMEM((toks, width), F32)], heavy, True,
    )(place, ranks, log_total, fetched, queries, inner)
    return (losses.reshape(toks), grad_queries, grad_passages)


def solution(mesh):
    in_specs = (
        P(("grp", "rep"), None),
        P(("grp", "rep"), None),
        P(("grp", "rep"), None),
        P(("grp", "rep"), None),
    )
    out_specs = (P(("grp", "rep")), P(("grp", "rep"), None), P(("grp", "rep"), None))
    return jax.shard_map(shards, mesh=mesh, in_specs=in_specs, out_specs=out_specs, check_vma=False)
```

```python
import functools
import math

import jax
import jax.numpy as jnp
from jax import lax
from jax.experimental import pallas as pl
from jax.experimental.pallas import tpu as pltpu
from jax.sharding import PartitionSpec as P

F32 = jnp.float32
BF16 = jnp.bfloat16
I32 = jnp.int32
LOW = -1e30
NT = (((1,), (1,)), ((), ()))
TN = (((0,), (0,)), ((), ()))
NN = (((1,), (0,)), ((), ()))
VMEM_LIMIT = 60 * 1024 * 1024


def mm(a, b, dims=NN):
    return lax.dot_general(a, b, dims, preferred_element_type=F32)


def iota(shape, dim):
    return lax.broadcasted_iota(I32, shape, dim)


def split3(x):
    a = x.astype(BF16)
    rest = x - a.astype(F32)
    b = rest.astype(BF16)
    c = (rest - b.astype(F32)).astype(BF16)
    return jnp.concatenate([a, b, c], axis=0)


def full(shape):
    return pl.BlockSpec(shape, lambda *_: (0,) * len(shape))


def call(kernel, name, steps, ins, outs, shapes, scratch, weight):
    return pl.pallas_call(
        kernel,
        grid_spec=pltpu.PrefetchScalarGridSpec(
            num_scalar_prefetch=1, grid=(steps,), in_specs=ins, out_specs=outs,
            scratch_shapes=scratch,
        ),
        out_shape=shapes,
        compiler_params=pltpu.CompilerParams(
            dimension_semantics=("arbitrary",), vmem_limit_bytes=VMEM_LIMIT
        ),
        cost_estimate=pl.CostEstimate(flops=weight, bytes_accessed=1 << 16, transcendentals=0),
        name=name,
    )


LIGHT, MIDDLE, HEAVY = 1 << 20, 1 << 32, 1 << 39
SIDE = 4
CORES = 2


def rep_of(x, y):
    return x % SIDE * SIDE + y % SIDE


def columns_of(place_ref, half, shift):
    x, y = place_ref[2], place_ref[3]
    return rep_of(x, y + shift) if half == 0 else rep_of(x + shift, y)


def source_of(place_ref, half, shift):
    x, y = place_ref[2], place_ref[3]
    return rep_of(x + SIDE - shift, y) if half == 0 else rep_of(x, y + SIDE - shift)


def pick_of(source, groups, cap):
    shape = (groups * cap, SIDE * groups)
    return (iota(shape, 1) == source * groups + iota(shape, 0) // cap).astype(BF16)


def hits_of(pick, ranks, cap):
    spread = mm(pick, ranks)
    return spread == (iota(spread.shape, 0) % cap + 1).astype(F32)


def mid_kernel(shift, cap, groups, reps, negs, place_ref, *refs):
    sources = (refs[0:SIDE], refs[SIDE : 2 * SIDE])
    outs, ranks_out = refs[2 * SIDE : 2 * SIDE + 2], refs[2 * SIDE + 2 :]
    rows, half_width = sources[0][0].shape
    toks = rows - 16
    before = (iota((toks, toks), 0) < iota((toks, toks), 1)).astype(BF16)
    for half in range(2):
        col = columns_of(place_ref, half, shift)
        dev = (iota((groups, toks), 0) * reps + col).astype(F32)
        named_all, rows_all = [], []
        for source in sources[half]:
            table = source[toks:, :toks].astype(F32)
            named = jnp.zeros((groups, toks), F32)
            wanted = jnp.zeros((groups, toks), F32)
            for k in range(negs):
                hit = dev == table[k : k + 1]
                named = named + jnp.where(hit, 1.0, 0.0)
                wanted = wanted + jnp.where(hit, table[8 + k : 9 + k] + 1.0, 0.0)
            named_all.append(named)
            rows_all.append(wanted)
        named = jnp.concatenate(named_all, axis=0)
        wanted = jnp.concatenate(rows_all, axis=0).astype(BF16)
        ranks = (named * (mm(named.astype(BF16), before) + 1.0)).astype(BF16)
        ranks_out[half][...] = ranks
        ids, tok = [], []
        index = iota((8, toks), 1).astype(F32).astype(BF16)
        for s, source in enumerate(sources[half]):
            pick = pick_of(s, groups, cap)
            hit = hits_of(pick, ranks, cap)
            hot = hit.astype(BF16)
            moved = mm(hot, source[:toks, :]).astype(BF16)
            for g in range(groups):
                first = (g * SIDE + s) * cap
                outs[half][first : first + cap, :] = moved[g * cap : (g + 1) * cap]
            row = jnp.where(hit, mm(pick, wanted), 0.0).astype(BF16)
            ids.append(mm(jnp.ones((8, toks), BF16), row, NT)[0:1])
            tok.append(mm(index, hot, NT)[0:1])
        codes = jnp.concatenate(ids + tok, axis=0)
        codes = jnp.concatenate([codes, jnp.zeros_like(codes)], axis=0)
        codes = jnp.concatenate(
            [codes, jnp.zeros((16, half_width - codes.shape[1]), F32)], axis=1
        )
        outs[half][groups * SIDE * cap :, :] = codes.astype(BF16)


def mid(place, shift, first, second, groups, reps, cap, negs):
    rows, half_width = first[0].shape
    slots = jax.ShapeDtypeStruct((groups * SIDE * cap + 16, half_width), BF16)
    ranks = jax.ShapeDtypeStruct((SIDE * groups, rows - 16), BF16)
    return call(
        functools.partial(mid_kernel, shift, cap, groups, reps, negs), "mid", 1,
        [full((rows, half_width))] * (2 * SIDE),
        [full(slots.shape)] * 2 + [full(ranks.shape)] * 2,
        [slots, slots, ranks, ranks], [], LIGHT,
    )(place, *first, *second)


def inside_kernel(temper, place_ref, p_ref, q_ref, out_ref, top, total):
    step = pl.program_id(0)

    @pl.when(step == 0)
    def _():
        top[...] = jnp.full(top.shape, LOW, F32)
        total[...] = jnp.zeros(total.shape, F32)

    scores = temper * mm(p_ref[...], q_ref[...], NT)
    high = jnp.maximum(top[...], jnp.max(scores, axis=0, keepdims=True))
    total[...] = total[...] * jnp.exp(top[...] - high) + jnp.sum(
        jnp.exp(scores - high), axis=0, keepdims=True
    )
    top[...] = high

    @pl.when(step == pl.num_programs(0) - 1)
    def _():
        out_ref[...] = top[...] + jnp.log(total[...])


def inside(place, gathered, queries, temper):
    toks, width = queries.shape
    steps = gathered.shape[0] // (CORES * toks)
    return call(
        functools.partial(inside_kernel, temper), "inside", steps,
        [pl.BlockSpec((CORES * toks, width), lambda s, _: (s, 0)), full((toks, width))],
        full((1, toks)), jax.ShapeDtypeStruct((1, toks), F32),
        [pltpu.VMEM((1, toks), F32), pltpu.VMEM((1, toks), F32)], MIDDLE,
    )(place, gathered, queries)


def asking_rows(first, second, base, cap):
    def piece(ref, s):
        return ref[base + s * cap : base + (s + 1) * cap, :]

    pairs = [(dx, dy) for dx in range(SIDE) for dy in range(SIDE)]
    one = jnp.concatenate([piece(first[dy], dx) for dx, dy in pairs], axis=0)
    two = jnp.concatenate([piece(second[dx], dy) for dx, dy in pairs], axis=0)
    return one, two


def source_mask(place_ref, reps, cap):
    shape = (reps, reps * cap)
    dx = iota(shape, 1) // (SIDE * cap)
    dy = iota(shape, 1) // cap % SIDE
    x = (place_ref[2] + SIDE - dx) % SIDE
    y = (place_ref[3] + SIDE - dy) % SIDE
    return iota(shape, 0) == x * SIDE + y


def hard_kernel(
    reps, cap, temper, place_ref, *refs
):
    first, second, exts = refs[0:4], refs[4:8], refs[8:12]
    p_ref, inside_ref = refs[12:14]
    out_first, out_second = refs[14:18], refs[18:22]
    hs_ref, code_ref, part_ref, top, total = refs[22:]
    step = pl.program_id(0)
    levels = pl.num_programs(0) - 1
    toks = inside_ref.shape[1]
    half_width = p_ref.shape[1] // 2
    slots = reps * cap
    groups = code_ref.shape[0] // 2
    source = source_mask(place_ref, reps, cap)

    @pl.when(step == 0)
    def _():
        top[...] = jnp.full(top.shape, LOW, F32)
        total[...] = jnp.zeros(total.shape, F32)
        table = jnp.concatenate([ext[...] for ext in exts], axis=0)[:, : groups * cap]
        shape = (table.shape[0], slots)
        row = iota(shape, 0)
        dx, dy = iota(shape, 1) // (SIDE * cap), iota(shape, 1) // cap % SIDE
        here = row // 16 == dy
        is_id = here & (row % 16 == dx)
        is_tok = here & (row % 16 == SIDE + dx)
        lane = iota((groups * cap, slots), 0)
        for g in range(groups):
            to_slot = lane == g * cap + iota((groups * cap, slots), 1) % cap
            laid = mm(table, to_slot.astype(BF16))
            ids = jnp.sum(jnp.where(is_id, laid, 0.0), axis=0, keepdims=True)
            tok = jnp.sum(jnp.where(is_tok, laid, 0.0), axis=0, keepdims=True)
            code_ref[g : g + 1, :] = ids.astype(I32)
            code_ref[groups + g : groups + g + 1, :] = tok.astype(I32)

    @pl.when(step < levels)
    def _():
        level = (place_ref[0] + step) % levels
        for core in range(CORES):
            group = CORES * level + core
            ids = code_ref[pl.ds(group, 1), :]
            tok = code_ref[pl.ds(groups + group, 1), :]
            valid = ids > 0
            base = core * SIDE * cap
            one, two = asking_rows(first, second, base, cap)
            passages = p_ref[core * toks : (core + 1) * toks, :]
            cross = mm(passages[:, :half_width], one, NT) + mm(passages[:, half_width:], two, NT)
            hit = iota((toks, slots), 0) + 1 == ids
            hs = temper * jnp.sum(jnp.where(hit, cross, 0.0), axis=0, keepdims=True)
            hs_ref[pl.ds(group, 1), :] = hs
            served = mm(hit.astype(BF16), passages, TN).astype(BF16)
            for dx in range(SIDE):
                for dy in range(SIDE):
                    at = (dx * SIDE + dy) * cap
                    out_first[dy][base + dx * cap : base + (dx + 1) * cap, :] = served[
                        at : at + cap, :half_width
                    ]
                    out_second[dx][base + dy * cap : base + (dy + 1) * cap, :] = served[
                        at : at + cap, half_width:
                    ]
            token = ((iota((toks, slots), 0) == tok) & valid).astype(BF16)
            live = source & valid
            parts = jnp.concatenate(
                [split3(jnp.where(live, hs, 0.0)), live.astype(BF16)], axis=0
            )
            laid = mm(parts, token, NT)
            there = laid[3 * reps :] > 0.5
            value = laid[:reps] + laid[reps : 2 * reps] + laid[2 * reps : 3 * reps]
            value = jnp.where(there, value, LOW)
            high = jnp.maximum(top[...], value)
            total[...] = total[...] * jnp.exp(top[...] - high) + jnp.where(
                there, jnp.exp(value - high), 0.0
            )
            top[...] = high

    @pl.when(step == levels)
    def _():
        part = jnp.where(total[...] > 0.0, top[...] + jnp.log(total[...]), LOW)
        within = inside_ref[...]
        high = jnp.maximum(part, within)
        both = high + jnp.log(jnp.exp(part - high) + jnp.exp(within - high))
        own = iota(part.shape, 0) == rep_of(place_ref[2], place_ref[3])
        part_ref[...] = jnp.broadcast_to(jnp.where(own, both, part)[None], part_ref.shape)
        pieces = split3(hs_ref[...])
        which = pieces.shape[0]
        lanes = groups * cap
        for line in range(SIDE):
            for half, out in ((0, out_first[line]), (1, out_second[line])):
                table = jnp.zeros((16, lanes), F32)
                for s in range(SIDE):
                    dx, dy = (s, line) if half == 0 else (line, s)
                    at = (dx * SIDE + dy) * cap
                    to_lane = (
                        iota((slots, lanes), 0) == at + iota((slots, lanes), 1) % cap
                    ).astype(BF16)
                    laid = mm(pieces, to_lane)
                    keep = iota((which, lanes), 0) % groups == iota((which, lanes), 1) // cap
                    laid = jnp.where(keep, laid, 0.0)
                    to_row = (
                        iota((16, which), 0) == SIDE * (iota((16, which), 1) // groups) + s
                    ).astype(BF16)
                    table = table + mm(to_row, laid.astype(BF16))
                table = jnp.concatenate(
                    [table, jnp.zeros((16, half_width - lanes), F32)], axis=1
                )
                out[0:16, :] = table.astype(BF16)


def hard(place, first, second, gathered, within, temper, reps, cap):
    rows, half_width = first[0].shape
    toks = within.shape[1]
    groups = gathered.shape[0] // toks
    levels = groups // CORES
    slots = reps * cap
    per = CORES * SIDE * cap

    def level(s, place):
        return lax.select(s < levels, (place[0] + s) % levels, (place[0] + levels - 1) % levels)

    ins = pl.BlockSpec((per, half_width), lambda s, place: (level(s, place), 0))
    outs = pl.BlockSpec(
        (per, half_width),
        lambda s, place: (lax.select(s < levels, (place[0] + s) % levels, levels), 0),
    )
    ext = pl.BlockSpec((16, half_width), lambda s, place: (groups * SIDE * cap // 16, 0))
    made = call(
        functools.partial(hard_kernel, reps, cap, temper), "hard", levels + 1,
        [ins] * 8 + [ext] * 4
        + [pl.BlockSpec((CORES * toks, CORES * half_width),
                        lambda s, _: (lax.min(s, levels - 1), 0)), full((1, toks))],
        [outs] * 8 + [full((groups, slots)), full((2 * groups, slots)), full((reps, reps, toks))],
        [jax.ShapeDtypeStruct((rows, half_width), BF16)] * 8
        + [jax.ShapeDtypeStruct((groups, slots), F32),
           jax.ShapeDtypeStruct((2 * groups, slots), I32),
           jax.ShapeDtypeStruct((reps, reps, toks), F32)],
        [pltpu.VMEM((reps, toks), F32), pltpu.VMEM((reps, toks), F32)], LIGHT,
    )(place, *first, *second, *first, gathered, within)
    return made[0:4], made[4:8], made[8], made[9], made[10]


def own_row(lt_ref, rep):
    lt = lt_ref[...]
    return jnp.sum(jnp.where(iota(lt.shape, 0) == rep, lt, 0.0), axis=0, keepdims=True)


def column_kernel(reps, cap, temper, own_core, place_ref, code_ref, hs_ref, lt_ref, *refs):
    first, second = refs[0:4], refs[4:8]
    p_ref, q_ref, gp_ref = refs[8:]
    step = pl.program_id(0)
    toks, width = q_ref.shape
    half_width = width // 2
    slots = reps * cap
    groups = code_ref.shape[0] // 2
    core = place_ref[1] if own_core else 1 - place_ref[1]
    group = CORES * ((place_ref[0] + step) % pl.num_programs(0)) + core
    ids = code_ref[pl.ds(group, 1), :]
    tok = code_ref[pl.ds(groups + group, 1), :]
    valid = ids > 0
    token = ((iota((toks, slots), 0) == tok) & valid).astype(BF16)
    found = mm(split3(lt_ref[...]), token)
    found = found[:reps] + found[reps : 2 * reps] + found[2 * reps :]
    source = source_mask(place_ref, reps, cap)
    log_slot = jnp.sum(jnp.where(source, found, 0.0), axis=0, keepdims=True)
    d_hard = jnp.where(valid, jnp.exp(hs_ref[pl.ds(group, 1), :] - log_slot), 0.0)
    hot = jnp.where(iota((toks, slots), 0) + 1 == ids, d_hard, 0.0).astype(BF16)
    queries = q_ref[...]
    scores = temper * mm(p_ref[...], queries, NT)
    d_scores = jnp.exp(scores - own_row(lt_ref, rep_of(place_ref[2], place_ref[3])))
    if own_core:
        eye = (iota((toks, toks), 0) == iota((toks, toks), 1)) & (step == 0)
        d_scores = d_scores - jnp.where(eye, 1.0, 0.0)
    both = jnp.concatenate([hot, d_scores.astype(BF16)], axis=1)
    one, two = asking_rows(first, second, 0, cap)
    one = jnp.concatenate([one, queries[:, :half_width]], axis=0)
    two = jnp.concatenate([two, queries[:, half_width:]], axis=0)
    gp_ref[0, :, :half_width] = (temper * mm(both, one)).astype(BF16)
    gp_ref[0, :, half_width:] = (temper * mm(both, two)).astype(BF16)


def column(own_core, place, codes, hard_scores, log_total, first, second, gathered, queries,
           temper, cap):
    reps = log_total.shape[0]
    toks, width = queries.shape
    levels = gathered.shape[0] // (CORES * toks)

    def core(place):
        return place[1] if own_core else 1 - place[1]

    slots = pl.BlockSpec(
        (SIDE * cap, width // 2),
        lambda s, place: (CORES * ((place[0] + s) % levels) + core(place), 0),
    )
    return call(
        functools.partial(column_kernel, reps, cap, temper, own_core),
        "own" if own_core else "other", levels,
        [full(codes.shape), full(hard_scores.shape), full(log_total.shape)] + [slots] * 8
        + [pl.BlockSpec((toks, width), lambda s, place: (CORES * s + core(place), 0)),
           full((toks, width))],
        pl.BlockSpec((1, toks, width), lambda s, _: (s, 0, 0)),
        jax.ShapeDtypeStruct((levels, toks, width), BF16), [], LIGHT,
    )(place, codes, hard_scores, log_total, *first, *second, gathered, queries)


def inner_kernel(temper, place_ref, lt_ref, p_ref, q_ref, gq_ref, loss_ref, acc):
    step = pl.program_id(0)
    toks, width = q_ref.shape
    lt_own = own_row(lt_ref, rep_of(place_ref[2], place_ref[3]))
    passages = p_ref[...]
    scores = temper * mm(passages, q_ref[...], NT)
    row = iota(scores.shape, 0) - toks * place_ref[1]
    eye = (row == iota(scores.shape, 1)) & (step == 0)
    d_scores = (jnp.exp(scores - lt_own) - jnp.where(eye, 1.0, 0.0)).astype(BF16)
    new = mm(d_scores, passages, TN)

    @pl.when(step == 0)
    def _():
        acc[...] = new
        loss_ref[...] = lt_own - jnp.sum(jnp.where(eye, scores, 0.0), axis=0, keepdims=True)

    @pl.when(step > 0)
    def _():
        acc[...] += new

    @pl.when(step == pl.num_programs(0) - 1)
    def _():
        gq_ref[...] = acc[...]


def inner(place, log_total, gathered, queries, temper):
    toks, width = queries.shape
    return call(
        functools.partial(inner_kernel, temper), "inner", gathered.shape[0] // (CORES * toks),
        [full(log_total.shape), pl.BlockSpec((CORES * toks, width), lambda s, _: (s, 0)),
         full((toks, width))],
        [full((toks, width)), full((1, toks))],
        [jax.ShapeDtypeStruct((toks, width), F32), jax.ShapeDtypeStruct((1, toks), F32)],
        [pltpu.VMEM((toks, width), F32)], LIGHT,
    )(place, log_total, gathered, queries)


def reduce_kernel(half, cap, groups, place_ref, lt_ref, *refs):
    ranks, rows, outs = refs[0:4], refs[4:8], refs[8:12]
    toks = lt_ref.shape[1]
    slots = groups * cap
    for s in range(SIDE):
        lt = own_row(lt_ref, source_of(place_ref, half, s))
        pick = pick_of(s, groups, cap)
        part = (iota((16, toks), 0) % SIDE == s) & (iota((16, toks), 0) < 3 * SIDE)
        weights, values = [], []
        for line in range(SIDE):
            ext = rows[line][slots * SIDE :, :slots]
            hs = mm(ext, part.astype(BF16), TN)
            hit = hits_of(pick, ranks[line][...], cap)
            weights.append(jnp.where(hit, jnp.exp(hs - lt), 0.0).astype(BF16))
            for g in range(groups):
                at = (g * SIDE + s) * cap
                values.append(rows[line][at : at + cap, :])
        total = mm(jnp.concatenate(weights, axis=0), jnp.concatenate(values, axis=0), TN)
        outs[s][...] = total.astype(outs[s].dtype)


def reduce(place, half, log_total, ranks, rows, groups, cap):
    toks = log_total.shape[1]
    shape = (toks, rows[0].shape[1])
    return call(
        functools.partial(reduce_kernel, half, cap, groups), "reduce", 1,
        [full(log_total.shape)] + [full(ranks[0].shape)] * 4 + [full(rows[0].shape)] * 4,
        [full(shape)] * 4,
        [jax.ShapeDtypeStruct(shape, F32)] + [jax.ShapeDtypeStruct(shape, BF16)] * 3, [], LIGHT,
    )(place, log_total, *ranks, *rows)


def final_kernel(temper, place_ref, gq_ref, *refs):
    out_ref = refs[8]
    half_width = out_ref.shape[1] // 2
    for half in range(2):
        lanes = slice(half * half_width, (half + 1) * half_width)
        total = gq_ref[:, lanes]
        for ref in refs[4 * half : 4 * half + 4]:
            total = total + ref[...].astype(F32)
        out_ref[:, lanes] = (temper * total).astype(BF16)


def final(place, within, first, second, temper):
    shape = within.shape
    return call(
        functools.partial(final_kernel, temper), "final", 1,
        [full(shape)] + [full(first[0].shape)] * 8,
        full(shape), jax.ShapeDtypeStruct(shape, BF16), [], HEAVY,
    )(place, within, *first, *second)


def along_z(x, shift, groups):
    return lax.ppermute(x, "grp", [(i, (i + CORES * shift) % groups) for i in range(groups)])


def other_core(x, groups):
    return lax.ppermute(x, "grp", [(i, i ^ 1) for i in range(groups)])


def along(x, half, shift):
    pairs = []
    for i in range(SIDE * SIDE):
        a, b = i // SIDE, i % SIDE
        pairs.append((i, rep_of(a + shift, b) if half == 0 else rep_of(a, b + shift)))
    return lax.ppermute(x, "rep", pairs)


def gather_group(block, core, groups):
    half = block.shape[0] // 2
    below = along_z(block, 1, groups)
    above = along_z(block, -1, groups)
    far = jnp.concatenate(
        [along_z(below[:half], 1, groups), along_z(above[half:], -1, groups)], axis=0
    )
    own = jnp.stack([block, above, far, below])
    theirs = other_core(own, groups)
    first = core == 0
    return jnp.stack([jnp.where(first, own, theirs), jnp.where(first, theirs, own)], axis=1)


def scatter_group(own, other, groups):
    half = own.shape[1] // 2
    whole = own.astype(F32) + other_core(other, groups).astype(F32)
    up = along_z(whole[2, :half].astype(BF16), 1, groups).astype(F32)
    down = along_z(whole[2, half:].astype(BF16), -1, groups).astype(F32)
    to_above = jnp.concatenate([whole[1, :half] + up, whole[1, half:]], axis=0)
    to_below = jnp.concatenate([whole[3, :half], whole[3, half:] + down], axis=0)
    from_below = along_z(to_above.astype(BF16), 1, groups).astype(F32)
    from_above = along_z(to_below.astype(BF16), -1, groups).astype(F32)
    return (whole[0] + from_below + from_above).astype(BF16)


def shards(queries, passages, neg_device, neg_row):
    toks, width = queries.shape
    negs = neg_device.shape[1]
    groups = lax.axis_size("grp")
    reps = lax.axis_size("rep")
    cap = 8 * toks // (groups * reps)
    half_width = width // 2
    temper = 3.0 / math.sqrt(width)
    grp, rep = lax.axis_index("grp"), lax.axis_index("rep")
    place = jnp.stack([grp // CORES, grp % CORES, rep // SIDE, rep % SIDE]).astype(I32)

    lines = jnp.pad(jnp.stack([neg_device.T, neg_row.T]), ((0, 0), (0, 8 - negs), (0, 0)))
    lines = jnp.pad(lines.reshape(16, toks), ((0, 0), (0, half_width - toks))).astype(BF16)
    sources = []
    for half in range(2):
        block = queries[:, half * half_width : (half + 1) * half_width]
        block = jnp.concatenate([block, lines], axis=0)
        sources.append([block] + [along(block, half, s) for s in range(1, SIDE)])
    gathered = gather_group(passages, grp % CORES, groups).reshape(groups * toks, width)

    first, second, ranks_first, ranks_second = [], [], [], []
    for shift in range(SIDE):
        one, two, rank_one, rank_two = mid(place, shift, *sources, groups, reps, cap, negs)
        first.append(along(one, 1, shift) if shift else one)
        second.append(along(two, 0, shift) if shift else two)
        ranks_first.append(rank_one)
        ranks_second.append(rank_two)

    within = inside(place, gathered, queries, temper)
    back_first, back_second, hard_scores, codes, part = hard(
        place, first, second, gathered, within, temper, reps, cap
    )
    parts = lax.all_to_all(part, "rep", split_axis=0, concat_axis=0, tiled=True)
    parts, back_first, back_second = lax.optimization_barrier((parts, back_first, back_second))
    high = jnp.max(parts, axis=0)
    log_total = high + jnp.log(jnp.sum(jnp.exp(parts - high), axis=0))

    back_first = [along(v, 1, -s) if s else v for s, v in enumerate(back_first)]
    back_second = [along(v, 0, -s) if s else v for s, v in enumerate(back_second)]

    def column_of(own_core):
        return column(own_core, place, codes, hard_scores, log_total, first, second, gathered,
                      queries, temper, cap)

    other = column_of(False)
    grad_passages = scatter_group(column_of(True), other, groups)
    grad_inner, losses = inner(place, log_total, gathered, queries, temper)

    sums = []
    for half, ranks, rows in ((0, ranks_first, back_first), (1, ranks_second, back_second)):
        made = reduce(place, half, log_total, ranks, rows, groups, cap)
        sums.append([along(v, half, -s) if s else v for s, v in enumerate(made)])
    grad_queries = final(place, grad_inner, *sums, temper)
    return (losses.reshape(toks), grad_queries, grad_passages)


def solution(mesh):
    in_specs = (
        P(("grp", "rep"), None),
        P(("grp", "rep"), None),
        P(("grp", "rep"), None),
        P(("grp", "rep"), None),
    )
    out_specs = (P(("grp", "rep")), P(("grp", "rep"), None), P(("grp", "rep"), None))
    return jax.shard_map(shards, mesh=mesh, in_specs=in_specs, out_specs=out_specs, check_vma=False)
```

```python
import functools
import math

import jax
import jax.numpy as jnp
from jax import lax
from jax.experimental import pallas as pl
from jax.experimental.pallas import tpu as pltpu
from jax.sharding import PartitionSpec as P

F32 = jnp.float32
BF16 = jnp.bfloat16
I32 = jnp.int32
LOW = -1e30
NT = (((1,), (1,)), ((), ()))
TN = (((0,), (0,)), ((), ()))
NN = (((1,), (0,)), ((), ()))
VMEM_LIMIT = 60 * 1024 * 1024


def mm(a, b, dims=NN):
    return lax.dot_general(a, b, dims, preferred_element_type=F32)


def iota(shape, dim):
    return lax.broadcasted_iota(I32, shape, dim)


def split3(x):
    a = x.astype(BF16)
    rest = x - a.astype(F32)
    b = rest.astype(BF16)
    c = (rest - b.astype(F32)).astype(BF16)
    return jnp.concatenate([a, b, c], axis=0)


def full(shape):
    return pl.BlockSpec(shape, lambda *_: (0,) * len(shape))


def call(kernel, name, steps, ins, outs, shapes, scratch, weight):
    return pl.pallas_call(
        kernel,
        grid_spec=pltpu.PrefetchScalarGridSpec(
            num_scalar_prefetch=1, grid=(steps,), in_specs=ins, out_specs=outs,
            scratch_shapes=scratch,
        ),
        out_shape=shapes,
        compiler_params=pltpu.CompilerParams(
            dimension_semantics=("arbitrary",), vmem_limit_bytes=VMEM_LIMIT
        ),
        cost_estimate=pl.CostEstimate(flops=weight, bytes_accessed=1 << 16, transcendentals=0),
        name=name,
    )


LIGHT, MIDDLE, HEAVY = 1 << 20, 1 << 32, 1 << 39
SIDE = 4
CORES = 2


def rep_of(x, y):
    return x % SIDE * SIDE + y % SIDE


def columns_of(place_ref, half, shift):
    x, y = place_ref[1], place_ref[2]
    return rep_of(x, y + shift) if half == 0 else rep_of(x + shift, y)


def source_of(place_ref, half, shift):
    x, y = place_ref[1], place_ref[2]
    return rep_of(x + SIDE - shift, y) if half == 0 else rep_of(x, y + SIDE - shift)


def hits_of(ranks, groups, cap):
    shape = (ranks.shape[0] * cap, ranks.shape[0])
    pick = (iota(shape, 1) == iota(shape, 0) // cap).astype(BF16)
    spread = mm(pick, ranks)
    return pick, spread == (iota(spread.shape, 0) % cap + 1).astype(F32)


def mid_kernel(shift, cap, groups, reps, negs, place_ref, *refs):
    sources = (refs[0:SIDE], refs[SIDE : 2 * SIDE])
    outs, ranks_out = refs[2 * SIDE : 2 * SIDE + 2], refs[2 * SIDE + 2 :]
    rows, half_width = sources[0][0].shape
    toks = rows - 16
    slots = groups * cap
    before = (iota((toks, toks), 0) < iota((toks, toks), 1)).astype(BF16)
    for half in range(2):
        col = columns_of(place_ref, half, shift)
        dev = (iota((groups, toks), 0) * reps + col).astype(F32)
        named_all, rows_all = [], []
        for source in sources[half]:
            table = source[toks:, :toks].astype(F32)
            named = jnp.zeros((groups, toks), F32)
            wanted = jnp.zeros((groups, toks), F32)
            for k in range(negs):
                hit = dev == table[k : k + 1]
                named = named + jnp.where(hit, 1.0, 0.0)
                wanted = wanted + jnp.where(hit, table[8 + k : 9 + k] + 1.0, 0.0)
            named_all.append(named)
            rows_all.append(wanted)
        named = jnp.concatenate(named_all, axis=0)
        wanted = jnp.concatenate(rows_all, axis=0).astype(BF16)
        ranks = (named * (mm(named.astype(BF16), before) + 1.0)).astype(BF16)
        ranks_out[half][...] = ranks
        pick, hit = hits_of(ranks, groups, cap)
        hot = hit.astype(BF16)
        row = jnp.where(hit, mm(pick, wanted), 0.0).astype(BF16)
        ids = mm(jnp.ones((8, toks), BF16), row, NT)[0:1]
        tok = mm(iota((8, toks), 1).astype(F32).astype(BF16), hot, NT)[0:1]
        for s, source in enumerate(sources[half]):
            moved = mm(hot[s * slots : (s + 1) * slots], source[:toks, :]).astype(BF16)
            for g in range(groups):
                first = (g * SIDE + s) * cap
                outs[half][first : first + cap, :] = moved[g * cap : (g + 1) * cap]
        codes = [v[:, s * slots : (s + 1) * slots] for v in (ids, tok) for s in range(SIDE)]
        codes = jnp.concatenate(codes + [jnp.zeros((8, slots), F32)], axis=0)
        codes = jnp.concatenate([codes, jnp.zeros((16, half_width - slots), F32)], axis=1)
        outs[half][groups * SIDE * cap :, :] = codes.astype(BF16)


def mid(place, shift, first, second, groups, reps, cap, negs):
    rows, half_width = first[0].shape
    slots = jax.ShapeDtypeStruct((groups * SIDE * cap + 16, half_width), BF16)
    ranks = jax.ShapeDtypeStruct((SIDE * groups, rows - 16), BF16)
    return call(
        functools.partial(mid_kernel, shift, cap, groups, reps, negs), "mid", 1,
        [full((rows, half_width))] * (2 * SIDE),
        [full(slots.shape)] * 2 + [full(ranks.shape)] * 2,
        [slots, slots, ranks, ranks], [], LIGHT,
    )(place, *first, *second)


def inside_kernel(temper, place_ref, p_ref, q_ref, out_ref, top, total):
    step = pl.program_id(0)

    @pl.when(step == 0)
    def _():
        top[...] = jnp.full(top.shape, LOW, F32)
        total[...] = jnp.zeros(total.shape, F32)

    scores = temper * mm(p_ref[...], q_ref[...], NT)
    high = jnp.maximum(top[...], jnp.max(scores, axis=0, keepdims=True))
    total[...] = total[...] * jnp.exp(top[...] - high) + jnp.sum(
        jnp.exp(scores - high), axis=0, keepdims=True
    )
    top[...] = high

    @pl.when(step == pl.num_programs(0) - 1)
    def _():
        out_ref[...] = top[...] + jnp.log(total[...])


def inside(place, gathered, queries, temper):
    toks, width = queries.shape
    return call(
        functools.partial(inside_kernel, temper), "inside", 2,
        [pl.BlockSpec((gathered.shape[0] // 2, width), lambda s, _: (s, 0)), full((toks, width))],
        full((1, toks)), jax.ShapeDtypeStruct((1, toks), F32),
        [pltpu.VMEM((1, toks), F32), pltpu.VMEM((1, toks), F32)], MIDDLE,
    )(place, gathered, queries)


def asking_rows(first, second, base, cap):
    def piece(ref, s):
        return ref[base + s * cap : base + (s + 1) * cap, :]

    pairs = [(dx, dy) for dx in range(SIDE) for dy in range(SIDE)]
    one = jnp.concatenate([piece(first[dy], dx) for dx, dy in pairs], axis=0)
    two = jnp.concatenate([piece(second[dx], dy) for dx, dy in pairs], axis=0)
    return one, two


def source_mask(place_ref, reps, cap):
    shape = (reps, reps * cap)
    dx = iota(shape, 1) // (SIDE * cap)
    dy = iota(shape, 1) // cap % SIDE
    x = (place_ref[1] + SIDE - dx) % SIDE
    y = (place_ref[2] + SIDE - dy) % SIDE
    return iota(shape, 0) == x * SIDE + y


def hard_kernel(reps, cap, temper, place_ref, *refs):
    first, second, exts = refs[0:4], refs[4:8], refs[8:12]
    p_ref, inside_ref = refs[12:14]
    out_first, out_second = refs[14:18], refs[18:22]
    hs_ref, code_ref, part_ref, top, total = refs[22:]
    step = pl.program_id(0)
    levels = pl.num_programs(0) - 1
    toks = inside_ref.shape[1]
    half_width = p_ref.shape[1] // 2
    slots = reps * cap
    groups = code_ref.shape[0] // 2
    source = source_mask(place_ref, reps, cap)

    @pl.when(step == 0)
    def _():
        top[...] = jnp.full(top.shape, LOW, F32)
        total[...] = jnp.zeros(total.shape, F32)
        table = jnp.concatenate([ext[...] for ext in exts], axis=0)[:, : groups * cap]
        shape = (groups * cap, groups * slots)
        lane, slot = iota(shape, 0), iota(shape, 1)
        to_slot = (lane == slot // slots * cap + slot % cap).astype(BF16)
        laid = mm(table, to_slot)
        row, slot = iota(laid.shape, 0), iota(laid.shape, 1) % slots
        dx, dy = slot // (SIDE * cap), slot // cap % SIDE
        want = dy * 16 + dx
        ids = jnp.sum(jnp.where(row == want, laid, 0.0), axis=0, keepdims=True).astype(I32)
        tok = jnp.sum(jnp.where(row == want + SIDE, laid, 0.0), axis=0, keepdims=True).astype(I32)
        for g in range(groups):
            code_ref[g : g + 1, :] = ids[:, g * slots : (g + 1) * slots]
            code_ref[groups + g : groups + g + 1, :] = tok[:, g * slots : (g + 1) * slots]

    @pl.when(step < levels)
    def _():
        values = []
        for core in range(CORES):
            group = CORES * step + core
            ids = code_ref[pl.ds(group, 1), :]
            tok = code_ref[pl.ds(groups + group, 1), :]
            valid = ids > 0
            base = core * SIDE * cap
            one, two = asking_rows(first, second, base, cap)
            passages = p_ref[core * toks : (core + 1) * toks, :]
            cross = mm(passages, jnp.concatenate([one, two], axis=1), NT)
            hit = iota((toks, slots), 0) + 1 == ids
            hs = temper * jnp.sum(jnp.where(hit, cross, 0.0), axis=0, keepdims=True)
            hs_ref[pl.ds(group, 1), :] = hs
            served = mm(hit.astype(BF16), passages, TN).astype(BF16)
            for dx in range(SIDE):
                for dy in range(SIDE):
                    at = (dx * SIDE + dy) * cap
                    out_first[dy][base + dx * cap : base + (dx + 1) * cap, :] = served[
                        at : at + cap, :half_width
                    ]
                    out_second[dx][base + dy * cap : base + (dy + 1) * cap, :] = served[
                        at : at + cap, half_width:
                    ]
            token = ((iota((toks, slots), 0) == tok) & valid).astype(BF16)
            live = source & valid
            parts = jnp.concatenate(
                [split3(jnp.where(live, hs, 0.0)), live.astype(BF16)], axis=0
            )
            laid = mm(parts, token, NT)
            there = laid[3 * reps :] > 0.5
            value = laid[:reps] + laid[reps : 2 * reps] + laid[2 * reps : 3 * reps]
            values.append((there, jnp.where(there, value, LOW)))
        high = top[...]
        for there, value in values:
            high = jnp.maximum(high, value)
        new = total[...] * jnp.exp(top[...] - high)
        for there, value in values:
            new = new + jnp.where(there, jnp.exp(value - high), 0.0)
        total[...] = new
        top[...] = high

    @pl.when(step == levels)
    def _():
        part = jnp.where(total[...] > 0.0, top[...] + jnp.log(total[...]), LOW)
        within = inside_ref[...]
        high = jnp.maximum(part, within)
        both = high + jnp.log(jnp.exp(part - high) + jnp.exp(within - high))
        own = iota(part.shape, 0) == rep_of(place_ref[1], place_ref[2])
        part_ref[...] = jnp.broadcast_to(jnp.where(own, both, part)[None], part_ref.shape)
        pieces = split3(hs_ref[...]).astype(F32)
        pieces = jnp.concatenate([pieces, jnp.zeros((groups, slots), F32)], axis=0)
        pieces = jnp.concatenate(
            [pieces, jnp.zeros((4 * groups, half_width - slots), F32)], axis=1
        ).astype(BF16)
        for out in (*out_first, *out_second):
            out[: 4 * groups, :] = pieces


def hard(place, first, second, gathered, within, temper, reps, cap):
    rows, half_width = first[0].shape
    toks = within.shape[1]
    groups = gathered.shape[0] // toks
    levels = groups // CORES
    slots = reps * cap
    per = CORES * SIDE * cap
    ins = pl.BlockSpec((per, half_width), lambda s, _: (lax.min(s, levels - 1), 0))
    outs = pl.BlockSpec((per, half_width), lambda s, _: (s, 0))
    ext = pl.BlockSpec((16, half_width), lambda s, _: (groups * SIDE * cap // 16, 0))
    made = call(
        functools.partial(hard_kernel, reps, cap, temper), "hard", levels + 1,
        [ins] * 8 + [ext] * 4
        + [pl.BlockSpec((CORES * toks, CORES * half_width),
                        lambda s, _: (lax.min(s, levels - 1), 0)), full((1, toks))],
        [outs] * 8 + [full((groups, slots)), full((2 * groups, slots)), full((reps, reps, toks))],
        [jax.ShapeDtypeStruct((groups * SIDE * cap + 4 * groups, half_width), BF16)] * 8
        + [jax.ShapeDtypeStruct((groups, slots), F32),
           jax.ShapeDtypeStruct((2 * groups, slots), I32),
           jax.ShapeDtypeStruct((reps, reps, toks), F32)],
        [pltpu.VMEM((reps, toks), F32), pltpu.VMEM((reps, toks), F32)], LIGHT,
    )(place, *first, *second, *first, gathered, within)
    return made[0:4], made[4:8], made[8], made[9], made[10]


def own_row(lt_ref, rep):
    lt = lt_ref[...]
    return jnp.sum(jnp.where(iota(lt.shape, 0) == rep, lt, 0.0), axis=0, keepdims=True)


def column_kernel(reps, cap, temper, place_ref, code_ref, hs_ref, lt_ref, *refs):
    first, second = refs[0:4], refs[4:8]
    p_ref, q_ref, gp_ref, d_ref = refs[8:]
    step = pl.program_id(0)
    toks, width = q_ref.shape
    half_width = width // 2
    slots = reps * cap
    groups = code_ref.shape[0] // 2

    @pl.when(step == 0)
    def _():
        log_parts = split3(lt_ref[...])
        source = source_mask(place_ref, reps, cap)
        rows = []
        for g in range(groups):
            valid = code_ref[g : g + 1, :] > 0
            tok = code_ref[groups + g : groups + g + 1, :]
            token = ((iota((toks, slots), 0) == tok) & valid).astype(BF16)
            found = mm(log_parts, token)
            found = found[:reps] + found[reps : 2 * reps] + found[2 * reps :]
            log_slot = jnp.sum(jnp.where(source, found, 0.0), axis=0, keepdims=True)
            rows.append(jnp.where(valid, jnp.exp(hs_ref[g : g + 1, :] - log_slot), 0.0))
        d_ref[...] = jnp.concatenate(rows, axis=0)

    queries = q_ref[...]
    lt_own = own_row(lt_ref, rep_of(place_ref[1], place_ref[2]))
    for core in range(CORES):
        group = CORES * step + core
        here = pl.ds(core * toks, toks)
        ids = code_ref[pl.ds(group, 1), :]
        d_hard = d_ref[pl.ds(group, 1), :]
        hot = jnp.where(iota((toks, slots), 0) + 1 == ids, d_hard, 0.0).astype(BF16)
        scores = temper * mm(p_ref[here, :], queries, NT)
        eye = (iota((toks, toks), 0) == iota((toks, toks), 1)) & (group == place_ref[0])
        d_scores = (jnp.exp(scores - lt_own) - jnp.where(eye, 1.0, 0.0)).astype(BF16)
        both = jnp.concatenate([hot, d_scores], axis=1)
        one, two = asking_rows(first, second, core * SIDE * cap, cap)
        rows = jnp.concatenate([jnp.concatenate([one, two], axis=1), queries], axis=0)
        gp_ref[here, :] = (temper * mm(both, rows)).astype(BF16)


def column(place, codes, hard_scores, log_total, first, second, gathered, queries, temper, cap):
    reps = log_total.shape[0]
    toks, width = queries.shape
    slots = pl.BlockSpec((CORES * SIDE * cap, width // 2), lambda s, _: (s, 0))
    block = pl.BlockSpec((CORES * toks, width), lambda s, _: (s, 0))
    return call(
        functools.partial(column_kernel, reps, cap, temper), "column",
        gathered.shape[0] // (CORES * toks),
        [full(codes.shape), full(hard_scores.shape), full(log_total.shape)] + [slots] * 8
        + [block, full((toks, width))],
        block, jax.ShapeDtypeStruct(gathered.shape, BF16),
        [pltpu.VMEM(hard_scores.shape, F32)], LIGHT,
    )(place, codes, hard_scores, log_total, *first, *second, gathered, queries)


def inner_kernel(temper, place_ref, lt_ref, p_ref, q_ref, gq_ref, loss_ref):
    step = pl.program_id(0)
    toks, width = q_ref.shape
    lt_own = own_row(lt_ref, rep_of(place_ref[1], place_ref[2]))
    passages = p_ref[...]
    scores = temper * mm(passages, q_ref[...], NT)
    row = iota(scores.shape, 0) + passages.shape[0] * step - toks * place_ref[0]
    eye = row == iota(scores.shape, 1)
    d_scores = (jnp.exp(scores - lt_own) - jnp.where(eye, 1.0, 0.0)).astype(BF16)
    new = mm(d_scores, passages, TN)
    own = jnp.sum(jnp.where(eye, scores, 0.0), axis=0, keepdims=True)

    @pl.when(step == 0)
    def _():
        gq_ref[...] = new
        loss_ref[...] = lt_own - own

    @pl.when(step > 0)
    def _():
        gq_ref[...] += new
        loss_ref[...] -= own


def inner(place, log_total, gathered, queries, temper):
    toks, width = queries.shape
    return call(
        functools.partial(inner_kernel, temper), "inner", 2,
        [full(log_total.shape), pl.BlockSpec((gathered.shape[0] // 2, width), lambda s, _: (s, 0)),
         full((toks, width))],
        [full((toks, width)), full((1, toks))],
        [jax.ShapeDtypeStruct((toks, width), F32), jax.ShapeDtypeStruct((1, toks), F32)],
        [], LIGHT,
    )(place, log_total, gathered, queries)


def reduce_kernel(half, cap, groups, place_ref, lt_ref, *refs):
    ranks, rows, outs = refs[0:4], refs[4:8], refs[8:12]
    toks = lt_ref.shape[1]
    slots = groups * cap
    reps = lt_ref.shape[0]
    shape = (SIDE * slots, 4 * groups)
    group = iota(shape, 0) // cap % groups
    parts = (iota(shape, 1) % groups == group) & (iota(shape, 1) < 3 * groups)
    parts = parts.astype(BF16)
    log_rows = jnp.concatenate(
        [jnp.broadcast_to(own_row(lt_ref, source_of(place_ref, half, s)), (slots, toks))
         for s in range(SIDE)], axis=0
    )
    weights = []
    for line in range(SIDE):
        scores = mm(parts, rows[line][slots * SIDE :, : reps * cap])
        slot, lane = iota(scores.shape, 0), iota(scores.shape, 1)
        s = slot // slots
        block = s * SIDE + line if half == 0 else line * SIDE + s
        hs = jnp.sum(
            jnp.where(lane == block * cap + slot % cap, scores, 0.0), axis=1, keepdims=True
        )
        _, hit = hits_of(ranks[line][...], groups, cap)
        weights.append(jnp.where(hit, jnp.exp(hs - log_rows), 0.0).astype(BF16))
    for s in range(SIDE):
        values = [
            rows[line][(g * SIDE + s) * cap : (g * SIDE + s + 1) * cap, :]
            for line in range(SIDE) for g in range(groups)
        ]
        weight = jnp.concatenate([w[s * slots : (s + 1) * slots] for w in weights], axis=0)
        outs[s][...] = mm(weight, jnp.concatenate(values, axis=0), TN).astype(outs[s].dtype)


def reduce(place, half, log_total, ranks, rows, groups, cap):
    toks = log_total.shape[1]
    shape = (toks, rows[0].shape[1])
    return call(
        functools.partial(reduce_kernel, half, cap, groups), "reduce", 1,
        [full(log_total.shape)] + [full(ranks[0].shape)] * 4 + [full(rows[0].shape)] * 4,
        [full(shape)] * 4,
        [jax.ShapeDtypeStruct(shape, F32)] + [jax.ShapeDtypeStruct(shape, BF16)] * 3, [], LIGHT,
    )(place, log_total, *ranks, *rows)


def final_kernel(temper, place_ref, gq_ref, *refs):
    out_ref = refs[8]
    half_width = out_ref.shape[1] // 2
    for half in range(2):
        lanes = slice(half * half_width, (half + 1) * half_width)
        total = gq_ref[:, lanes]
        for ref in refs[4 * half : 4 * half + 4]:
            total = total + ref[...].astype(F32)
        out_ref[:, lanes] = (temper * total).astype(BF16)


def final(place, within, first, second, temper):
    rows, width = within.shape
    wide = pl.BlockSpec((rows // 4, width), lambda s, _: (s, 0))
    narrow = pl.BlockSpec((rows // 4, width // 2), lambda s, _: (s, 0))
    return call(
        functools.partial(final_kernel, temper), "final", 4, [wide] + [narrow] * 8, wide,
        jax.ShapeDtypeStruct((rows, width), BF16), [], HEAVY,
    )(place, within, *first, *second)


def along(x, half, shift):
    pairs = []
    for i in range(SIDE * SIDE):
        a, b = i // SIDE, i % SIDE
        pairs.append((i, rep_of(a + shift, b) if half == 0 else rep_of(a, b + shift)))
    return lax.ppermute(x, "rep", pairs)


def shards(queries, passages, neg_device, neg_row):
    toks, width = queries.shape
    negs = neg_device.shape[1]
    groups = lax.axis_size("grp")
    reps = lax.axis_size("rep")
    cap = 8 * toks // (groups * reps)
    half_width = width // 2
    temper = 3.0 / math.sqrt(width)
    grp, rep = lax.axis_index("grp"), lax.axis_index("rep")
    place = jnp.stack([grp, rep // SIDE, rep % SIDE]).astype(I32)

    lines = jnp.pad(jnp.stack([neg_device.T, neg_row.T]), ((0, 0), (0, 8 - negs), (0, 0)))
    lines = jnp.pad(lines.reshape(16, toks), ((0, 0), (0, half_width - toks))).astype(BF16)
    sources = []
    for half in range(2):
        block = queries[:, half * half_width : (half + 1) * half_width]
        block = jnp.concatenate([block, lines], axis=0)
        sources.append([block] + [along(block, half, s) for s in range(1, SIDE)])
    gathered = lax.all_gather(passages, "grp", axis=0, tiled=True)

    first, second, ranks_first, ranks_second = [], [], [], []
    for shift in range(SIDE):
        one, two, rank_one, rank_two = mid(place, shift, *sources, groups, reps, cap, negs)
        first.append(along(one, 1, shift) if shift else one)
        second.append(along(two, 0, shift) if shift else two)
        ranks_first.append(rank_one)
        ranks_second.append(rank_two)

    within = inside(place, gathered, queries, temper)
    back_first, back_second, hard_scores, codes, part = hard(
        place, first, second, gathered, within, temper, reps, cap
    )
    parts = lax.all_to_all(part, "rep", split_axis=0, concat_axis=0, tiled=True)
    parts, back_first, back_second = lax.optimization_barrier((parts, back_first, back_second))
    high = jnp.max(parts, axis=0)
    log_total = high + jnp.log(jnp.sum(jnp.exp(parts - high), axis=0))

    back_first = [along(v, 1, -s) if s else v for s, v in enumerate(back_first)]
    back_second = [along(v, 0, -s) if s else v for s, v in enumerate(back_second)]

    partial_sum = column(
        place, codes, hard_scores, log_total, first, second, gathered, queries, temper, cap
    )
    grad_passages = lax.psum_scatter(partial_sum, "grp", scatter_dimension=0, tiled=True)
    grad_inner, losses = inner(place, log_total, gathered, queries, temper)

    sums = []
    for half, ranks, rows in ((0, ranks_first, back_first), (1, ranks_second, back_second)):
        made = reduce(place, half, log_total, ranks, rows, groups, cap)
        sums.append([along(v, half, -s) if s else v for s, v in enumerate(made)])
    grad_queries = final(place, grad_inner, *sums, temper)
    return (losses.reshape(toks), grad_queries, grad_passages)


def solution(mesh):
    in_specs = (
        P(("grp", "rep"), None),
        P(("grp", "rep"), None),
        P(("grp", "rep"), None),
        P(("grp", "rep"), None),
    )
    out_specs = (P(("grp", "rep")), P(("grp", "rep"), None), P(("grp", "rep"), None))
    return jax.shard_map(shards, mesh=mesh, in_specs=in_specs, out_specs=out_specs, check_vma=False)
```

```python
import functools
import math

import jax
import jax.numpy as jnp
from jax import lax
from jax.experimental import pallas as pl
from jax.experimental.pallas import tpu as pltpu
from jax.sharding import PartitionSpec as P

F32 = jnp.float32
BF16 = jnp.bfloat16
I32 = jnp.int32
LOW = -1e30
NT = (((1,), (1,)), ((), ()))
TN = (((0,), (0,)), ((), ()))
NN = (((1,), (0,)), ((), ()))
VMEM_LIMIT = 60 * 1024 * 1024


def mm(a, b, dims=NN):
    return lax.dot_general(a, b, dims, preferred_element_type=F32)


def iota(shape, dim):
    return lax.broadcasted_iota(I32, shape, dim)


def split3(x):
    a = x.astype(BF16)
    rest = x - a.astype(F32)
    b = rest.astype(BF16)
    c = (rest - b.astype(F32)).astype(BF16)
    return jnp.concatenate([a, b, c], axis=0)


def full(shape):
    return pl.BlockSpec(shape, lambda *_: (0,) * len(shape))


def call(kernel, name, steps, ins, outs, shapes, scratch, weight):
    return pl.pallas_call(
        kernel,
        grid_spec=pltpu.PrefetchScalarGridSpec(
            num_scalar_prefetch=1, grid=(steps,), in_specs=ins, out_specs=outs,
            scratch_shapes=scratch,
        ),
        out_shape=shapes,
        compiler_params=pltpu.CompilerParams(
            dimension_semantics=("arbitrary",), vmem_limit_bytes=VMEM_LIMIT
        ),
        cost_estimate=pl.CostEstimate(flops=weight, bytes_accessed=1 << 16, transcendentals=0),
        name=name,
    )


LIGHT, MIDDLE, HEAVY = 1 << 20, 1 << 20, 1 << 39
SIDE = 4
CORES = 2


def rep_of(x, y):
    return x % SIDE * SIDE + y % SIDE


def columns_of(place_ref, half, shift):
    x, y = place_ref[1], place_ref[2]
    return rep_of(x, y + shift) if half == 0 else rep_of(x + shift, y)


def source_of(place_ref, half, shift):
    x, y = place_ref[1], place_ref[2]
    return rep_of(x + SIDE - shift, y) if half == 0 else rep_of(x, y + SIDE - shift)


def hits_of(ranks, groups, cap):
    shape = (ranks.shape[0] * cap, ranks.shape[0])
    pick = (iota(shape, 1) == iota(shape, 0) // cap).astype(BF16)
    spread = mm(pick, ranks)
    return pick, spread == (iota(spread.shape, 0) % cap + 1).astype(F32)


def mid_kernel(shift, cap, groups, reps, negs, place_ref, *refs):
    sources = (refs[0:SIDE], refs[SIDE : 2 * SIDE])
    outs, ranks_out = refs[2 * SIDE : 2 * SIDE + 2], refs[2 * SIDE + 2 :]
    rows, half_width = sources[0][0].shape
    toks = rows - 16
    slots = groups * cap
    before = (iota((toks, toks), 0) < iota((toks, toks), 1)).astype(BF16)
    for half in range(2):
        col = columns_of(place_ref, half, shift)
        dev = (iota((groups, toks), 0) * reps + col).astype(F32)
        named_all, rows_all = [], []
        for source in sources[half]:
            table = source[toks:, :toks].astype(F32)
            named = jnp.zeros((groups, toks), F32)
            wanted = jnp.zeros((groups, toks), F32)
            for k in range(negs):
                hit = dev == table[k : k + 1]
                named = named + jnp.where(hit, 1.0, 0.0)
                wanted = wanted + jnp.where(hit, table[8 + k : 9 + k] + 1.0, 0.0)
            named_all.append(named)
            rows_all.append(wanted)
        named = jnp.concatenate(named_all, axis=0)
        wanted = jnp.concatenate(rows_all, axis=0).astype(BF16)
        ranks = (named * (mm(named.astype(BF16), before) + 1.0)).astype(BF16)
        ranks_out[half][...] = ranks
        pick, hit = hits_of(ranks, groups, cap)
        hot = hit.astype(BF16)
        row = jnp.where(hit, mm(pick, wanted), 0.0).astype(BF16)
        ids = mm(jnp.ones((8, toks), BF16), row, NT)[0:1]
        tok = mm(iota((8, toks), 1).astype(F32).astype(BF16), hot, NT)[0:1]
        for s, source in enumerate(sources[half]):
            moved = mm(hot[s * slots : (s + 1) * slots], source[:toks, :]).astype(BF16)
            for g in range(groups):
                first = (g * SIDE + s) * cap
                outs[half][first : first + cap, :] = moved[g * cap : (g + 1) * cap]
        codes = [v[:, s * slots : (s + 1) * slots] for v in (ids, tok) for s in range(SIDE)]
        codes = jnp.concatenate(codes + [jnp.zeros((8, slots), F32)], axis=0)
        codes = jnp.concatenate([codes, jnp.zeros((16, half_width - slots), F32)], axis=1)
        outs[half][groups * SIDE * cap :, :] = codes.astype(BF16)


def mid(place, shift, first, second, groups, reps, cap, negs):
    rows, half_width = first[0].shape
    slots = jax.ShapeDtypeStruct((groups * SIDE * cap + 16, half_width), BF16)
    ranks = jax.ShapeDtypeStruct((SIDE * groups, rows - 16), BF16)
    return call(
        functools.partial(mid_kernel, shift, cap, groups, reps, negs), "mid", 1,
        [full((rows, half_width))] * (2 * SIDE),
        [full(slots.shape)] * 2 + [full(ranks.shape)] * 2,
        [slots, slots, ranks, ranks], [], LIGHT,
    )(place, *first, *second)


def inside_kernel(temper, place_ref, p_ref, q_ref, out_ref, top, total):
    step = pl.program_id(0)

    @pl.when(step == 0)
    def _():
        top[...] = jnp.full(top.shape, LOW, F32)
        total[...] = jnp.zeros(total.shape, F32)

    scores = temper * mm(p_ref[...], q_ref[...], NT)
    high = jnp.maximum(top[...], jnp.max(scores, axis=0, keepdims=True))
    total[...] = total[...] * jnp.exp(top[...] - high) + jnp.sum(
        jnp.exp(scores - high), axis=0, keepdims=True
    )
    top[...] = high

    @pl.when(step == pl.num_programs(0) - 1)
    def _():
        out_ref[...] = top[...] + jnp.log(total[...])


def inside(place, gathered, queries, temper):
    toks, width = queries.shape
    return call(
        functools.partial(inside_kernel, temper), "inside", 2,
        [pl.BlockSpec((gathered.shape[0] // 2, width), lambda s, _: (s, 0)), full((toks, width))],
        full((1, toks)), jax.ShapeDtypeStruct((1, toks), F32),
        [pltpu.VMEM((1, toks), F32), pltpu.VMEM((1, toks), F32)], MIDDLE,
    )(place, gathered, queries)


def asking_rows(first, second, base, cap):
    def piece(ref, s):
        return ref[base + s * cap : base + (s + 1) * cap, :]

    pairs = [(dx, dy) for dx in range(SIDE) for dy in range(SIDE)]
    one = jnp.concatenate([piece(first[dy], dx) for dx, dy in pairs], axis=0)
    two = jnp.concatenate([piece(second[dx], dy) for dx, dy in pairs], axis=0)
    return one, two


def source_mask(place_ref, reps, cap):
    shape = (reps, reps * cap)
    dx = iota(shape, 1) // (SIDE * cap)
    dy = iota(shape, 1) // cap % SIDE
    x = (place_ref[1] + SIDE - dx) % SIDE
    y = (place_ref[2] + SIDE - dy) % SIDE
    return iota(shape, 0) == x * SIDE + y


def hard_kernel(reps, cap, temper, place_ref, *refs):
    first, second, exts = refs[0:4], refs[4:8], refs[8:12]
    p_ref, inside_ref = refs[12:14]
    out_first, out_second = refs[14:18], refs[18:22]
    hs_ref, code_ref, part_ref, top, total = refs[22:]
    step = pl.program_id(0)
    levels = pl.num_programs(0) - 1
    toks = inside_ref.shape[1]
    half_width = p_ref.shape[1] // 2
    slots = reps * cap
    groups = code_ref.shape[0] // 2
    source = source_mask(place_ref, reps, cap)

    @pl.when(step == 0)
    def _():
        top[...] = jnp.full(top.shape, LOW, F32)
        total[...] = jnp.zeros(total.shape, F32)
        table = jnp.concatenate([ext[...] for ext in exts], axis=0)[:, : groups * cap]
        shape = (groups * cap, groups * slots)
        lane, slot = iota(shape, 0), iota(shape, 1)
        to_slot = (lane == slot // slots * cap + slot % cap).astype(BF16)
        laid = mm(table, to_slot)
        row, slot = iota(laid.shape, 0), iota(laid.shape, 1) % slots
        dx, dy = slot // (SIDE * cap), slot // cap % SIDE
        want = dy * 16 + dx
        ids = jnp.sum(jnp.where(row == want, laid, 0.0), axis=0, keepdims=True).astype(I32)
        tok = jnp.sum(jnp.where(row == want + SIDE, laid, 0.0), axis=0, keepdims=True).astype(I32)
        for g in range(groups):
            code_ref[g : g + 1, :] = ids[:, g * slots : (g + 1) * slots]
            code_ref[groups + g : groups + g + 1, :] = tok[:, g * slots : (g + 1) * slots]

    @pl.when(step < levels)
    def _():
        values = []
        for core in range(CORES):
            group = CORES * step + core
            ids = code_ref[pl.ds(group, 1), :]
            tok = code_ref[pl.ds(groups + group, 1), :]
            valid = ids > 0
            base = core * SIDE * cap
            one, two = asking_rows(first, second, base, cap)
            passages = p_ref[core * toks : (core + 1) * toks, :]
            cross = mm(passages, jnp.concatenate([one, two], axis=1), NT)
            hit = iota((toks, slots), 0) + 1 == ids
            hs = temper * jnp.sum(jnp.where(hit, cross, 0.0), axis=0, keepdims=True)
            hs_ref[pl.ds(group, 1), :] = hs
            served = mm(hit.astype(BF16), passages, TN).astype(BF16)
            for dx in range(SIDE):
                for dy in range(SIDE):
                    at = (dx * SIDE + dy) * cap
                    out_first[dy][base + dx * cap : base + (dx + 1) * cap, :] = served[
                        at : at + cap, :half_width
                    ]
                    out_second[dx][base + dy * cap : base + (dy + 1) * cap, :] = served[
                        at : at + cap, half_width:
                    ]
            token = ((iota((toks, slots), 0) == tok) & valid).astype(BF16)
            live = source & valid
            parts = jnp.concatenate(
                [split3(jnp.where(live, hs, 0.0)), live.astype(BF16)], axis=0
            )
            laid = mm(parts, token, NT)
            there = laid[3 * reps :] > 0.5
            value = laid[:reps] + laid[reps : 2 * reps] + laid[2 * reps : 3 * reps]
            values.append((there, jnp.where(there, value, LOW)))
        high = top[...]
        for there, value in values:
            high = jnp.maximum(high, value)
        new = total[...] * jnp.exp(top[...] - high)
        for there, value in values:
            new = new + jnp.where(there, jnp.exp(value - high), 0.0)
        total[...] = new
        top[...] = high

    @pl.when(step == levels)
    def _():
        part = jnp.where(total[...] > 0.0, top[...] + jnp.log(total[...]), LOW)
        within = inside_ref[...]
        high = jnp.maximum(part, within)
        both = high + jnp.log(jnp.exp(part - high) + jnp.exp(within - high))
        own = iota(part.shape, 0) == rep_of(place_ref[1], place_ref[2])
        part_ref[...] = jnp.broadcast_to(jnp.where(own, both, part)[None], part_ref.shape)
        pieces = split3(hs_ref[...]).astype(F32)
        pieces = jnp.concatenate([pieces, jnp.zeros((groups, slots), F32)], axis=0)
        pieces = jnp.concatenate(
            [pieces, jnp.zeros((4 * groups, half_width - slots), F32)], axis=1
        ).astype(BF16)
        for out in (*out_first, *out_second):
            out[: 4 * groups, :] = pieces


def hard(place, first, second, gathered, within, temper, reps, cap):
    rows, half_width = first[0].shape
    toks = within.shape[1]
    groups = gathered.shape[0] // toks
    levels = groups // CORES
    slots = reps * cap
    per = CORES * SIDE * cap
    ins = pl.BlockSpec((per, half_width), lambda s, _: (lax.min(s, levels - 1), 0))
    outs = pl.BlockSpec((per, half_width), lambda s, _: (s, 0))
    ext = pl.BlockSpec((16, half_width), lambda s, _: (groups * SIDE * cap // 16, 0))
    made = call(
        functools.partial(hard_kernel, reps, cap, temper), "hard", levels + 1,
        [ins] * 8 + [ext] * 4
        + [pl.BlockSpec((CORES * toks, CORES * half_width),
                        lambda s, _: (lax.min(s, levels - 1), 0)), full((1, toks))],
        [outs] * 8 + [full((groups, slots)), full((2 * groups, slots)), full((reps, reps, toks))],
        [jax.ShapeDtypeStruct((groups * SIDE * cap + 4 * groups, half_width), BF16)] * 8
        + [jax.ShapeDtypeStruct((groups, slots), F32),
           jax.ShapeDtypeStruct((2 * groups, slots), I32),
           jax.ShapeDtypeStruct((reps, reps, toks), F32)],
        [pltpu.VMEM((reps, toks), F32), pltpu.VMEM((reps, toks), F32)], LIGHT,
    )(place, *first, *second, *first, gathered, within)
    return made[0:4], made[4:8], made[8], made[9], made[10]


def own_row(lt_ref, rep):
    lt = lt_ref[...]
    return jnp.sum(jnp.where(iota(lt.shape, 0) == rep, lt, 0.0), axis=0, keepdims=True)


def column_kernel(reps, cap, temper, place_ref, code_ref, hs_ref, lt_ref, *refs):
    first, second = refs[0:4], refs[4:8]
    p_ref, q_ref, gp_ref, mark_ref, d_ref = refs[8:]
    step = pl.program_id(0)
    toks, width = q_ref.shape
    half_width = width // 2
    slots = reps * cap
    groups = code_ref.shape[0] // 2

    @pl.when(step == 0)
    def _():
        log_parts = split3(lt_ref[...])
        source = source_mask(place_ref, reps, cap)
        rows = []
        for g in range(groups):
            valid = code_ref[g : g + 1, :] > 0
            tok = code_ref[groups + g : groups + g + 1, :]
            token = ((iota((toks, slots), 0) == tok) & valid).astype(BF16)
            found = mm(log_parts, token)
            found = found[:reps] + found[reps : 2 * reps] + found[2 * reps :]
            log_slot = jnp.sum(jnp.where(source, found, 0.0), axis=0, keepdims=True)
            rows.append(jnp.where(valid, jnp.exp(hs_ref[g : g + 1, :] - log_slot), 0.0))
        d_ref[...] = jnp.concatenate(rows, axis=0)
        mark_ref[...] = jnp.zeros(mark_ref.shape, F32)

    queries = q_ref[...]
    lt_own = own_row(lt_ref, rep_of(place_ref[1], place_ref[2]))
    for core in range(CORES):
        group = CORES * step + core
        here = pl.ds(core * toks, toks)
        ids = code_ref[pl.ds(group, 1), :]
        d_hard = d_ref[pl.ds(group, 1), :]
        hot = jnp.where(iota((toks, slots), 0) + 1 == ids, d_hard, 0.0).astype(BF16)
        scores = temper * mm(p_ref[here, :], queries, NT)
        eye = (iota((toks, toks), 0) == iota((toks, toks), 1)) & (group == place_ref[0])
        d_scores = (jnp.exp(scores - lt_own) - jnp.where(eye, 1.0, 0.0)).astype(BF16)
        both = jnp.concatenate([hot, d_scores], axis=1)
        one, two = asking_rows(first, second, core * SIDE * cap, cap)
        rows = jnp.concatenate([jnp.concatenate([one, two], axis=1), queries], axis=0)
        gp_ref[here, :] = (temper * mm(both, rows)).astype(BF16)


def column(place, codes, hard_scores, log_total, first, second, gathered, queries, temper, cap):
    reps = log_total.shape[0]
    toks, width = queries.shape
    slots = pl.BlockSpec((CORES * SIDE * cap, width // 2), lambda s, _: (s, 0))
    block = pl.BlockSpec((CORES * toks, width), lambda s, _: (s, 0))
    return call(
        functools.partial(column_kernel, reps, cap, temper), "column",
        gathered.shape[0] // (CORES * toks),
        [full(codes.shape), full(hard_scores.shape), full(log_total.shape)] + [slots] * 8
        + [block, full((toks, width))],
        [block, full((8, 128))],
        [jax.ShapeDtypeStruct(gathered.shape, BF16), jax.ShapeDtypeStruct((8, 128), F32)],
        [pltpu.VMEM(hard_scores.shape, F32)], LIGHT,
    )(place, codes, hard_scores, log_total, *first, *second, gathered, queries)


def inner_kernel(temper, place_ref, lt_ref, p_ref, q_ref, gq_ref, loss_ref):
    step = pl.program_id(0)
    toks, width = q_ref.shape
    lt_own = own_row(lt_ref, rep_of(place_ref[1], place_ref[2]))
    passages = p_ref[...]
    scores = temper * mm(passages, q_ref[...], NT)
    row = iota(scores.shape, 0) + passages.shape[0] * step - toks * place_ref[0]
    eye = row == iota(scores.shape, 1)
    d_scores = (jnp.exp(scores - lt_own) - jnp.where(eye, 1.0, 0.0)).astype(BF16)
    new = mm(d_scores, passages, TN)
    own = jnp.sum(jnp.where(eye, scores, 0.0), axis=0, keepdims=True)

    @pl.when(step == 0)
    def _():
        gq_ref[...] = new
        loss_ref[...] = lt_own - own

    @pl.when(step > 0)
    def _():
        gq_ref[...] += new
        loss_ref[...] -= own


def inner(place, log_total, gathered, queries, temper):
    toks, width = queries.shape
    return call(
        functools.partial(inner_kernel, temper), "inner", 2,
        [full(log_total.shape), pl.BlockSpec((gathered.shape[0] // 2, width), lambda s, _: (s, 0)),
         full((toks, width))],
        [full((toks, width)), full((1, toks))],
        [jax.ShapeDtypeStruct((toks, width), F32), jax.ShapeDtypeStruct((1, toks), F32)],
        [], LIGHT,
    )(place, log_total, gathered, queries)


def reduce_kernel(half, cap, groups, place_ref, lt_ref, *refs):
    ranks, rows, outs = refs[0:4], refs[4:8], refs[9:13]
    toks = lt_ref.shape[1]
    slots = groups * cap
    reps = lt_ref.shape[0]
    shape = (SIDE * slots, 4 * groups)
    group = iota(shape, 0) // cap % groups
    parts = (iota(shape, 1) % groups == group) & (iota(shape, 1) < 3 * groups)
    parts = parts.astype(BF16)
    log_rows = jnp.concatenate(
        [jnp.broadcast_to(own_row(lt_ref, source_of(place_ref, half, s)), (slots, toks))
         for s in range(SIDE)], axis=0
    )
    weights = []
    for line in range(SIDE):
        scores = mm(parts, rows[line][slots * SIDE :, : reps * cap])
        slot, lane = iota(scores.shape, 0), iota(scores.shape, 1)
        s = slot // slots
        block = s * SIDE + line if half == 0 else line * SIDE + s
        hs = jnp.sum(
            jnp.where(lane == block * cap + slot % cap, scores, 0.0), axis=1, keepdims=True
        )
        _, hit = hits_of(ranks[line][...], groups, cap)
        weights.append(jnp.where(hit, jnp.exp(hs - log_rows), 0.0).astype(BF16))
    for s in range(SIDE):
        values = [
            rows[line][(g * SIDE + s) * cap : (g * SIDE + s + 1) * cap, :]
            for line in range(SIDE) for g in range(groups)
        ]
        weight = jnp.concatenate([w[s * slots : (s + 1) * slots] for w in weights], axis=0)
        outs[s][...] = mm(weight, jnp.concatenate(values, axis=0), TN).astype(outs[s].dtype)


def reduce(place, half, log_total, ranks, rows, mark, groups, cap):
    toks = log_total.shape[1]
    shape = (toks, rows[0].shape[1])
    return call(
        functools.partial(reduce_kernel, half, cap, groups), "reduce", 1,
        [full(log_total.shape)] + [full(ranks[0].shape)] * 4 + [full(rows[0].shape)] * 4
        + [full(mark.shape)],
        [full(shape)] * 4,
        [jax.ShapeDtypeStruct(shape, F32)] + [jax.ShapeDtypeStruct(shape, BF16)] * 3, [], HEAVY,
    )(place, log_total, *ranks, *rows, mark)


def final_kernel(temper, place_ref, gq_ref, *refs):
    out_ref = refs[8]
    half_width = out_ref.shape[1] // 2
    for half in range(2):
        lanes = slice(half * half_width, (half + 1) * half_width)
        total = gq_ref[:, lanes]
        for ref in refs[4 * half : 4 * half + 4]:
            total = total + ref[...].astype(F32)
        out_ref[:, lanes] = (temper * total).astype(BF16)


def final(place, within, first, second, temper):
    rows, width = within.shape
    wide = pl.BlockSpec((rows // 4, width), lambda s, _: (s, 0))
    narrow = pl.BlockSpec((rows // 4, width // 2), lambda s, _: (s, 0))
    return call(
        functools.partial(final_kernel, temper), "final", 4, [wide] + [narrow] * 8, wide,
        jax.ShapeDtypeStruct((rows, width), BF16), [], LIGHT,
    )(place, within, *first, *second)


def along(x, half, shift):
    pairs = []
    for i in range(SIDE * SIDE):
        a, b = i // SIDE, i % SIDE
        pairs.append((i, rep_of(a + shift, b) if half == 0 else rep_of(a, b + shift)))
    return lax.ppermute(x, "rep", pairs)


def shards(queries, passages, neg_device, neg_row):
    toks, width = queries.shape
    negs = neg_device.shape[1]
    groups = lax.axis_size("grp")
    reps = lax.axis_size("rep")
    cap = 8 * toks // (groups * reps)
    half_width = width // 2
    temper = 3.0 / math.sqrt(width)
    grp, rep = lax.axis_index("grp"), lax.axis_index("rep")
    place = jnp.stack([grp, rep // SIDE, rep % SIDE]).astype(I32)

    lines = jnp.pad(jnp.stack([neg_device.T, neg_row.T]), ((0, 0), (0, 8 - negs), (0, 0)))
    lines = jnp.pad(lines.reshape(16, toks), ((0, 0), (0, half_width - toks))).astype(BF16)
    sources = []
    for half in range(2):
        block = queries[:, half * half_width : (half + 1) * half_width]
        block = jnp.concatenate([block, lines], axis=0)
        sources.append([block] + [along(block, half, s) for s in range(1, SIDE)])
    gathered = lax.all_gather(passages, "grp", axis=0, tiled=True)

    first, second, ranks_first, ranks_second = [], [], [], []
    for shift in range(SIDE):
        one, two, rank_one, rank_two = mid(place, shift, *sources, groups, reps, cap, negs)
        first.append(along(one, 1, shift) if shift else one)
        second.append(along(two, 0, shift) if shift else two)
        ranks_first.append(rank_one)
        ranks_second.append(rank_two)

    within = inside(place, gathered, queries, temper)
    back_first, back_second, hard_scores, codes, part = hard(
        place, first, second, gathered, within, temper, reps, cap
    )
    parts = lax.all_to_all(part, "rep", split_axis=0, concat_axis=0, tiled=True)
    high = jnp.max(parts, axis=0)
    log_total = high + jnp.log(jnp.sum(jnp.exp(parts - high), axis=0))

    partial_sum, mark = column(
        place, codes, hard_scores, log_total, first, second, gathered, queries, temper, cap
    )
    grad_passages = lax.psum_scatter(partial_sum, "grp", scatter_dimension=0, tiled=True)
    back_first = [along(v, 1, -s) if s else v for s, v in enumerate(back_first)]
    back_second = [along(v, 0, -s) if s else v for s, v in enumerate(back_second)]
    grad_inner, losses = inner(place, log_total, gathered, queries, temper)

    sums = []
    for half, ranks, rows in ((0, ranks_first, back_first), (1, ranks_second, back_second)):
        made = reduce(place, half, log_total, ranks, rows, mark, groups, cap)
        sums.append([along(v, half, -s) if s else v for s, v in enumerate(made)])
    grad_queries = final(place, grad_inner, *sums, temper)
    return (losses.reshape(toks), grad_queries, grad_passages)


def solution(mesh):
    in_specs = (
        P(("grp", "rep"), None),
        P(("grp", "rep"), None),
        P(("grp", "rep"), None),
        P(("grp", "rep"), None),
    )
    out_specs = (P(("grp", "rep")), P(("grp", "rep"), None), P(("grp", "rep"), None))
    return jax.shard_map(shards, mesh=mesh, in_specs=in_specs, out_specs=out_specs, check_vma=False)
```

```python
import functools
import math

import jax
import jax.numpy as jnp
from jax import lax
from jax.experimental import pallas as pl
from jax.experimental.pallas import tpu as pltpu
from jax.sharding import PartitionSpec as P

F32 = jnp.float32
BF16 = jnp.bfloat16
I32 = jnp.int32
LOW = -1e30
NT = (((1,), (1,)), ((), ()))
TN = (((0,), (0,)), ((), ()))
NN = (((1,), (0,)), ((), ()))
VMEM_LIMIT = 60 * 1024 * 1024


def mm(a, b, dims=NN):
    return lax.dot_general(a, b, dims, preferred_element_type=F32)


def iota(shape, dim):
    return lax.broadcasted_iota(I32, shape, dim)


def split3(x):
    a = x.astype(BF16)
    rest = x - a.astype(F32)
    b = rest.astype(BF16)
    c = (rest - b.astype(F32)).astype(BF16)
    return jnp.concatenate([a, b, c], axis=0)


def full(shape):
    return pl.BlockSpec(shape, lambda *_: (0,) * len(shape))


def call(kernel, name, steps, ins, outs, shapes, scratch, weight):
    return pl.pallas_call(
        kernel,
        grid_spec=pltpu.PrefetchScalarGridSpec(
            num_scalar_prefetch=1, grid=(steps,), in_specs=ins, out_specs=outs,
            scratch_shapes=scratch,
        ),
        out_shape=shapes,
        compiler_params=pltpu.CompilerParams(
            dimension_semantics=("arbitrary",), vmem_limit_bytes=VMEM_LIMIT
        ),
        cost_estimate=pl.CostEstimate(flops=weight, bytes_accessed=1 << 16, transcendentals=0),
        name=name,
    )


LIGHT, MIDDLE, HEAVY = 1 << 20, 1 << 20, 1 << 39
SIDE = 4
CORES = 2


def rep_of(x, y):
    return x % SIDE * SIDE + y % SIDE


def columns_of(place_ref, half, shift):
    x, y = place_ref[1], place_ref[2]
    return rep_of(x, y + shift) if half == 0 else rep_of(x + shift, y)


def source_of(place_ref, half, shift):
    x, y = place_ref[1], place_ref[2]
    return rep_of(x + SIDE - shift, y) if half == 0 else rep_of(x, y + SIDE - shift)


def hits_of(ranks, groups, cap):
    shape = (ranks.shape[0] * cap, ranks.shape[0])
    pick = (iota(shape, 1) == iota(shape, 0) // cap).astype(BF16)
    spread = mm(pick, ranks)
    return pick, spread == (iota(spread.shape, 0) % cap + 1).astype(F32)


def mid_kernel(shift, cap, groups, reps, negs, place_ref, *refs):
    sources = (refs[0:SIDE], refs[SIDE : 2 * SIDE])
    outs, ranks_out = refs[-4:-2], refs[-2:]
    rows, half_width = sources[0][0].shape
    toks = rows - 16
    slots = groups * cap
    before = (iota((toks, toks), 0) < iota((toks, toks), 1)).astype(BF16)
    for half in range(2):
        col = columns_of(place_ref, half, shift)
        dev = (iota((groups, toks), 0) * reps + col).astype(F32)
        named_all, rows_all = [], []
        for source in sources[half]:
            table = source[toks:, :toks].astype(F32)
            named = jnp.zeros((groups, toks), F32)
            wanted = jnp.zeros((groups, toks), F32)
            for k in range(negs):
                hit = dev == table[k : k + 1]
                named = named + jnp.where(hit, 1.0, 0.0)
                wanted = wanted + jnp.where(hit, table[8 + k : 9 + k] + 1.0, 0.0)
            named_all.append(named)
            rows_all.append(wanted)
        named = jnp.concatenate(named_all, axis=0)
        wanted = jnp.concatenate(rows_all, axis=0).astype(BF16)
        ranks = (named * (mm(named.astype(BF16), before) + 1.0)).astype(BF16)
        ranks_out[half][...] = ranks
        pick, hit = hits_of(ranks, groups, cap)
        hot = hit.astype(BF16)
        row = jnp.where(hit, mm(pick, wanted), 0.0).astype(BF16)
        ids = mm(jnp.ones((8, toks), BF16), row, NT)[0:1]
        tok = mm(iota((8, toks), 1).astype(F32).astype(BF16), hot, NT)[0:1]
        for s, source in enumerate(sources[half]):
            moved = mm(hot[s * slots : (s + 1) * slots], source[:toks, :]).astype(BF16)
            for g in range(groups):
                first = (g * SIDE + s) * cap
                outs[half][first : first + cap, :] = moved[g * cap : (g + 1) * cap]
        codes = [v[:, s * slots : (s + 1) * slots] for v in (ids, tok) for s in range(SIDE)]
        codes = jnp.concatenate(codes + [jnp.zeros((8, slots), F32)], axis=0)
        codes = jnp.concatenate([codes, jnp.zeros((16, half_width - slots), F32)], axis=1)
        outs[half][groups * SIDE * cap :, :] = codes.astype(BF16)


def mid(place, shift, first, second, earlier, groups, reps, cap, negs):
    rows, half_width = first[0].shape
    slots = jax.ShapeDtypeStruct((groups * SIDE * cap + 16, half_width), BF16)
    ranks = jax.ShapeDtypeStruct((SIDE * groups, rows - 16), BF16)
    return call(
        functools.partial(mid_kernel, shift, cap, groups, reps, negs), "mid", 1,
        [full((rows, half_width))] * (2 * SIDE) + [full(v.shape) for v in earlier],
        [full(slots.shape)] * 2 + [full(ranks.shape)] * 2,
        [slots, slots, ranks, ranks], [], LIGHT,
    )(place, *first, *second, *earlier)


def inside_kernel(temper, place_ref, p_ref, q_ref, out_ref, top, total):
    step = pl.program_id(0)

    @pl.when(step == 0)
    def _():
        top[...] = jnp.full(top.shape, LOW, F32)
        total[...] = jnp.zeros(total.shape, F32)

    scores = temper * mm(p_ref[...], q_ref[...], NT)
    high = jnp.maximum(top[...], jnp.max(scores, axis=0, keepdims=True))
    total[...] = total[...] * jnp.exp(top[...] - high) + jnp.sum(
        jnp.exp(scores - high), axis=0, keepdims=True
    )
    top[...] = high

    @pl.when(step == pl.num_programs(0) - 1)
    def _():
        out_ref[...] = top[...] + jnp.log(total[...])


def inside(place, gathered, queries, temper):
    toks, width = queries.shape
    return call(
        functools.partial(inside_kernel, temper), "inside", 2,
        [pl.BlockSpec((gathered.shape[0] // 2, width), lambda s, _: (s, 0)), full((toks, width))],
        full((1, toks)), jax.ShapeDtypeStruct((1, toks), F32),
        [pltpu.VMEM((1, toks), F32), pltpu.VMEM((1, toks), F32)], MIDDLE,
    )(place, gathered, queries)


def asking_rows(first, second, base, cap):
    def piece(ref, s):
        return ref[base + s * cap : base + (s + 1) * cap, :]

    pairs = [(dx, dy) for dx in range(SIDE) for dy in range(SIDE)]
    one = jnp.concatenate([piece(first[dy], dx) for dx, dy in pairs], axis=0)
    two = jnp.concatenate([piece(second[dx], dy) for dx, dy in pairs], axis=0)
    return one, two


def source_mask(place_ref, reps, cap):
    shape = (reps, reps * cap)
    dx = iota(shape, 1) // (SIDE * cap)
    dy = iota(shape, 1) // cap % SIDE
    x = (place_ref[1] + SIDE - dx) % SIDE
    y = (place_ref[2] + SIDE - dy) % SIDE
    return iota(shape, 0) == x * SIDE + y


def hard_kernel(reps, cap, temper, place_ref, *refs):
    first, second, exts = refs[0:4], refs[4:8], refs[8:12]
    p_ref, inside_ref = refs[12:14]
    out_first, out_second = refs[14:18], refs[18:22]
    hs_ref, code_ref, part_ref, top, total = refs[22:]
    step = pl.program_id(0)
    levels = pl.num_programs(0) - 1
    toks = inside_ref.shape[1]
    half_width = p_ref.shape[1] // 2
    slots = reps * cap
    groups = code_ref.shape[0] // 2
    source = source_mask(place_ref, reps, cap)

    @pl.when(step == 0)
    def _():
        top[...] = jnp.full(top.shape, LOW, F32)
        total[...] = jnp.zeros(total.shape, F32)
        table = jnp.concatenate([ext[...] for ext in exts], axis=0)[:, : groups * cap]
        shape = (groups * cap, groups * slots)
        lane, slot = iota(shape, 0), iota(shape, 1)
        to_slot = (lane == slot // slots * cap + slot % cap).astype(BF16)
        laid = mm(table, to_slot)
        row, slot = iota(laid.shape, 0), iota(laid.shape, 1) % slots
        dx, dy = slot // (SIDE * cap), slot // cap % SIDE
        want = dy * 16 + dx
        ids = jnp.sum(jnp.where(row == want, laid, 0.0), axis=0, keepdims=True).astype(I32)
        tok = jnp.sum(jnp.where(row == want + SIDE, laid, 0.0), axis=0, keepdims=True).astype(I32)
        for g in range(groups):
            code_ref[g : g + 1, :] = ids[:, g * slots : (g + 1) * slots]
            code_ref[groups + g : groups + g + 1, :] = tok[:, g * slots : (g + 1) * slots]

    @pl.when(step < levels)
    def _():
        values = []
        for core in range(CORES):
            group = CORES * step + core
            ids = code_ref[pl.ds(group, 1), :]
            tok = code_ref[pl.ds(groups + group, 1), :]
            valid = ids > 0
            base = core * SIDE * cap
            one, two = asking_rows(first, second, base, cap)
            passages = p_ref[core * toks : (core + 1) * toks, :]
            cross = mm(passages, jnp.concatenate([one, two], axis=1), NT)
            hit = iota((toks, slots), 0) + 1 == ids
            hs = temper * jnp.sum(jnp.where(hit, cross, 0.0), axis=0, keepdims=True)
            hs_ref[pl.ds(group, 1), :] = hs
            served = mm(hit.astype(BF16), passages, TN).astype(BF16)
            for dx in range(SIDE):
                for dy in range(SIDE):
                    at = (dx * SIDE + dy) * cap
                    out_first[dy][base + dx * cap : base + (dx + 1) * cap, :] = served[
                        at : at + cap, :half_width
                    ]
                    out_second[dx][base + dy * cap : base + (dy + 1) * cap, :] = served[
                        at : at + cap, half_width:
                    ]
            token = ((iota((toks, slots), 0) == tok) & valid).astype(BF16)
            live = source & valid
            parts = jnp.concatenate(
                [split3(jnp.where(live, hs, 0.0)), live.astype(BF16)], axis=0
            )
            laid = mm(parts, token, NT)
            there = laid[3 * reps :] > 0.5
            value = laid[:reps] + laid[reps : 2 * reps] + laid[2 * reps : 3 * reps]
            values.append((there, jnp.where(there, value, LOW)))
        high = top[...]
        for there, value in values:
            high = jnp.maximum(high, value)
        new = total[...] * jnp.exp(top[...] - high)
        for there, value in values:
            new = new + jnp.where(there, jnp.exp(value - high), 0.0)
        total[...] = new
        top[...] = high

    @pl.when(step == levels)
    def _():
        part = jnp.where(total[...] > 0.0, top[...] + jnp.log(total[...]), LOW)
        within = inside_ref[...]
        high = jnp.maximum(part, within)
        both = high + jnp.log(jnp.exp(part - high) + jnp.exp(within - high))
        own = iota(part.shape, 0) == rep_of(place_ref[1], place_ref[2])
        part_ref[...] = jnp.broadcast_to(jnp.where(own, both, part)[None], part_ref.shape)
        pieces = split3(hs_ref[...]).astype(F32)
        pieces = jnp.concatenate([pieces, jnp.zeros((groups, slots), F32)], axis=0)
        pieces = jnp.concatenate(
            [pieces, jnp.zeros((4 * groups, half_width - slots), F32)], axis=1
        ).astype(BF16)
        for out in (*out_first, *out_second):
            out[: 4 * groups, :] = pieces


def hard(place, first, second, gathered, within, temper, reps, cap):
    rows, half_width = first[0].shape
    toks = within.shape[1]
    groups = gathered.shape[0] // toks
    levels = groups // CORES
    slots = reps * cap
    per = CORES * SIDE * cap
    ins = pl.BlockSpec((per, half_width), lambda s, _: (lax.min(s, levels - 1), 0))
    outs = pl.BlockSpec((per, half_width), lambda s, _: (s, 0))
    ext = pl.BlockSpec((16, half_width), lambda s, _: (groups * SIDE * cap // 16, 0))
    made = call(
        functools.partial(hard_kernel, reps, cap, temper), "hard", levels + 1,
        [ins] * 8 + [ext] * 4
        + [pl.BlockSpec((CORES * toks, CORES * half_width),
                        lambda s, _: (lax.min(s, levels - 1), 0)), full((1, toks))],
        [outs] * 8 + [full((groups, slots)), full((2 * groups, slots)), full((reps, reps, toks))],
        [jax.ShapeDtypeStruct((groups * SIDE * cap + 4 * groups, half_width), BF16)] * 8
        + [jax.ShapeDtypeStruct((groups, slots), F32),
           jax.ShapeDtypeStruct((2 * groups, slots), I32),
           jax.ShapeDtypeStruct((reps, reps, toks), F32)],
        [pltpu.VMEM((reps, toks), F32), pltpu.VMEM((reps, toks), F32)], LIGHT,
    )(place, *first, *second, *first, gathered, within)
    return made[0:4], made[4:8], made[8], made[9], made[10]


def own_row(lt_ref, rep):
    lt = lt_ref[...]
    return jnp.sum(jnp.where(iota(lt.shape, 0) == rep, lt, 0.0), axis=0, keepdims=True)


def column_kernel(reps, cap, temper, place_ref, code_ref, hs_ref, lt_ref, *refs):
    first, second = refs[0:4], refs[4:8]
    p_ref, q_ref, gp_ref, mark_ref, d_ref = refs[8:]
    step = pl.program_id(0)
    toks, width = q_ref.shape
    half_width = width // 2
    slots = reps * cap
    groups = code_ref.shape[0] // 2

    @pl.when(step == 0)
    def _():
        log_parts = split3(lt_ref[...])
        source = source_mask(place_ref, reps, cap)
        rows = []
        for g in range(groups):
            valid = code_ref[g : g + 1, :] > 0
            tok = code_ref[groups + g : groups + g + 1, :]
            token = ((iota((toks, slots), 0) == tok) & valid).astype(BF16)
            found = mm(log_parts, token)
            found = found[:reps] + found[reps : 2 * reps] + found[2 * reps :]
            log_slot = jnp.sum(jnp.where(source, found, 0.0), axis=0, keepdims=True)
            rows.append(jnp.where(valid, jnp.exp(hs_ref[g : g + 1, :] - log_slot), 0.0))
        d_ref[...] = jnp.concatenate(rows, axis=0)
        mark_ref[...] = jnp.zeros(mark_ref.shape, F32)

    queries = q_ref[...]
    lt_own = own_row(lt_ref, rep_of(place_ref[1], place_ref[2]))
    for core in range(CORES):
        group = CORES * step + core
        here = pl.ds(core * toks, toks)
        ids = code_ref[pl.ds(group, 1), :]
        d_hard = d_ref[pl.ds(group, 1), :]
        hot = jnp.where(iota((toks, slots), 0) + 1 == ids, d_hard, 0.0).astype(BF16)
        scores = temper * mm(p_ref[here, :], queries, NT)
        eye = (iota((toks, toks), 0) == iota((toks, toks), 1)) & (group == place_ref[0])
        d_scores = (jnp.exp(scores - lt_own) - jnp.where(eye, 1.0, 0.0)).astype(BF16)
        both = jnp.concatenate([hot, d_scores], axis=1)
        one, two = asking_rows(first, second, core * SIDE * cap, cap)
        rows = jnp.concatenate([jnp.concatenate([one, two], axis=1), queries], axis=0)
        gp_ref[here, :] = (temper * mm(both, rows)).astype(BF16)


def column(place, codes, hard_scores, log_total, first, second, gathered, queries, temper, cap):
    reps = log_total.shape[0]
    toks, width = queries.shape
    slots = pl.BlockSpec((CORES * SIDE * cap, width // 2), lambda s, _: (s, 0))
    block = pl.BlockSpec((CORES * toks, width), lambda s, _: (s, 0))
    return call(
        functools.partial(column_kernel, reps, cap, temper), "column",
        gathered.shape[0] // (CORES * toks),
        [full(codes.shape), full(hard_scores.shape), full(log_total.shape)] + [slots] * 8
        + [block, full((toks, width))],
        [block, full((8, 128))],
        [jax.ShapeDtypeStruct(gathered.shape, BF16), jax.ShapeDtypeStruct((8, 128), F32)],
        [pltpu.VMEM(hard_scores.shape, F32)], LIGHT,
    )(place, codes, hard_scores, log_total, *first, *second, gathered, queries)


def inner_kernel(temper, place_ref, lt_ref, p_ref, q_ref, gq_ref, loss_ref):
    step = pl.program_id(0)
    toks, width = q_ref.shape
    lt_own = own_row(lt_ref, rep_of(place_ref[1], place_ref[2]))
    passages = p_ref[...]
    scores = temper * mm(passages, q_ref[...], NT)
    row = iota(scores.shape, 0) + passages.shape[0] * step - toks * place_ref[0]
    eye = row == iota(scores.shape, 1)
    d_scores = (jnp.exp(scores - lt_own) - jnp.where(eye, 1.0, 0.0)).astype(BF16)
    new = mm(d_scores, passages, TN)
    own = jnp.sum(jnp.where(eye, scores, 0.0), axis=0, keepdims=True)

    @pl.when(step == 0)
    def _():
        gq_ref[...] = new
        loss_ref[...] = lt_own - own

    @pl.when(step > 0)
    def _():
        gq_ref[...] += new
        loss_ref[...] -= own


def inner(place, log_total, gathered, queries, temper):
    toks, width = queries.shape
    return call(
        functools.partial(inner_kernel, temper), "inner", 2,
        [full(log_total.shape), pl.BlockSpec((gathered.shape[0] // 2, width), lambda s, _: (s, 0)),
         full((toks, width))],
        [full((toks, width)), full((1, toks))],
        [jax.ShapeDtypeStruct((toks, width), F32), jax.ShapeDtypeStruct((1, toks), F32)],
        [], LIGHT,
    )(place, log_total, gathered, queries)


def reduce_kernel(half, cap, groups, place_ref, lt_ref, *refs):
    ranks, rows, outs = refs[0:4], refs[4:8], refs[9:13]
    toks = lt_ref.shape[1]
    slots = groups * cap
    reps = lt_ref.shape[0]
    shape = (SIDE * slots, 4 * groups)
    group = iota(shape, 0) // cap % groups
    parts = (iota(shape, 1) % groups == group) & (iota(shape, 1) < 3 * groups)
    parts = parts.astype(BF16)
    log_rows = jnp.concatenate(
        [jnp.broadcast_to(own_row(lt_ref, source_of(place_ref, half, s)), (slots, toks))
         for s in range(SIDE)], axis=0
    )
    weights = []
    for line in range(SIDE):
        scores = mm(parts, rows[line][slots * SIDE :, : reps * cap])
        slot, lane = iota(scores.shape, 0), iota(scores.shape, 1)
        s = slot // slots
        block = s * SIDE + line if half == 0 else line * SIDE + s
        hs = jnp.sum(
            jnp.where(lane == block * cap + slot % cap, scores, 0.0), axis=1, keepdims=True
        )
        _, hit = hits_of(ranks[line][...], groups, cap)
        weights.append(jnp.where(hit, jnp.exp(hs - log_rows), 0.0).astype(BF16))
    for s in range(SIDE):
        values = [
            rows[line][(g * SIDE + s) * cap : (g * SIDE + s + 1) * cap, :]
            for line in range(SIDE) for g in range(groups)
        ]
        weight = jnp.concatenate([w[s * slots : (s + 1) * slots] for w in weights], axis=0)
        outs[s][...] = mm(weight, jnp.concatenate(values, axis=0), TN).astype(outs[s].dtype)


def reduce(place, half, log_total, ranks, rows, mark, groups, cap):
    toks = log_total.shape[1]
    shape = (toks, rows[0].shape[1])
    return call(
        functools.partial(reduce_kernel, half, cap, groups), "reduce", 1,
        [full(log_total.shape)] + [full(ranks[0].shape)] * 4 + [full(rows[0].shape)] * 4
        + [full(mark.shape)],
        [full(shape)] * 4,
        [jax.ShapeDtypeStruct(shape, F32)] + [jax.ShapeDtypeStruct(shape, BF16)] * 3, [], HEAVY,
    )(place, log_total, *ranks, *rows, mark)


def final_kernel(temper, place_ref, gq_ref, *refs):
    out_ref = refs[8]
    half_width = out_ref.shape[1] // 2
    for half in range(2):
        lanes = slice(half * half_width, (half + 1) * half_width)
        total = gq_ref[:, lanes]
        for ref in refs[4 * half : 4 * half + 4]:
            total = total + ref[...].astype(F32)
        out_ref[:, lanes] = (temper * total).astype(BF16)


def final(place, within, first, second, temper):
    rows, width = within.shape
    wide = pl.BlockSpec((rows // 4, width), lambda s, _: (s, 0))
    narrow = pl.BlockSpec((rows // 4, width // 2), lambda s, _: (s, 0))
    return call(
        functools.partial(final_kernel, temper), "final", 4, [wide] + [narrow] * 8, wide,
        jax.ShapeDtypeStruct((rows, width), BF16), [], LIGHT,
    )(place, within, *first, *second)


def along(x, half, shift):
    pairs = []
    for i in range(SIDE * SIDE):
        a, b = i // SIDE, i % SIDE
        pairs.append((i, rep_of(a + shift, b) if half == 0 else rep_of(a, b + shift)))
    return lax.ppermute(x, "rep", pairs)


def shards(queries, passages, neg_device, neg_row):
    toks, width = queries.shape
    negs = neg_device.shape[1]
    groups = lax.axis_size("grp")
    reps = lax.axis_size("rep")
    cap = 8 * toks // (groups * reps)
    half_width = width // 2
    temper = 3.0 / math.sqrt(width)
    grp, rep = lax.axis_index("grp"), lax.axis_index("rep")
    place = jnp.stack([grp, rep // SIDE, rep % SIDE]).astype(I32)

    lines = jnp.pad(jnp.stack([neg_device.T, neg_row.T]), ((0, 0), (0, 8 - negs), (0, 0)))
    lines = jnp.pad(lines.reshape(16, toks), ((0, 0), (0, half_width - toks))).astype(BF16)
    sources = []
    for half in range(2):
        block = queries[:, half * half_width : (half + 1) * half_width]
        block = jnp.concatenate([block, lines], axis=0)
        sources.append([block] + [along(block, half, s) for s in range(1, SIDE)])
    gathered = lax.all_gather(passages, "grp", axis=0, tiled=True)

    first, second, ranks_first, ranks_second = ([None] * SIDE for _ in range(4))
    earlier = []
    for shift in (3, 1, 2, 0):
        one, two, ranks_first[shift], ranks_second[shift] = mid(
            place, shift, *sources, earlier, groups, reps, cap, negs
        )
        earlier = [ranks_first[shift]]
        first[shift] = along(one, 1, shift) if shift else one
        second[shift] = along(two, 0, shift) if shift else two

    within = inside(place, gathered, queries, temper)
    back_first, back_second, hard_scores, codes, part = hard(
        place, first, second, gathered, within, temper, reps, cap
    )
    parts = lax.all_to_all(part, "rep", split_axis=0, concat_axis=0, tiled=True)
    high = jnp.max(parts, axis=0)
    log_total = high + jnp.log(jnp.sum(jnp.exp(parts - high), axis=0))

    partial_sum, mark = column(
        place, codes, hard_scores, log_total, first, second, gathered, queries, temper, cap
    )
    grad_passages = lax.psum_scatter(partial_sum, "grp", scatter_dimension=0, tiled=True)
    back_first = [along(v, 1, -s) if s else v for s, v in enumerate(back_first)]
    back_second = [along(v, 0, -s) if s else v for s, v in enumerate(back_second)]
    grad_inner, losses = inner(place, log_total, gathered, queries, temper)

    sums = []
    for half, ranks, rows in ((0, ranks_first, back_first), (1, ranks_second, back_second)):
        made = reduce(place, half, log_total, ranks, rows, mark, groups, cap)
        sums.append([along(v, half, -s) if s else v for s, v in enumerate(made)])
    grad_queries = final(place, grad_inner, *sums, temper)
    return (losses.reshape(toks), grad_queries, grad_passages)


def solution(mesh):
    in_specs = (
        P(("grp", "rep"), None),
        P(("grp", "rep"), None),
        P(("grp", "rep"), None),
        P(("grp", "rep"), None),
    )
    out_specs = (P(("grp", "rep")), P(("grp", "rep"), None), P(("grp", "rep"), None))
    return jax.shard_map(shards, mesh=mesh, in_specs=in_specs, out_specs=out_specs, check_vma=False)
```

```python
import functools
import math

import jax
import jax.numpy as jnp
from jax import lax
from jax.experimental import pallas as pl
from jax.experimental.pallas import tpu as pltpu
from jax.sharding import PartitionSpec as P

F32 = jnp.float32
BF16 = jnp.bfloat16
I32 = jnp.int32
LOW = -1e30
NT = (((1,), (1,)), ((), ()))
TN = (((0,), (0,)), ((), ()))
NN = (((1,), (0,)), ((), ()))
VMEM_LIMIT = 60 * 1024 * 1024


def mm(a, b, dims=NN):
    return lax.dot_general(a, b, dims, preferred_element_type=F32)


def iota(shape, dim):
    return lax.broadcasted_iota(I32, shape, dim)


def split3(x):
    a = x.astype(BF16)
    rest = x - a.astype(F32)
    b = rest.astype(BF16)
    c = (rest - b.astype(F32)).astype(BF16)
    return jnp.concatenate([a, b, c], axis=0)


def full(shape):
    return pl.BlockSpec(shape, lambda *_: (0,) * len(shape))


def call(kernel, name, steps, ins, outs, shapes, scratch, weight):
    return pl.pallas_call(
        kernel,
        grid_spec=pltpu.PrefetchScalarGridSpec(
            num_scalar_prefetch=1, grid=(steps,), in_specs=ins, out_specs=outs,
            scratch_shapes=scratch,
        ),
        out_shape=shapes,
        compiler_params=pltpu.CompilerParams(
            dimension_semantics=("arbitrary",), vmem_limit_bytes=VMEM_LIMIT
        ),
        cost_estimate=pl.CostEstimate(flops=weight, bytes_accessed=1 << 16, transcendentals=0),
        name=name,
    )


LIGHT, MIDDLE, HEAVY = 1 << 20, 1 << 20, 1 << 39
SIDE = 4
CORES = 2


def rep_of(x, y):
    return x % SIDE * SIDE + y % SIDE


def columns_of(place_ref, half, shift):
    x, y = place_ref[1], place_ref[2]
    return rep_of(x, y + shift) if half == 0 else rep_of(x + shift, y)


def source_of(place_ref, half, shift):
    x, y = place_ref[1], place_ref[2]
    return rep_of(x + SIDE - shift, y) if half == 0 else rep_of(x, y + SIDE - shift)


def hits_of(ranks, groups, cap):
    shape = (ranks.shape[0] * cap, ranks.shape[0])
    pick = (iota(shape, 1) == iota(shape, 0) // cap).astype(BF16)
    spread = mm(pick, ranks)
    return pick, spread == (iota(spread.shape, 0) % cap + 1).astype(F32)


def mid_kernel(shift, cap, groups, reps, negs, place_ref, *refs):
    sources = (refs[0:SIDE], refs[SIDE : 2 * SIDE])
    outs, ranks_out = refs[-4:-2], refs[-2:]
    rows, half_width = sources[0][0].shape
    toks = rows - 16
    slots = groups * cap
    before = (iota((toks, toks), 0) < iota((toks, toks), 1)).astype(BF16)
    for half in range(2):
        col = columns_of(place_ref, half, shift)
        dev = (iota((groups, toks), 0) * reps + col).astype(F32)
        named_all, rows_all = [], []
        for source in sources[half]:
            table = source[toks:, :toks].astype(F32)
            named = jnp.zeros((groups, toks), F32)
            wanted = jnp.zeros((groups, toks), F32)
            for k in range(negs):
                hit = dev == table[k : k + 1]
                named = named + jnp.where(hit, 1.0, 0.0)
                wanted = wanted + jnp.where(hit, table[8 + k : 9 + k] + 1.0, 0.0)
            named_all.append(named)
            rows_all.append(wanted)
        named = jnp.concatenate(named_all, axis=0)
        wanted = jnp.concatenate(rows_all, axis=0).astype(BF16)
        ranks = (named * (mm(named.astype(BF16), before) + 1.0)).astype(BF16)
        ranks_out[half][...] = ranks
        pick, hit = hits_of(ranks, groups, cap)
        hot = hit.astype(BF16)
        row = jnp.where(hit, mm(pick, wanted), 0.0).astype(BF16)
        ids = mm(jnp.ones((8, toks), BF16), row, NT)[0:1]
        tok = mm(iota((8, toks), 1).astype(F32).astype(BF16), hot, NT)[0:1]
        for s, source in enumerate(sources[half]):
            moved = mm(hot[s * slots : (s + 1) * slots], source[:toks, :]).astype(BF16)
            for g in range(groups):
                first = (g * SIDE + s) * cap
                outs[half][first : first + cap, :] = moved[g * cap : (g + 1) * cap]
        codes = [v[:, s * slots : (s + 1) * slots] for v in (ids, tok) for s in range(SIDE)]
        codes = jnp.concatenate(codes + [jnp.zeros((8, slots), F32)], axis=0)
        codes = jnp.concatenate([codes, jnp.zeros((16, half_width - slots), F32)], axis=1)
        outs[half][groups * SIDE * cap :, :] = codes.astype(BF16)


def mid(place, shift, first, second, earlier, groups, reps, cap, negs):
    rows, half_width = first[0].shape
    slots = jax.ShapeDtypeStruct((groups * SIDE * cap + 16, half_width), BF16)
    ranks = jax.ShapeDtypeStruct((SIDE * groups, rows - 16), BF16)
    return call(
        functools.partial(mid_kernel, shift, cap, groups, reps, negs), "mid", 1,
        [full((rows, half_width))] * (2 * SIDE) + [full(v.shape) for v in earlier],
        [full(slots.shape)] * 2 + [full(ranks.shape)] * 2,
        [slots, slots, ranks, ranks], [], LIGHT,
    )(place, *first, *second, *earlier)


def inside_kernel(temper, place_ref, p_ref, q_ref, out_ref, top, total):
    step = pl.program_id(0)

    @pl.when(step == 0)
    def _():
        top[...] = jnp.full(top.shape, LOW, F32)
        total[...] = jnp.zeros(total.shape, F32)

    scores = temper * mm(p_ref[...], q_ref[...], NT)
    high = jnp.maximum(top[...], jnp.max(scores, axis=0, keepdims=True))
    total[...] = total[...] * jnp.exp(top[...] - high) + jnp.sum(
        jnp.exp(scores - high), axis=0, keepdims=True
    )
    top[...] = high

    @pl.when(step == pl.num_programs(0) - 1)
    def _():
        out_ref[...] = top[...] + jnp.log(total[...])


def inside(place, gathered, queries, temper):
    toks, width = queries.shape
    return call(
        functools.partial(inside_kernel, temper), "inside", 2,
        [pl.BlockSpec((gathered.shape[0] // 2, width), lambda s, _: (s, 0)), full((toks, width))],
        full((1, toks)), jax.ShapeDtypeStruct((1, toks), F32),
        [pltpu.VMEM((1, toks), F32), pltpu.VMEM((1, toks), F32)], MIDDLE,
    )(place, gathered, queries)


def asking_rows(first, second, base, cap):
    def piece(ref, s):
        return ref[base + s * cap : base + (s + 1) * cap, :]

    pairs = [(dx, dy) for dx in range(SIDE) for dy in range(SIDE)]
    one = jnp.concatenate([piece(first[dy], dx) for dx, dy in pairs], axis=0)
    two = jnp.concatenate([piece(second[dx], dy) for dx, dy in pairs], axis=0)
    return one, two


def source_mask(place_ref, reps, cap):
    shape = (reps, reps * cap)
    dx = iota(shape, 1) // (SIDE * cap)
    dy = iota(shape, 1) // cap % SIDE
    x = (place_ref[1] + SIDE - dx) % SIDE
    y = (place_ref[2] + SIDE - dy) % SIDE
    return iota(shape, 0) == x * SIDE + y


def hard_kernel(reps, cap, temper, place_ref, *refs):
    first, second, exts = refs[0:4], refs[4:8], refs[8:12]
    p_ref, inside_ref = refs[12:14]
    out_first, out_second = refs[14:18], refs[18:22]
    hs_ref, code_ref, part_ref, top, total = refs[22:]
    step = pl.program_id(0)
    levels = pl.num_programs(0) - 1
    toks = inside_ref.shape[1]
    half_width = p_ref.shape[1] // 2
    slots = reps * cap
    groups = code_ref.shape[0] // 2
    source = source_mask(place_ref, reps, cap)

    @pl.when(step == 0)
    def _():
        top[...] = jnp.full(top.shape, LOW, F32)
        total[...] = jnp.zeros(total.shape, F32)
        table = jnp.concatenate([ext[...] for ext in exts], axis=0)[:, : groups * cap]
        shape = (groups * cap, groups * slots)
        lane, slot = iota(shape, 0), iota(shape, 1)
        to_slot = (lane == slot // slots * cap + slot % cap).astype(BF16)
        laid = mm(table, to_slot)
        row, slot = iota(laid.shape, 0), iota(laid.shape, 1) % slots
        dx, dy = slot // (SIDE * cap), slot // cap % SIDE
        want = dy * 16 + dx
        ids = jnp.sum(jnp.where(row == want, laid, 0.0), axis=0, keepdims=True).astype(I32)
        tok = jnp.sum(jnp.where(row == want + SIDE, laid, 0.0), axis=0, keepdims=True).astype(I32)
        for g in range(groups):
            code_ref[g : g + 1, :] = ids[:, g * slots : (g + 1) * slots]
            code_ref[groups + g : groups + g + 1, :] = tok[:, g * slots : (g + 1) * slots]

    @pl.when(step < levels)
    def _():
        values = []
        for core in range(CORES):
            group = CORES * step + core
            ids = code_ref[pl.ds(group, 1), :]
            tok = code_ref[pl.ds(groups + group, 1), :]
            valid = ids > 0
            base = core * SIDE * cap
            one, two = asking_rows(first, second, base, cap)
            passages = p_ref[core * toks : (core + 1) * toks, :]
            cross = mm(passages, jnp.concatenate([one, two], axis=1), NT)
            hit = iota((toks, slots), 0) + 1 == ids
            hs = temper * jnp.sum(jnp.where(hit, cross, 0.0), axis=0, keepdims=True)
            hs_ref[pl.ds(group, 1), :] = hs
            served = mm(hit.astype(BF16), passages, TN).astype(BF16)
            for dx in range(SIDE):
                for dy in range(SIDE):
                    at = (dx * SIDE + dy) * cap
                    out_first[dy][base + dx * cap : base + (dx + 1) * cap, :] = served[
                        at : at + cap, :half_width
                    ]
                    out_second[dx][base + dy * cap : base + (dy + 1) * cap, :] = served[
                        at : at + cap, half_width:
                    ]
            token = ((iota((toks, slots), 0) == tok) & valid).astype(BF16)
            live = source & valid
            parts = jnp.concatenate(
                [split3(jnp.where(live, hs, 0.0)), live.astype(BF16)], axis=0
            )
            laid = mm(parts, token, NT)
            there = laid[3 * reps :] > 0.5
            value = laid[:reps] + laid[reps : 2 * reps] + laid[2 * reps : 3 * reps]
            values.append((there, jnp.where(there, value, LOW)))
        high = top[...]
        for there, value in values:
            high = jnp.maximum(high, value)
        new = total[...] * jnp.exp(top[...] - high)
        for there, value in values:
            new = new + jnp.where(there, jnp.exp(value - high), 0.0)
        total[...] = new
        top[...] = high

    @pl.when(step == levels)
    def _():
        part = jnp.where(total[...] > 0.0, top[...] + jnp.log(total[...]), LOW)
        within = inside_ref[...]
        high = jnp.maximum(part, within)
        both = high + jnp.log(jnp.exp(part - high) + jnp.exp(within - high))
        own = iota(part.shape, 0) == rep_of(place_ref[1], place_ref[2])
        part_ref[...] = jnp.broadcast_to(jnp.where(own, both, part)[None], part_ref.shape)
        pieces = split3(hs_ref[...]).astype(F32)
        pieces = jnp.concatenate([pieces, jnp.zeros((groups, slots), F32)], axis=0)
        pieces = jnp.concatenate(
            [pieces, jnp.zeros((4 * groups, half_width - slots), F32)], axis=1
        ).astype(BF16)
        for out in (*out_first, *out_second):
            out[: 4 * groups, :] = pieces


def hard(place, first, second, gathered, within, temper, reps, cap):
    rows, half_width = first[0].shape
    toks = within.shape[1]
    groups = gathered.shape[0] // toks
    levels = groups // CORES
    slots = reps * cap
    per = CORES * SIDE * cap
    ins = pl.BlockSpec((per, half_width), lambda s, _: (lax.min(s, levels - 1), 0))
    outs = pl.BlockSpec((per, half_width), lambda s, _: (s, 0))
    ext = pl.BlockSpec((16, half_width), lambda s, _: (groups * SIDE * cap // 16, 0))
    made = call(
        functools.partial(hard_kernel, reps, cap, temper), "hard", levels + 1,
        [ins] * 8 + [ext] * 4
        + [pl.BlockSpec((CORES * toks, CORES * half_width),
                        lambda s, _: (lax.min(s, levels - 1), 0)), full((1, toks))],
        [outs] * 8 + [full((groups, slots)), full((2 * groups, slots)), full((reps, reps, toks))],
        [jax.ShapeDtypeStruct((groups * SIDE * cap + 4 * groups, half_width), BF16)] * 8
        + [jax.ShapeDtypeStruct((groups, slots), F32),
           jax.ShapeDtypeStruct((2 * groups, slots), I32),
           jax.ShapeDtypeStruct((reps, reps, toks), F32)],
        [pltpu.VMEM((reps, toks), F32), pltpu.VMEM((reps, toks), F32)], LIGHT,
    )(place, *first, *second, *first, gathered, within)
    return made[0:4], made[4:8], made[8], made[9], made[10]


def own_row(lt_ref, rep):
    lt = lt_ref[...]
    return jnp.sum(jnp.where(iota(lt.shape, 0) == rep, lt, 0.0), axis=0, keepdims=True)


def column_kernel(reps, cap, temper, place_ref, code_ref, hs_ref, lt_ref, *refs):
    first, second = refs[0:4], refs[4:8]
    p_ref, q_ref, gp_ref, gq_ref, loss_ref, mark_ref, d_ref = refs[8:]
    step = pl.program_id(0)
    toks, width = q_ref.shape
    slots = reps * cap
    groups = code_ref.shape[0] // 2

    @pl.when(step == 0)
    def _():
        log_parts = split3(lt_ref[...])
        source = source_mask(place_ref, reps, cap)
        rows = []
        for g in range(groups):
            valid = code_ref[g : g + 1, :] > 0
            tok = code_ref[groups + g : groups + g + 1, :]
            token = ((iota((toks, slots), 0) == tok) & valid).astype(BF16)
            found = mm(log_parts, token)
            found = found[:reps] + found[reps : 2 * reps] + found[2 * reps :]
            log_slot = jnp.sum(jnp.where(source, found, 0.0), axis=0, keepdims=True)
            rows.append(jnp.where(valid, jnp.exp(hs_ref[g : g + 1, :] - log_slot), 0.0))
        d_ref[...] = jnp.concatenate(rows, axis=0)
        mark_ref[...] = jnp.zeros(mark_ref.shape, F32)
        loss_ref[...] = own_row(lt_ref, rep_of(place_ref[1], place_ref[2]))

    queries = q_ref[...]
    passages = p_ref[...]
    lt_own = own_row(lt_ref, rep_of(place_ref[1], place_ref[2]))
    scores = temper * mm(passages, queries, NT)
    row = iota(scores.shape, 0) + CORES * toks * step - toks * place_ref[0]
    eye = row == iota(scores.shape, 1)
    d_scores = (jnp.exp(scores - lt_own) - jnp.where(eye, 1.0, 0.0)).astype(BF16)
    loss_ref[...] -= jnp.sum(jnp.where(eye, scores, 0.0), axis=0, keepdims=True)
    for core in range(CORES):
        group = CORES * step + core
        here = slice(core * toks, (core + 1) * toks)
        ids = code_ref[pl.ds(group, 1), :]
        d_hard = d_ref[pl.ds(group, 1), :]
        hot = jnp.where(iota((toks, slots), 0) + 1 == ids, d_hard, 0.0).astype(BF16)
        both = jnp.concatenate([hot, d_scores[here]], axis=1)
        one, two = asking_rows(first, second, core * SIDE * cap, cap)
        rows = jnp.concatenate([jnp.concatenate([one, two], axis=1), queries], axis=0)
        gp_ref[here, :] = (temper * mm(both, rows)).astype(BF16)
    new = mm(d_scores, passages, TN)

    @pl.when(step == 0)
    def _():
        gq_ref[...] = new

    @pl.when(step > 0)
    def _():
        gq_ref[...] += new


def column(place, codes, hard_scores, log_total, first, second, gathered, queries, temper, cap):
    reps = log_total.shape[0]
    toks, width = queries.shape
    slots = pl.BlockSpec((CORES * SIDE * cap, width // 2), lambda s, _: (s, 0))
    block = pl.BlockSpec((CORES * toks, width), lambda s, _: (s, 0))
    return call(
        functools.partial(column_kernel, reps, cap, temper), "column",
        gathered.shape[0] // (CORES * toks),
        [full(codes.shape), full(hard_scores.shape), full(log_total.shape)] + [slots] * 8
        + [block, full((toks, width))],
        [block, full((toks, width)), full((1, toks)), full((8, 128))],
        [jax.ShapeDtypeStruct(gathered.shape, BF16), jax.ShapeDtypeStruct((toks, width), F32),
         jax.ShapeDtypeStruct((1, toks), F32), jax.ShapeDtypeStruct((8, 128), F32)],
        [pltpu.VMEM(hard_scores.shape, F32)], LIGHT,
    )(place, codes, hard_scores, log_total, *first, *second, gathered, queries)


def reduce_kernel(half, cap, groups, place_ref, lt_ref, *refs):
    ranks, rows, outs = refs[0:4], refs[4:8], refs[9:13]
    toks = lt_ref.shape[1]
    slots = groups * cap
    reps = lt_ref.shape[0]
    shape = (SIDE * slots, 4 * groups)
    group = iota(shape, 0) // cap % groups
    parts = (iota(shape, 1) % groups == group) & (iota(shape, 1) < 3 * groups)
    parts = parts.astype(BF16)
    log_rows = jnp.concatenate(
        [jnp.broadcast_to(own_row(lt_ref, source_of(place_ref, half, s)), (slots, toks))
         for s in range(SIDE)], axis=0
    )
    weights = []
    for line in range(SIDE):
        scores = mm(parts, rows[line][slots * SIDE :, : reps * cap])
        slot, lane = iota(scores.shape, 0), iota(scores.shape, 1)
        s = slot // slots
        block = s * SIDE + line if half == 0 else line * SIDE + s
        hs = jnp.sum(
            jnp.where(lane == block * cap + slot % cap, scores, 0.0), axis=1, keepdims=True
        )
        _, hit = hits_of(ranks[line][...], groups, cap)
        weights.append(jnp.where(hit, jnp.exp(hs - log_rows), 0.0).astype(BF16))
    for s in range(SIDE):
        values = [
            rows[line][(g * SIDE + s) * cap : (g * SIDE + s + 1) * cap, :]
            for line in range(SIDE) for g in range(groups)
        ]
        weight = jnp.concatenate([w[s * slots : (s + 1) * slots] for w in weights], axis=0)
        outs[s][...] = mm(weight, jnp.concatenate(values, axis=0), TN).astype(outs[s].dtype)


def reduce(place, half, log_total, ranks, rows, mark, groups, cap):
    toks = log_total.shape[1]
    shape = (toks, rows[0].shape[1])
    return call(
        functools.partial(reduce_kernel, half, cap, groups), "reduce", 1,
        [full(log_total.shape)] + [full(ranks[0].shape)] * 4 + [full(rows[0].shape)] * 4
        + [full(mark.shape)],
        [full(shape)] * 4,
        [jax.ShapeDtypeStruct(shape, F32)] + [jax.ShapeDtypeStruct(shape, BF16)] * 3, [], HEAVY,
    )(place, log_total, *ranks, *rows, mark)


def final_kernel(temper, place_ref, gq_ref, *refs):
    out_ref = refs[8]
    half_width = out_ref.shape[1] // 2
    for half in range(2):
        lanes = slice(half * half_width, (half + 1) * half_width)
        total = gq_ref[:, lanes]
        for ref in refs[4 * half : 4 * half + 4]:
            total = total + ref[...].astype(F32)
        out_ref[:, lanes] = (temper * total).astype(BF16)


def final(place, within, first, second, temper):
    shape = within.shape
    return call(
        functools.partial(final_kernel, temper), "final", 1,
        [full(shape)] + [full(first[0].shape)] * 8, full(shape),
        jax.ShapeDtypeStruct(shape, BF16), [], LIGHT,
    )(place, within, *first, *second)


def along(x, half, shift):
    pairs = []
    for i in range(SIDE * SIDE):
        a, b = i // SIDE, i % SIDE
        pairs.append((i, rep_of(a + shift, b) if half == 0 else rep_of(a, b + shift)))
    return lax.ppermute(x, "rep", pairs)


def shards(queries, passages, neg_device, neg_row):
    toks, width = queries.shape
    negs = neg_device.shape[1]
    groups = lax.axis_size("grp")
    reps = lax.axis_size("rep")
    cap = 8 * toks // (groups * reps)
    half_width = width // 2
    temper = 3.0 / math.sqrt(width)
    grp, rep = lax.axis_index("grp"), lax.axis_index("rep")
    place = jnp.stack([grp, rep // SIDE, rep % SIDE]).astype(I32)

    lines = jnp.pad(jnp.stack([neg_device.T, neg_row.T]), ((0, 0), (0, 8 - negs), (0, 0)))
    lines = jnp.pad(lines.reshape(16, toks), ((0, 0), (0, half_width - toks))).astype(BF16)
    sources = []
    for half in range(2):
        block = queries[:, half * half_width : (half + 1) * half_width]
        block = jnp.concatenate([block, lines], axis=0)
        sources.append([block] + [along(block, half, s) for s in range(1, SIDE)])
    gathered = lax.all_gather(passages, "grp", axis=0, tiled=True)

    first, second, ranks_first, ranks_second = ([None] * SIDE for _ in range(4))
    earlier = []
    for shift in (2, 1, 3, 0):
        one, two, ranks_first[shift], ranks_second[shift] = mid(
            place, shift, *sources, earlier, groups, reps, cap, negs
        )
        earlier = [ranks_first[shift]]
        first[shift] = along(one, 1, shift) if shift else one
        second[shift] = along(two, 0, shift) if shift else two

    within = inside(place, gathered, queries, temper)
    back_first, back_second, hard_scores, codes, part = hard(
        place, first, second, gathered, within, temper, reps, cap
    )
    parts = lax.all_to_all(part, "rep", split_axis=0, concat_axis=0, tiled=True)
    high = jnp.max(parts, axis=0)
    log_total = high + jnp.log(jnp.sum(jnp.exp(parts - high), axis=0))

    partial_sum, grad_inner, losses, mark = column(
        place, codes, hard_scores, log_total, first, second, gathered, queries, temper, cap
    )
    grad_passages = lax.psum_scatter(partial_sum, "grp", scatter_dimension=0, tiled=True)
    back_first = [along(v, 1, -s) if s else v for s, v in enumerate(back_first)]
    back_second = [along(v, 0, -s) if s else v for s, v in enumerate(back_second)]

    sums = []
    for half, ranks, rows in ((0, ranks_first, back_first), (1, ranks_second, back_second)):
        made = reduce(place, half, log_total, ranks, rows, mark, groups, cap)
        sums.append([along(v, half, -s) if s else v for s, v in enumerate(made)])
    grad_queries = final(place, grad_inner, *sums, temper)
    return (losses.reshape(toks), grad_queries, grad_passages)


def solution(mesh):
    in_specs = (
        P(("grp", "rep"), None),
        P(("grp", "rep"), None),
        P(("grp", "rep"), None),
        P(("grp", "rep"), None),
    )
    out_specs = (P(("grp", "rep")), P(("grp", "rep"), None), P(("grp", "rep"), None))
    return jax.shard_map(shards, mesh=mesh, in_specs=in_specs, out_specs=out_specs, check_vma=False)
```

```python
import functools
import math

import jax
import jax.numpy as jnp
from jax import lax
from jax.experimental import pallas as pl
from jax.experimental.pallas import tpu as pltpu
from jax.sharding import PartitionSpec as P

F32 = jnp.float32
BF16 = jnp.bfloat16
I32 = jnp.int32
LOW = -1e30
NT = (((1,), (1,)), ((), ()))
TN = (((0,), (0,)), ((), ()))
NN = (((1,), (0,)), ((), ()))
VMEM_LIMIT = 63 * 1024 * 1024


def mm(a, b, dims=NN):
    return lax.dot_general(a, b, dims, preferred_element_type=F32)


def iota(shape, dim):
    return lax.broadcasted_iota(I32, shape, dim)


def split3(x):
    a = x.astype(BF16)
    rest = x - a.astype(F32)
    b = rest.astype(BF16)
    c = (rest - b.astype(F32)).astype(BF16)
    return jnp.concatenate([a, b, c], axis=0)


def full(shape):
    return pl.BlockSpec(shape, lambda *_: (0,) * len(shape))


def call(kernel, name, steps, ins, outs, shapes, scratch, weight):
    return pl.pallas_call(
        kernel,
        grid_spec=pltpu.PrefetchScalarGridSpec(
            num_scalar_prefetch=1, grid=(steps,), in_specs=ins, out_specs=outs,
            scratch_shapes=scratch,
        ),
        out_shape=shapes,
        compiler_params=pltpu.CompilerParams(
            dimension_semantics=("arbitrary",), vmem_limit_bytes=VMEM_LIMIT
        ),
        cost_estimate=pl.CostEstimate(flops=weight, bytes_accessed=1 << 16, transcendentals=0),
        name=name,
    )


ANY = pl.BlockSpec(memory_space=pl.ANY)
LIGHT, MIDDLE, HEAVY = 1 << 20, 1 << 20, 1 << 39
SIDE = 4
CORES = 2


def rep_of(x, y):
    return x % SIDE * SIDE + y % SIDE


def columns_of(place_ref, half, shift):
    x, y = place_ref[1], place_ref[2]
    return rep_of(x, y + shift) if half == 0 else rep_of(x + shift, y)


def source_of(place_ref, half, shift):
    x, y = place_ref[1], place_ref[2]
    return rep_of(x + SIDE - shift, y) if half == 0 else rep_of(x, y + SIDE - shift)


def hits_of(ranks, groups, cap):
    shape = (ranks.shape[0] * cap, ranks.shape[0])
    pick = (iota(shape, 1) == iota(shape, 0) // cap).astype(BF16)
    spread = mm(pick, ranks)
    return pick, spread == (iota(spread.shape, 0) % cap + 1).astype(F32)


def mid_kernel(shift, cap, groups, reps, negs, place_ref, *refs):
    sources = (refs[0:SIDE], refs[SIDE : 2 * SIDE])
    outs, ranks_out = refs[-4:-2], refs[-2:]
    rows, half_width = sources[0][0].shape
    toks = rows - 16
    slots = groups * cap
    before = (iota((toks, toks), 0) < iota((toks, toks), 1)).astype(BF16)
    for half in range(2):
        col = columns_of(place_ref, half, shift)
        dev = (iota((groups, toks), 0) * reps + col).astype(F32)
        named_all, rows_all = [], []
        for source in sources[half]:
            table = source[toks:, :toks].astype(F32)
            named = jnp.zeros((groups, toks), F32)
            wanted = jnp.zeros((groups, toks), F32)
            for k in range(negs):
                hit = dev == table[k : k + 1]
                named = named + jnp.where(hit, 1.0, 0.0)
                wanted = wanted + jnp.where(hit, table[8 + k : 9 + k] + 1.0, 0.0)
            named_all.append(named)
            rows_all.append(wanted)
        named = jnp.concatenate(named_all, axis=0)
        wanted = jnp.concatenate(rows_all, axis=0).astype(BF16)
        ranks = (named * (mm(named.astype(BF16), before) + 1.0)).astype(BF16)
        ranks_out[half][...] = ranks
        pick, hit = hits_of(ranks, groups, cap)
        hot = hit.astype(BF16)
        row = jnp.where(hit, mm(pick, wanted), 0.0).astype(BF16)
        ids = mm(jnp.ones((8, toks), BF16), row, NT)[0:1]
        tok = mm(iota((8, toks), 1).astype(F32).astype(BF16), hot, NT)[0:1]
        for s, source in enumerate(sources[half]):
            moved = mm(hot[s * slots : (s + 1) * slots], source[:toks, :]).astype(BF16)
            for g in range(groups):
                first = (g * SIDE + s) * cap
                outs[half][first : first + cap, :] = moved[g * cap : (g + 1) * cap]
        codes = [v[:, s * slots : (s + 1) * slots] for v in (ids, tok) for s in range(SIDE)]
        codes = jnp.concatenate(codes + [jnp.zeros((8, slots), F32)], axis=0)
        codes = jnp.concatenate([codes, jnp.zeros((16, half_width - slots), F32)], axis=1)
        outs[half][groups * SIDE * cap :, :] = codes.astype(BF16)


def mid(place, shift, first, second, earlier, groups, reps, cap, negs):
    rows, half_width = first[0].shape
    slots = jax.ShapeDtypeStruct((groups * SIDE * cap + 16, half_width), BF16)
    ranks = jax.ShapeDtypeStruct((SIDE * groups, rows - 16), BF16)
    return call(
        functools.partial(mid_kernel, shift, cap, groups, reps, negs), "mid", 1,
        [full((rows, half_width))] * (2 * SIDE) + [full(v.shape) for v in earlier],
        [full(slots.shape)] * 2 + [full(ranks.shape)] * 2,
        [slots, slots, ranks, ranks], [], LIGHT,
    )(place, *first, *second, *earlier)


def inside_kernel(temper, place_ref, p_ref, q_ref, out_ref, top, total):
    step = pl.program_id(0)

    @pl.when(step == 0)
    def _():
        top[...] = jnp.full(top.shape, LOW, F32)
        total[...] = jnp.zeros(total.shape, F32)

    scores = temper * mm(p_ref[...], q_ref[...], NT)
    high = jnp.maximum(top[...], jnp.max(scores, axis=0, keepdims=True))
    total[...] = total[...] * jnp.exp(top[...] - high) + jnp.sum(
        jnp.exp(scores - high), axis=0, keepdims=True
    )
    top[...] = high

    @pl.when(step == pl.num_programs(0) - 1)
    def _():
        out_ref[...] = top[...] + jnp.log(total[...])


def inside(place, gathered, queries, temper):
    toks, width = queries.shape
    return call(
        functools.partial(inside_kernel, temper), "inside", 2,
        [pl.BlockSpec((gathered.shape[0] // 2, width), lambda s, _: (s, 0)), full((toks, width))],
        full((1, toks)), jax.ShapeDtypeStruct((1, toks), F32),
        [pltpu.VMEM((1, toks), F32), pltpu.VMEM((1, toks), F32)], MIDDLE,
    )(place, gathered, queries)


def asking_rows(first, second, base, cap):
    def piece(ref, s):
        return ref[base + s * cap : base + (s + 1) * cap, :]

    pairs = [(dx, dy) for dx in range(SIDE) for dy in range(SIDE)]
    one = jnp.concatenate([piece(first[dy], dx) for dx, dy in pairs], axis=0)
    two = jnp.concatenate([piece(second[dx], dy) for dx, dy in pairs], axis=0)
    return one, two


def source_mask(place_ref, reps, cap):
    shape = (reps, reps * cap)
    dx = iota(shape, 1) // (SIDE * cap)
    dy = iota(shape, 1) // cap % SIDE
    x = (place_ref[1] + SIDE - dx) % SIDE
    y = (place_ref[2] + SIDE - dy) % SIDE
    return iota(shape, 0) == x * SIDE + y


def hard_kernel(reps, cap, temper, place_ref, *refs):
    first, second, exts = refs[0:4], refs[4:8], refs[8:12]
    p_ref, inside_ref = refs[12:14]
    out_first, out_second = refs[14:18], refs[18:22]
    hs_ref, code_ref, part_ref, top, total = refs[22:]
    step = pl.program_id(0)
    levels = pl.num_programs(0) - 1
    toks = inside_ref.shape[1]
    half_width = p_ref.shape[1] // 2
    slots = reps * cap
    groups = code_ref.shape[0] // 2
    source = source_mask(place_ref, reps, cap)

    @pl.when(step == 0)
    def _():
        top[...] = jnp.full(top.shape, LOW, F32)
        total[...] = jnp.zeros(total.shape, F32)
        table = jnp.concatenate([ext[...] for ext in exts], axis=0)[:, : groups * cap]
        shape = (groups * cap, groups * slots)
        lane, slot = iota(shape, 0), iota(shape, 1)
        to_slot = (lane == slot // slots * cap + slot % cap).astype(BF16)
        laid = mm(table, to_slot)
        row, slot = iota(laid.shape, 0), iota(laid.shape, 1) % slots
        dx, dy = slot // (SIDE * cap), slot // cap % SIDE
        want = dy * 16 + dx
        ids = jnp.sum(jnp.where(row == want, laid, 0.0), axis=0, keepdims=True).astype(I32)
        tok = jnp.sum(jnp.where(row == want + SIDE, laid, 0.0), axis=0, keepdims=True).astype(I32)
        for g in range(groups):
            code_ref[g : g + 1, :] = ids[:, g * slots : (g + 1) * slots]
            code_ref[groups + g : groups + g + 1, :] = tok[:, g * slots : (g + 1) * slots]

    @pl.when(step < levels)
    def _():
        values = []
        for core in range(CORES):
            group = CORES * step + core
            ids = code_ref[pl.ds(group, 1), :]
            tok = code_ref[pl.ds(groups + group, 1), :]
            valid = ids > 0
            base = core * SIDE * cap
            one, two = asking_rows(first, second, base, cap)
            passages = p_ref[core * toks : (core + 1) * toks, :]
            cross = mm(passages, jnp.concatenate([one, two], axis=1), NT)
            hit = iota((toks, slots), 0) + 1 == ids
            hs = temper * jnp.sum(jnp.where(hit, cross, 0.0), axis=0, keepdims=True)
            hs_ref[pl.ds(group, 1), :] = hs
            served = mm(hit.astype(BF16), passages, TN).astype(BF16)
            for dx in range(SIDE):
                for dy in range(SIDE):
                    at = (dx * SIDE + dy) * cap
                    out_first[dy][base + dx * cap : base + (dx + 1) * cap, :] = served[
                        at : at + cap, :half_width
                    ]
                    out_second[dx][base + dy * cap : base + (dy + 1) * cap, :] = served[
                        at : at + cap, half_width:
                    ]
            token = ((iota((toks, slots), 0) == tok) & valid).astype(BF16)
            live = source & valid
            parts = jnp.concatenate(
                [split3(jnp.where(live, hs, 0.0)), live.astype(BF16)], axis=0
            )
            laid = mm(parts, token, NT)
            there = laid[3 * reps :] > 0.5
            value = laid[:reps] + laid[reps : 2 * reps] + laid[2 * reps : 3 * reps]
            values.append((there, jnp.where(there, value, LOW)))
        high = top[...]
        for there, value in values:
            high = jnp.maximum(high, value)
        new = total[...] * jnp.exp(top[...] - high)
        for there, value in values:
            new = new + jnp.where(there, jnp.exp(value - high), 0.0)
        total[...] = new
        top[...] = high

    @pl.when(step == levels)
    def _():
        part = jnp.where(total[...] > 0.0, top[...] + jnp.log(total[...]), LOW)
        within = inside_ref[...]
        high = jnp.maximum(part, within)
        both = high + jnp.log(jnp.exp(part - high) + jnp.exp(within - high))
        own = iota(part.shape, 0) == rep_of(place_ref[1], place_ref[2])
        part_ref[...] = jnp.broadcast_to(jnp.where(own, both, part)[None], part_ref.shape)
        pieces = split3(hs_ref[...]).astype(F32)
        pieces = jnp.concatenate([pieces, jnp.zeros((groups, slots), F32)], axis=0)
        pieces = jnp.concatenate(
            [pieces, jnp.zeros((4 * groups, half_width - slots), F32)], axis=1
        ).astype(BF16)
        for out in (*out_first, *out_second):
            out[: 4 * groups, :] = pieces


def hard(place, first, second, gathered, within, temper, reps, cap):
    rows, half_width = first[0].shape
    toks = within.shape[1]
    groups = gathered.shape[0] // toks
    levels = groups // CORES
    slots = reps * cap
    per = CORES * SIDE * cap
    ins = pl.BlockSpec((per, half_width), lambda s, _: (lax.min(s, levels - 1), 0))
    outs = pl.BlockSpec((per, half_width), lambda s, _: (s, 0))
    ext = pl.BlockSpec((16, half_width), lambda s, _: (groups * SIDE * cap // 16, 0))
    made = call(
        functools.partial(hard_kernel, reps, cap, temper), "hard", levels + 1,
        [ins] * 8 + [ext] * 4
        + [pl.BlockSpec((CORES * toks, CORES * half_width),
                        lambda s, _: (lax.min(s, levels - 1), 0)), full((1, toks))],
        [outs] * 8 + [full((groups, slots)), full((2 * groups, slots)), full((reps, reps, toks))],
        [jax.ShapeDtypeStruct((groups * SIDE * cap + 4 * groups, half_width), BF16)] * 8
        + [jax.ShapeDtypeStruct((groups, slots), F32),
           jax.ShapeDtypeStruct((2 * groups, slots), I32),
           jax.ShapeDtypeStruct((reps, reps, toks), F32)],
        [pltpu.VMEM((reps, toks), F32), pltpu.VMEM((reps, toks), F32)], LIGHT,
    )(place, *first, *second, *first, gathered, within)
    return made[0:4], made[4:8], made[8], made[9], made[10]


def own_row(lt_ref, rep):
    lt = lt_ref[...]
    return jnp.sum(jnp.where(iota(lt.shape, 0) == rep, lt, 0.0), axis=0, keepdims=True)


def column_kernel(reps, cap, temper, place_ref, code_ref, hs_ref, lt_ref, *refs):
    first, second = refs[0:4], refs[4:8]
    p_ref, q_ref, gp_ref, gq_ref, loss_ref, mark_ref, d_ref = refs[8:]
    step = pl.program_id(0)
    toks, width = q_ref.shape
    slots = reps * cap
    groups = code_ref.shape[0] // 2

    @pl.when(step == 0)
    def _():
        log_parts = split3(lt_ref[...])
        source = source_mask(place_ref, reps, cap)
        rows = []
        for g in range(groups):
            valid = code_ref[g : g + 1, :] > 0
            tok = code_ref[groups + g : groups + g + 1, :]
            token = ((iota((toks, slots), 0) == tok) & valid).astype(BF16)
            found = mm(log_parts, token)
            found = found[:reps] + found[reps : 2 * reps] + found[2 * reps :]
            log_slot = jnp.sum(jnp.where(source, found, 0.0), axis=0, keepdims=True)
            rows.append(jnp.where(valid, jnp.exp(hs_ref[g : g + 1, :] - log_slot), 0.0))
        d_ref[...] = jnp.concatenate(rows, axis=0)
        mark_ref[...] = jnp.zeros(mark_ref.shape, F32)
        loss_ref[...] = own_row(lt_ref, rep_of(place_ref[1], place_ref[2]))

    queries = q_ref[...]
    passages = p_ref[...]
    lt_own = own_row(lt_ref, rep_of(place_ref[1], place_ref[2]))
    scores = temper * mm(passages, queries, NT)
    row = iota(scores.shape, 0) + CORES * toks * step - toks * place_ref[0]
    eye = row == iota(scores.shape, 1)
    d_scores = (jnp.exp(scores - lt_own) - jnp.where(eye, 1.0, 0.0)).astype(BF16)
    loss_ref[...] -= jnp.sum(jnp.where(eye, scores, 0.0), axis=0, keepdims=True)
    for core in range(CORES):
        group = CORES * step + core
        here = slice(core * toks, (core + 1) * toks)
        ids = code_ref[pl.ds(group, 1), :]
        d_hard = d_ref[pl.ds(group, 1), :]
        hot = jnp.where(iota((toks, slots), 0) + 1 == ids, d_hard, 0.0).astype(BF16)
        both = jnp.concatenate([hot, d_scores[here]], axis=1)
        one, two = asking_rows(first, second, core * SIDE * cap, cap)
        rows = jnp.concatenate([jnp.concatenate([one, two], axis=1), queries], axis=0)
        gp_ref[here, :] = (temper * mm(both, rows)).astype(BF16)
    new = mm(d_scores, passages, TN)

    @pl.when(step == 0)
    def _():
        gq_ref[...] = new

    @pl.when(step > 0)
    def _():
        gq_ref[...] += new


def column(place, codes, hard_scores, log_total, first, second, gathered, queries, temper, cap):
    reps = log_total.shape[0]
    toks, width = queries.shape
    slots = pl.BlockSpec((CORES * SIDE * cap, width // 2), lambda s, _: (s, 0))
    block = pl.BlockSpec((CORES * toks, width), lambda s, _: (s, 0))
    return call(
        functools.partial(column_kernel, reps, cap, temper), "column",
        gathered.shape[0] // (CORES * toks),
        [full(codes.shape), full(hard_scores.shape), full(log_total.shape)] + [slots] * 8
        + [block, full((toks, width))],
        [block, full((toks, width)), full((1, toks)), full((8, 128))],
        [jax.ShapeDtypeStruct(gathered.shape, BF16), jax.ShapeDtypeStruct((toks, width), F32),
         jax.ShapeDtypeStruct((1, toks), F32), jax.ShapeDtypeStruct((8, 128), F32)],
        [pltpu.VMEM(hard_scores.shape, F32)], LIGHT,
    )(place, codes, hard_scores, log_total, *first, *second, gathered, queries)


def reduce_kernel(half, cap, groups, place_ref, lt_ref, *refs):
    ranks, rows, outs = refs[0:4], refs[4:8], refs[9:13]
    toks = lt_ref.shape[1]
    slots = groups * cap
    reps = lt_ref.shape[0]
    shape = (SIDE * slots, 4 * groups)
    group = iota(shape, 0) // cap % groups
    parts = (iota(shape, 1) % groups == group) & (iota(shape, 1) < 3 * groups)
    parts = parts.astype(BF16)
    log_rows = jnp.concatenate(
        [jnp.broadcast_to(own_row(lt_ref, source_of(place_ref, half, s)), (slots, toks))
         for s in range(SIDE)], axis=0
    )
    weights = []
    for line in range(SIDE):
        scores = mm(parts, rows[line][slots * SIDE :, : reps * cap])
        slot, lane = iota(scores.shape, 0), iota(scores.shape, 1)
        s = slot // slots
        block = s * SIDE + line if half == 0 else line * SIDE + s
        hs = jnp.sum(
            jnp.where(lane == block * cap + slot % cap, scores, 0.0), axis=1, keepdims=True
        )
        _, hit = hits_of(ranks[line][...], groups, cap)
        weights.append(jnp.where(hit, jnp.exp(hs - log_rows), 0.0).astype(BF16))
    for s in range(SIDE):
        values = [
            rows[line][(g * SIDE + s) * cap : (g * SIDE + s + 1) * cap, :]
            for line in range(SIDE) for g in range(groups)
        ]
        weight = jnp.concatenate([w[s * slots : (s + 1) * slots] for w in weights], axis=0)
        outs[s][...] = mm(weight, jnp.concatenate(values, axis=0), TN).astype(outs[s].dtype)


def reduce(place, half, log_total, ranks, rows, mark, groups, cap):
    toks = log_total.shape[1]
    shape = (toks, rows[0].shape[1])
    return call(
        functools.partial(reduce_kernel, half, cap, groups), "reduce", 1,
        [full(log_total.shape)] + [full(ranks[0].shape)] * 4 + [full(rows[0].shape)] * 4
        + [full(mark.shape)],
        [full(shape)] * 4,
        [jax.ShapeDtypeStruct(shape, F32)] + [jax.ShapeDtypeStruct(shape, BF16)] * 3, [], HEAVY,
    )(place, log_total, *ranks, *rows, mark)


def final_kernel(temper, place_ref, gq_ref, *refs):
    total = gq_ref[...]
    for ref in refs[0:SIDE]:
        total = total + ref[...].astype(F32)
    refs[-1][...] = (temper * total).astype(BF16)


def final(place, within, parts, half, temper, made=None):
    rows, half_width = parts[0].shape
    lanes = pl.BlockSpec((rows, half_width), lambda *_: (0, half))
    more = [] if made is None else [made]
    return pl.pallas_call(
        functools.partial(final_kernel, temper),
        grid_spec=pltpu.PrefetchScalarGridSpec(
            num_scalar_prefetch=1, grid=(1,),
            in_specs=[lanes] + [full((rows, half_width))] * SIDE + [ANY] * len(more),
            out_specs=lanes, scratch_shapes=[],
        ),
        out_shape=jax.ShapeDtypeStruct(within.shape, BF16),
        compiler_params=pltpu.CompilerParams(
            dimension_semantics=("arbitrary",), vmem_limit_bytes=VMEM_LIMIT
        ),
        input_output_aliases={2 + SIDE: 0} if more else {},
        cost_estimate=pl.CostEstimate(flops=LIGHT, bytes_accessed=1 << 16, transcendentals=0),
        name="final",
    )(place, within, *parts, *more)


def along(x, half, shift):
    pairs = []
    for i in range(SIDE * SIDE):
        a, b = i // SIDE, i % SIDE
        pairs.append((i, rep_of(a + shift, b) if half == 0 else rep_of(a, b + shift)))
    return lax.ppermute(x, "rep", pairs)


def shards(queries, passages, neg_device, neg_row):
    toks, width = queries.shape
    negs = neg_device.shape[1]
    groups = lax.axis_size("grp")
    reps = lax.axis_size("rep")
    cap = 8 * toks // (groups * reps)
    half_width = width // 2
    temper = 3.0 / math.sqrt(width)
    grp, rep = lax.axis_index("grp"), lax.axis_index("rep")
    place = jnp.stack([grp, rep // SIDE, rep % SIDE]).astype(I32)

    lines = jnp.pad(jnp.stack([neg_device.T, neg_row.T]), ((0, 0), (0, 8 - negs), (0, 0)))
    lines = jnp.pad(lines.reshape(16, toks), ((0, 0), (0, half_width - toks))).astype(BF16)
    sources = []
    for half in range(2):
        block = queries[:, half * half_width : (half + 1) * half_width]
        block = jnp.concatenate([block, lines], axis=0)
        sources.append([block] + [along(block, half, s) for s in range(1, SIDE)])
    gathered = lax.all_gather(passages, "grp", axis=0, tiled=True)

    first, second, ranks_first, ranks_second = ([None] * SIDE for _ in range(4))
    earlier = []
    for shift in (2, 1, 3, 0):
        one, two, ranks_first[shift], ranks_second[shift] = mid(
            place, shift, *sources, earlier, groups, reps, cap, negs
        )
        earlier = [ranks_first[shift]]
        first[shift] = along(one, 1, shift) if shift else one
        second[shift] = along(two, 0, shift) if shift else two

    within = inside(place, gathered, queries, temper)
    back_first, back_second, hard_scores, codes, part = hard(
        place, first, second, gathered, within, temper, reps, cap
    )
    parts = lax.all_to_all(part, "rep", split_axis=0, concat_axis=0, tiled=True)
    high = jnp.max(parts, axis=0)
    log_total = high + jnp.log(jnp.sum(jnp.exp(parts - high), axis=0))

    partial_sum, grad_inner, losses, mark = column(
        place, codes, hard_scores, log_total, first, second, gathered, queries, temper, cap
    )
    grad_passages = lax.psum_scatter(partial_sum, "grp", scatter_dimension=0, tiled=True)
    back_first = [along(v, 1, -s) if s else v for s, v in enumerate(back_first)]
    back_second = [along(v, 0, -s) if s else v for s, v in enumerate(back_second)]

    sums = []
    for half, ranks, rows in ((0, ranks_first, back_first), (1, ranks_second, back_second)):
        made = reduce(place, half, log_total, ranks, rows, mark, groups, cap)
        sums.append([along(v, half, -s) if s else v for s, v in enumerate(made)])
    grad_queries = final(place, grad_inner, sums[0], 0, temper)
    grad_queries = final(place, grad_inner, sums[1], 1, temper, grad_queries)
    return (losses.reshape(toks), grad_queries, grad_passages)


def solution(mesh):
    in_specs = (
        P(("grp", "rep"), None),
        P(("grp", "rep"), None),
        P(("grp", "rep"), None),
        P(("grp", "rep"), None),
    )
    out_specs = (P(("grp", "rep")), P(("grp", "rep"), None), P(("grp", "rep"), None))
    return jax.shard_map(shards, mesh=mesh, in_specs=in_specs, out_specs=out_specs, check_vma=False)
```

```python
import functools
import math

import jax
import jax.numpy as jnp
from jax import lax
from jax.experimental import pallas as pl
from jax.experimental.pallas import tpu as pltpu
from jax.sharding import PartitionSpec as P

F32 = jnp.float32
BF16 = jnp.bfloat16
I32 = jnp.int32
LOW = -1e30
NT = (((1,), (1,)), ((), ()))
TN = (((0,), (0,)), ((), ()))
NN = (((1,), (0,)), ((), ()))
VMEM_LIMIT = 63 * 1024 * 1024


def mm(a, b, dims=NN):
    return lax.dot_general(a, b, dims, preferred_element_type=F32)


def iota(shape, dim):
    return lax.broadcasted_iota(I32, shape, dim)


def split3(x):
    a = x.astype(BF16)
    rest = x - a.astype(F32)
    b = rest.astype(BF16)
    c = (rest - b.astype(F32)).astype(BF16)
    return jnp.concatenate([a, b, c], axis=0)


def full(shape):
    return pl.BlockSpec(shape, lambda *_: (0,) * len(shape))


def call(kernel, name, steps, ins, outs, shapes, scratch, weight):
    return pl.pallas_call(
        kernel,
        grid_spec=pltpu.PrefetchScalarGridSpec(
            num_scalar_prefetch=1, grid=(steps,), in_specs=ins, out_specs=outs,
            scratch_shapes=scratch,
        ),
        out_shape=shapes,
        compiler_params=pltpu.CompilerParams(
            dimension_semantics=("arbitrary",), vmem_limit_bytes=VMEM_LIMIT
        ),
        cost_estimate=pl.CostEstimate(flops=weight, bytes_accessed=1 << 16, transcendentals=0),
        name=name,
    )


ANY = pl.BlockSpec(memory_space=pl.ANY)
LIGHT, MIDDLE, HEAVY = 1 << 20, 1 << 20, 1 << 39
SIDE = 4
CORES = 2


def rep_of(x, y):
    return x % SIDE * SIDE + y % SIDE


def columns_of(place_ref, half, shift):
    x, y = place_ref[1], place_ref[2]
    return rep_of(x, y + shift) if half == 0 else rep_of(x + shift, y)


def source_of(place_ref, half, shift):
    x, y = place_ref[1], place_ref[2]
    return rep_of(x + SIDE - shift, y) if half == 0 else rep_of(x, y + SIDE - shift)


def hits_of(ranks, groups, cap):
    shape = (ranks.shape[0] * cap, ranks.shape[0])
    pick = (iota(shape, 1) == iota(shape, 0) // cap).astype(BF16)
    spread = mm(pick, ranks)
    return pick, spread == (iota(spread.shape, 0) % cap + 1).astype(F32)


def mid_kernel(shift, cap, groups, reps, negs, place_ref, *refs):
    sources = (refs[0:SIDE], refs[SIDE : 2 * SIDE])
    outs, ranks_out = refs[-4:-2], refs[-2:]
    rows, half_width = sources[0][0].shape
    toks = rows - 16
    slots = groups * cap
    before = (iota((toks, toks), 0) < iota((toks, toks), 1)).astype(BF16)
    for half in range(2):
        col = columns_of(place_ref, half, shift)
        dev = (iota((groups, toks), 0) * reps + col).astype(F32)
        named_all, rows_all = [], []
        for source in sources[half]:
            table = source[toks:, :toks].astype(F32)
            named = jnp.zeros((groups, toks), F32)
            wanted = jnp.zeros((groups, toks), F32)
            for k in range(negs):
                hit = dev == table[k : k + 1]
                named = named + jnp.where(hit, 1.0, 0.0)
                wanted = wanted + jnp.where(hit, table[8 + k : 9 + k] + 1.0, 0.0)
            named_all.append(named)
            rows_all.append(wanted)
        named = jnp.concatenate(named_all, axis=0)
        wanted = jnp.concatenate(rows_all, axis=0).astype(BF16)
        ranks = (named * (mm(named.astype(BF16), before) + 1.0)).astype(BF16)
        ranks_out[half][...] = ranks
        pick, hit = hits_of(ranks, groups, cap)
        hot = hit.astype(BF16)
        row = jnp.where(hit, mm(pick, wanted), 0.0).astype(BF16)
        ids = mm(jnp.ones((8, toks), BF16), row, NT)[0:1]
        tok = mm(iota((8, toks), 1).astype(F32).astype(BF16), hot, NT)[0:1]
        for s, source in enumerate(sources[half]):
            moved = mm(hot[s * slots : (s + 1) * slots], source[:toks, :]).astype(BF16)
            for g in range(groups):
                first = (g * SIDE + s) * cap
                outs[half][first : first + cap, :] = moved[g * cap : (g + 1) * cap]
        codes = [v[:, s * slots : (s + 1) * slots] for v in (ids, tok) for s in range(SIDE)]
        codes = jnp.concatenate(codes + [jnp.zeros((8, slots), F32)], axis=0)
        codes = jnp.concatenate([codes, jnp.zeros((16, half_width - slots), F32)], axis=1)
        outs[half][groups * SIDE * cap :, :] = codes.astype(BF16)


def mid(place, shift, first, second, earlier, groups, reps, cap, negs):
    rows, half_width = first[0].shape
    slots = jax.ShapeDtypeStruct((groups * SIDE * cap + 16, half_width), BF16)
    ranks = jax.ShapeDtypeStruct((SIDE * groups, rows - 16), BF16)
    return call(
        functools.partial(mid_kernel, shift, cap, groups, reps, negs), "mid", 1,
        [full((rows, half_width))] * (2 * SIDE) + [full(v.shape) for v in earlier],
        [full(slots.shape)] * 2 + [full(ranks.shape)] * 2,
        [slots, slots, ranks, ranks], [], LIGHT,
    )(place, *first, *second, *earlier)


def inside_kernel(temper, place_ref, p_ref, q_ref, out_ref, scores_ref, top, total):
    step = pl.program_id(0)

    @pl.when(step == 0)
    def _():
        top[...] = jnp.full(top.shape, LOW, F32)
        total[...] = jnp.zeros(total.shape, F32)

    scores = temper * mm(p_ref[...], q_ref[...], NT)
    scores_ref[...] = scores
    high = jnp.maximum(top[...], jnp.max(scores, axis=0, keepdims=True))
    total[...] = total[...] * jnp.exp(top[...] - high) + jnp.sum(
        jnp.exp(scores - high), axis=0, keepdims=True
    )
    top[...] = high

    @pl.when(step == pl.num_programs(0) - 1)
    def _():
        out_ref[...] = top[...] + jnp.log(total[...])


def inside(place, gathered, queries, temper):
    toks, width = queries.shape
    return call(
        functools.partial(inside_kernel, temper), "inside", 2,
        [pl.BlockSpec((gathered.shape[0] // 2, width), lambda s, _: (s, 0)), full((toks, width))],
        [full((1, toks)), pl.BlockSpec((gathered.shape[0] // 2, toks), lambda s, _: (s, 0))],
        [jax.ShapeDtypeStruct((1, toks), F32),
         jax.ShapeDtypeStruct((gathered.shape[0], toks), F32)],
        [pltpu.VMEM((1, toks), F32), pltpu.VMEM((1, toks), F32)], MIDDLE,
    )(place, gathered, queries)


def asking_rows(first, second, base, cap):
    def piece(ref, s):
        return ref[base + s * cap : base + (s + 1) * cap, :]

    pairs = [(dx, dy) for dx in range(SIDE) for dy in range(SIDE)]
    one = jnp.concatenate([piece(first[dy], dx) for dx, dy in pairs], axis=0)
    two = jnp.concatenate([piece(second[dx], dy) for dx, dy in pairs], axis=0)
    return one, two


def source_mask(place_ref, reps, cap):
    shape = (reps, reps * cap)
    dx = iota(shape, 1) // (SIDE * cap)
    dy = iota(shape, 1) // cap % SIDE
    x = (place_ref[1] + SIDE - dx) % SIDE
    y = (place_ref[2] + SIDE - dy) % SIDE
    return iota(shape, 0) == x * SIDE + y


def hard_kernel(reps, cap, temper, place_ref, *refs):
    first, second, exts = refs[0:4], refs[4:8], refs[8:12]
    p_ref, inside_ref = refs[12:14]
    out_first, out_second = refs[14:18], refs[18:22]
    hs_ref, code_ref, part_ref, top, total = refs[22:]
    step = pl.program_id(0)
    levels = pl.num_programs(0) - 1
    toks = inside_ref.shape[1]
    half_width = p_ref.shape[1] // 2
    slots = reps * cap
    groups = code_ref.shape[0] // 2
    source = source_mask(place_ref, reps, cap)

    @pl.when(step == 0)
    def _():
        top[...] = jnp.full(top.shape, LOW, F32)
        total[...] = jnp.zeros(total.shape, F32)
        table = jnp.concatenate([ext[...] for ext in exts], axis=0)[:, : groups * cap]
        shape = (groups * cap, groups * slots)
        lane, slot = iota(shape, 0), iota(shape, 1)
        to_slot = (lane == slot // slots * cap + slot % cap).astype(BF16)
        laid = mm(table, to_slot)
        row, slot = iota(laid.shape, 0), iota(laid.shape, 1) % slots
        dx, dy = slot // (SIDE * cap), slot // cap % SIDE
        want = dy * 16 + dx
        ids = jnp.sum(jnp.where(row == want, laid, 0.0), axis=0, keepdims=True).astype(I32)
        tok = jnp.sum(jnp.where(row == want + SIDE, laid, 0.0), axis=0, keepdims=True).astype(I32)
        for g in range(groups):
            code_ref[g : g + 1, :] = ids[:, g * slots : (g + 1) * slots]
            code_ref[groups + g : groups + g + 1, :] = tok[:, g * slots : (g + 1) * slots]

    @pl.when(step < levels)
    def _():
        values = []
        for core in range(CORES):
            group = CORES * step + core
            ids = code_ref[pl.ds(group, 1), :]
            tok = code_ref[pl.ds(groups + group, 1), :]
            valid = ids > 0
            base = core * SIDE * cap
            one, two = asking_rows(first, second, base, cap)
            passages = p_ref[core * toks : (core + 1) * toks, :]
            cross = mm(passages, jnp.concatenate([one, two], axis=1), NT)
            hit = iota((toks, slots), 0) + 1 == ids
            hs = temper * jnp.sum(jnp.where(hit, cross, 0.0), axis=0, keepdims=True)
            hs_ref[pl.ds(group, 1), :] = hs
            served = mm(hit.astype(BF16), passages, TN).astype(BF16)
            for dx in range(SIDE):
                for dy in range(SIDE):
                    at = (dx * SIDE + dy) * cap
                    out_first[dy][base + dx * cap : base + (dx + 1) * cap, :] = served[
                        at : at + cap, :half_width
                    ]
                    out_second[dx][base + dy * cap : base + (dy + 1) * cap, :] = served[
                        at : at + cap, half_width:
                    ]
            token = ((iota((toks, slots), 0) == tok) & valid).astype(BF16)
            live = source & valid
            parts = jnp.concatenate(
                [split3(jnp.where(live, hs, 0.0)), live.astype(BF16)], axis=0
            )
            laid = mm(parts, token, NT)
            there = laid[3 * reps :] > 0.5
            value = laid[:reps] + laid[reps : 2 * reps] + laid[2 * reps : 3 * reps]
            values.append((there, jnp.where(there, value, LOW)))
        high = top[...]
        for there, value in values:
            high = jnp.maximum(high, value)
        new = total[...] * jnp.exp(top[...] - high)
        for there, value in values:
            new = new + jnp.where(there, jnp.exp(value - high), 0.0)
        total[...] = new
        top[...] = high

    @pl.when(step == levels)
    def _():
        part = jnp.where(total[...] > 0.0, top[...] + jnp.log(total[...]), LOW)
        within = inside_ref[...]
        high = jnp.maximum(part, within)
        both = high + jnp.log(jnp.exp(part - high) + jnp.exp(within - high))
        own = iota(part.shape, 0) == rep_of(place_ref[1], place_ref[2])
        part_ref[...] = jnp.broadcast_to(jnp.where(own, both, part)[None], part_ref.shape)
        pieces = split3(hs_ref[...]).astype(F32)
        pieces = jnp.concatenate([pieces, jnp.zeros((groups, slots), F32)], axis=0)
        pieces = jnp.concatenate(
            [pieces, jnp.zeros((4 * groups, half_width - slots), F32)], axis=1
        ).astype(BF16)
        for out in (*out_first, *out_second):
            out[: 4 * groups, :] = pieces


def hard(place, first, second, gathered, within, temper, reps, cap):
    rows, half_width = first[0].shape
    toks = within.shape[1]
    groups = gathered.shape[0] // toks
    levels = groups // CORES
    slots = reps * cap
    per = CORES * SIDE * cap
    ins = pl.BlockSpec((per, half_width), lambda s, _: (lax.min(s, levels - 1), 0))
    outs = pl.BlockSpec((per, half_width), lambda s, _: (s, 0))
    ext = pl.BlockSpec((16, half_width), lambda s, _: (groups * SIDE * cap // 16, 0))
    made = call(
        functools.partial(hard_kernel, reps, cap, temper), "hard", levels + 1,
        [ins] * 8 + [ext] * 4
        + [pl.BlockSpec((CORES * toks, CORES * half_width),
                        lambda s, _: (lax.min(s, levels - 1), 0)), full((1, toks))],
        [outs] * 8 + [full((groups, slots)), full((2 * groups, slots)), full((reps, reps, toks))],
        [jax.ShapeDtypeStruct((groups * SIDE * cap + 4 * groups, half_width), BF16)] * 8
        + [jax.ShapeDtypeStruct((groups, slots), F32),
           jax.ShapeDtypeStruct((2 * groups, slots), I32),
           jax.ShapeDtypeStruct((reps, reps, toks), F32)],
        [pltpu.VMEM((reps, toks), F32), pltpu.VMEM((reps, toks), F32)], LIGHT,
    )(place, *first, *second, *first, gathered, within)
    return made[0:4], made[4:8], made[8], made[9], made[10]


def own_row(lt_ref, rep):
    lt = lt_ref[...]
    return jnp.sum(jnp.where(iota(lt.shape, 0) == rep, lt, 0.0), axis=0, keepdims=True)


def column_kernel(reps, cap, temper, place_ref, code_ref, hs_ref, lt_ref, *refs):
    first, second = refs[0:4], refs[4:8]
    p_ref, q_ref, scores_ref, gp_ref, gq_ref, loss_ref, mark_ref, d_ref = refs[8:]
    step = pl.program_id(0)
    toks, width = q_ref.shape
    slots = reps * cap
    groups = code_ref.shape[0] // 2

    @pl.when(step == 0)
    def _():
        log_parts = split3(lt_ref[...])
        source = source_mask(place_ref, reps, cap)
        rows = []
        for g in range(groups):
            valid = code_ref[g : g + 1, :] > 0
            tok = code_ref[groups + g : groups + g + 1, :]
            token = ((iota((toks, slots), 0) == tok) & valid).astype(BF16)
            found = mm(log_parts, token)
            found = found[:reps] + found[reps : 2 * reps] + found[2 * reps :]
            log_slot = jnp.sum(jnp.where(source, found, 0.0), axis=0, keepdims=True)
            rows.append(jnp.where(valid, jnp.exp(hs_ref[g : g + 1, :] - log_slot), 0.0))
        d_ref[...] = jnp.concatenate(rows, axis=0)
        mark_ref[...] = jnp.zeros(mark_ref.shape, F32)
        loss_ref[...] = own_row(lt_ref, rep_of(place_ref[1], place_ref[2]))

    queries = q_ref[...]
    passages = p_ref[...]
    lt_own = own_row(lt_ref, rep_of(place_ref[1], place_ref[2]))
    scores = scores_ref[...]
    row = iota(scores.shape, 0) + CORES * toks * step - toks * place_ref[0]
    eye = row == iota(scores.shape, 1)
    d_scores = (jnp.exp(scores - lt_own) - jnp.where(eye, 1.0, 0.0)).astype(BF16)
    loss_ref[...] -= jnp.sum(jnp.where(eye, scores, 0.0), axis=0, keepdims=True)
    for core in range(CORES):
        group = CORES * step + core
        here = slice(core * toks, (core + 1) * toks)
        ids = code_ref[pl.ds(group, 1), :]
        d_hard = d_ref[pl.ds(group, 1), :]
        hot = jnp.where(iota((toks, slots), 0) + 1 == ids, d_hard, 0.0).astype(BF16)
        both = jnp.concatenate([hot, d_scores[here]], axis=1)
        one, two = asking_rows(first, second, core * SIDE * cap, cap)
        rows = jnp.concatenate([jnp.concatenate([one, two], axis=1), queries], axis=0)
        gp_ref[here, :] = (temper * mm(both, rows)).astype(BF16)
    new = mm(d_scores, passages, TN)

    @pl.when(step == 0)
    def _():
        gq_ref[...] = new

    @pl.when(step > 0)
    def _():
        gq_ref[...] += new


def column(place, codes, hard_scores, log_total, first, second, gathered, queries, scores, temper,
           cap):
    reps = log_total.shape[0]
    toks, width = queries.shape
    slots = pl.BlockSpec((CORES * SIDE * cap, width // 2), lambda s, _: (s, 0))
    block = pl.BlockSpec((CORES * toks, width), lambda s, _: (s, 0))
    return call(
        functools.partial(column_kernel, reps, cap, temper), "column",
        gathered.shape[0] // (CORES * toks),
        [full(codes.shape), full(hard_scores.shape), full(log_total.shape)] + [slots] * 8
        + [block, full((toks, width)),
           pl.BlockSpec((CORES * toks, toks), lambda s, _: (s, 0))],
        [block, full((toks, width)), full((1, toks)), full((8, 128))],
        [jax.ShapeDtypeStruct(gathered.shape, BF16), jax.ShapeDtypeStruct((toks, width), F32),
         jax.ShapeDtypeStruct((1, toks), F32), jax.ShapeDtypeStruct((8, 128), F32)],
        [pltpu.VMEM(hard_scores.shape, F32)], LIGHT,
    )(place, codes, hard_scores, log_total, *first, *second, gathered, queries, scores)


def reduce_kernel(half, cap, groups, place_ref, lt_ref, *refs):
    ranks, rows, outs = refs[0:4], refs[4:8], refs[9:13]
    toks = lt_ref.shape[1]
    slots = groups * cap
    reps = lt_ref.shape[0]
    shape = (SIDE * slots, 4 * groups)
    group = iota(shape, 0) // cap % groups
    parts = (iota(shape, 1) % groups == group) & (iota(shape, 1) < 3 * groups)
    parts = parts.astype(BF16)
    log_rows = jnp.concatenate(
        [jnp.broadcast_to(own_row(lt_ref, source_of(place_ref, half, s)), (slots, toks))
         for s in range(SIDE)], axis=0
    )
    weights = []
    for line in range(SIDE):
        scores = mm(parts, rows[line][slots * SIDE :, : reps * cap])
        slot, lane = iota(scores.shape, 0), iota(scores.shape, 1)
        s = slot // slots
        block = s * SIDE + line if half == 0 else line * SIDE + s
        hs = jnp.sum(
            jnp.where(lane == block * cap + slot % cap, scores, 0.0), axis=1, keepdims=True
        )
        _, hit = hits_of(ranks[line][...], groups, cap)
        weights.append(jnp.where(hit, jnp.exp(hs - log_rows), 0.0).astype(BF16))
    for s in range(SIDE):
        values = [
            rows[line][(g * SIDE + s) * cap : (g * SIDE + s + 1) * cap, :]
            for line in range(SIDE) for g in range(groups)
        ]
        weight = jnp.concatenate([w[s * slots : (s + 1) * slots] for w in weights], axis=0)
        outs[s][...] = mm(weight, jnp.concatenate(values, axis=0), TN).astype(outs[s].dtype)


def reduce(place, half, log_total, ranks, rows, mark, groups, cap):
    toks = log_total.shape[1]
    shape = (toks, rows[0].shape[1])
    return call(
        functools.partial(reduce_kernel, half, cap, groups), "reduce", 1,
        [full(log_total.shape)] + [full(ranks[0].shape)] * 4 + [full(rows[0].shape)] * 4
        + [full(mark.shape)],
        [full(shape)] * 4,
        [jax.ShapeDtypeStruct(shape, F32)] + [jax.ShapeDtypeStruct(shape, BF16)] * 3, [], HEAVY,
    )(place, log_total, *ranks, *rows, mark)


def final_kernel(temper, place_ref, gq_ref, *refs):
    total = gq_ref[...]
    for ref in refs[0:SIDE]:
        total = total + ref[...].astype(F32)
    refs[-1][...] = (temper * total).astype(BF16)


def final(place, within, parts, half, temper, made=None):
    rows, half_width = parts[0].shape
    lanes = pl.BlockSpec((rows, half_width), lambda *_: (0, half))
    more = [] if made is None else [made]
    return pl.pallas_call(
        functools.partial(final_kernel, temper),
        grid_spec=pltpu.PrefetchScalarGridSpec(
            num_scalar_prefetch=1, grid=(1,),
            in_specs=[lanes] + [full((rows, half_width))] * SIDE + [ANY] * len(more),
            out_specs=lanes, scratch_shapes=[],
        ),
        out_shape=jax.ShapeDtypeStruct(within.shape, BF16),
        compiler_params=pltpu.CompilerParams(
            dimension_semantics=("arbitrary",), vmem_limit_bytes=VMEM_LIMIT
        ),
        input_output_aliases={2 + SIDE: 0} if more else {},
        cost_estimate=pl.CostEstimate(flops=LIGHT, bytes_accessed=1 << 16, transcendentals=0),
        name="final",
    )(place, within, *parts, *more)


def along(x, half, shift):
    pairs = []
    for i in range(SIDE * SIDE):
        a, b = i // SIDE, i % SIDE
        pairs.append((i, rep_of(a + shift, b) if half == 0 else rep_of(a, b + shift)))
    return lax.ppermute(x, "rep", pairs)


def shards(queries, passages, neg_device, neg_row):
    toks, width = queries.shape
    negs = neg_device.shape[1]
    groups = lax.axis_size("grp")
    reps = lax.axis_size("rep")
    cap = 8 * toks // (groups * reps)
    half_width = width // 2
    temper = 3.0 / math.sqrt(width)
    grp, rep = lax.axis_index("grp"), lax.axis_index("rep")
    place = jnp.stack([grp, rep // SIDE, rep % SIDE]).astype(I32)

    lines = jnp.pad(jnp.stack([neg_device.T, neg_row.T]), ((0, 0), (0, 8 - negs), (0, 0)))
    lines = jnp.pad(lines.reshape(16, toks), ((0, 0), (0, half_width - toks))).astype(BF16)
    sources = []
    for half in range(2):
        block = queries[:, half * half_width : (half + 1) * half_width]
        block = jnp.concatenate([block, lines], axis=0)
        sources.append([block] + [along(block, half, s) for s in range(1, SIDE)])
    gathered = lax.all_gather(passages, "grp", axis=0, tiled=True)

    first, second, ranks_first, ranks_second = ([None] * SIDE for _ in range(4))
    earlier = []
    for shift in (2, 1, 3, 0):
        one, two, ranks_first[shift], ranks_second[shift] = mid(
            place, shift, *sources, earlier, groups, reps, cap, negs
        )
        earlier = [ranks_first[shift]]
        first[shift] = along(one, 1, shift) if shift else one
        second[shift] = along(two, 0, shift) if shift else two

    within, scores = inside(place, gathered, queries, temper)
    back_first, back_second, hard_scores, codes, part = hard(
        place, first, second, gathered, within, temper, reps, cap
    )
    parts = lax.all_to_all(part, "rep", split_axis=0, concat_axis=0, tiled=True)
    high = jnp.max(parts, axis=0)
    log_total = high + jnp.log(jnp.sum(jnp.exp(parts - high), axis=0))

    partial_sum, grad_inner, losses, mark = column(
        place, codes, hard_scores, log_total, first, second, gathered, queries, scores, temper, cap
    )
    grad_passages = lax.psum_scatter(partial_sum, "grp", scatter_dimension=0, tiled=True)
    back_first = [along(v, 1, -s) if s else v for s, v in enumerate(back_first)]
    back_second = [along(v, 0, -s) if s else v for s, v in enumerate(back_second)]

    sums = []
    for half, ranks, rows in ((0, ranks_first, back_first), (1, ranks_second, back_second)):
        made = reduce(place, half, log_total, ranks, rows, mark, groups, cap)
        sums.append([along(v, half, -s) if s else v for s, v in enumerate(made)])
    grad_queries = final(place, grad_inner, sums[0], 0, temper)
    grad_queries = final(place, grad_inner, sums[1], 1, temper, grad_queries)
    return (losses.reshape(toks), grad_queries, grad_passages)


def solution(mesh):
    in_specs = (
        P(("grp", "rep"), None),
        P(("grp", "rep"), None),
        P(("grp", "rep"), None),
        P(("grp", "rep"), None),
    )
    out_specs = (P(("grp", "rep")), P(("grp", "rep"), None), P(("grp", "rep"), None))
    return jax.shard_map(shards, mesh=mesh, in_specs=in_specs, out_specs=out_specs, check_vma=False)
```

```python
import functools
import math

import jax
import jax.numpy as jnp
from jax import lax
from jax.experimental import pallas as pl
from jax.experimental.pallas import tpu as pltpu
from jax.sharding import PartitionSpec as P

F32 = jnp.float32
BF16 = jnp.bfloat16
I32 = jnp.int32
LOW = -1e30
NT = (((1,), (1,)), ((), ()))
TN = (((0,), (0,)), ((), ()))
NN = (((1,), (0,)), ((), ()))
VMEM_LIMIT = 63 * 1024 * 1024


def mm(a, b, dims=NN):
    return lax.dot_general(a, b, dims, preferred_element_type=F32)


def iota(shape, dim):
    return lax.broadcasted_iota(I32, shape, dim)


def split3(x):
    a = x.astype(BF16)
    rest = x - a.astype(F32)
    b = rest.astype(BF16)
    c = (rest - b.astype(F32)).astype(BF16)
    return jnp.concatenate([a, b, c], axis=0)


def full(shape):
    return pl.BlockSpec(shape, lambda *_: (0,) * len(shape))


def call(kernel, name, steps, ins, outs, shapes, scratch, weight):
    return pl.pallas_call(
        kernel,
        grid_spec=pltpu.PrefetchScalarGridSpec(
            num_scalar_prefetch=1, grid=(steps,), in_specs=ins, out_specs=outs,
            scratch_shapes=scratch,
        ),
        out_shape=shapes,
        compiler_params=pltpu.CompilerParams(
            dimension_semantics=("arbitrary",), vmem_limit_bytes=VMEM_LIMIT
        ),
        cost_estimate=pl.CostEstimate(flops=weight, bytes_accessed=1 << 16, transcendentals=0),
        name=name,
    )


ANY = pl.BlockSpec(memory_space=pl.ANY)
LIGHT, MIDDLE, HEAVY = 1 << 20, 1 << 20, 1 << 39
SIDE = 4
CORES = 2


def rep_of(x, y):
    return x % SIDE * SIDE + y % SIDE


def columns_of(place_ref, half, shift):
    x, y = place_ref[1], place_ref[2]
    return rep_of(x, y + shift) if half == 0 else rep_of(x + shift, y)


def source_of(place_ref, half, shift):
    x, y = place_ref[1], place_ref[2]
    return rep_of(x + SIDE - shift, y) if half == 0 else rep_of(x, y + SIDE - shift)


def hits_of(ranks, groups, cap):
    shape = (ranks.shape[0] * cap, ranks.shape[0])
    pick = (iota(shape, 1) == iota(shape, 0) // cap).astype(BF16)
    spread = mm(pick, ranks)
    return pick, spread == (iota(spread.shape, 0) % cap + 1).astype(F32)


def mid_kernel(shift, cap, groups, reps, negs, place_ref, *refs):
    sources = (refs[0:SIDE], refs[SIDE : 2 * SIDE])
    outs, ranks_out = refs[-4:-2], refs[-2:]
    rows, half_width = sources[0][0].shape
    toks = rows - 16
    slots = groups * cap
    before = (iota((toks, toks), 0) < iota((toks, toks), 1)).astype(BF16)
    for half in range(2):
        col = columns_of(place_ref, half, shift)
        dev = (iota((groups, toks), 0) * reps + col).astype(F32)
        named_all, rows_all = [], []
        for source in sources[half]:
            table = source[toks:, :toks].astype(F32)
            named = jnp.zeros((groups, toks), F32)
            wanted = jnp.zeros((groups, toks), F32)
            for k in range(negs):
                hit = dev == table[k : k + 1]
                named = named + jnp.where(hit, 1.0, 0.0)
                wanted = wanted + jnp.where(hit, table[8 + k : 9 + k] + 1.0, 0.0)
            named_all.append(named)
            rows_all.append(wanted)
        named = jnp.concatenate(named_all, axis=0)
        wanted = jnp.concatenate(rows_all, axis=0).astype(BF16)
        ranks = (named * (mm(named.astype(BF16), before) + 1.0)).astype(BF16)
        ranks_out[half][...] = ranks
        pick, hit = hits_of(ranks, groups, cap)
        hot = hit.astype(BF16)
        row = jnp.where(hit, mm(pick, wanted), 0.0).astype(BF16)
        ids = mm(jnp.ones((8, toks), BF16), row, NT)[0:1]
        tok = mm(iota((8, toks), 1).astype(F32).astype(BF16), hot, NT)[0:1]
        for s, source in enumerate(sources[half]):
            moved = mm(hot[s * slots : (s + 1) * slots], source[:toks, :]).astype(BF16)
            for g in range(groups):
                first = (g * SIDE + s) * cap
                outs[half][first : first + cap, :] = moved[g * cap : (g + 1) * cap]
        codes = [v[:, s * slots : (s + 1) * slots] for v in (ids, tok) for s in range(SIDE)]
        codes = jnp.concatenate(codes + [jnp.zeros((8, slots), F32)], axis=0)
        codes = jnp.concatenate([codes, jnp.zeros((16, half_width - slots), F32)], axis=1)
        outs[half][groups * SIDE * cap :, :] = codes.astype(BF16)


def mid(place, shift, first, second, earlier, groups, reps, cap, negs):
    rows, half_width = first[0].shape
    slots = jax.ShapeDtypeStruct((groups * SIDE * cap + 16, half_width), BF16)
    ranks = jax.ShapeDtypeStruct((SIDE * groups, rows - 16), BF16)
    return call(
        functools.partial(mid_kernel, shift, cap, groups, reps, negs), "mid", 1,
        [full((rows, half_width))] * (2 * SIDE) + [full(v.shape) for v in earlier],
        [full(slots.shape)] * 2 + [full(ranks.shape)] * 2,
        [slots, slots, ranks, ranks], [], LIGHT,
    )(place, *first, *second, *earlier)


def inside_kernel(temper, place_ref, p_ref, q_ref, out_ref, scores_ref, top, total):
    step = pl.program_id(0)

    @pl.when(step == 0)
    def _():
        top[...] = jnp.full(top.shape, LOW, F32)
        total[...] = jnp.zeros(total.shape, F32)

    scores = temper * mm(p_ref[...], q_ref[...], NT)
    scores_ref[...] = scores
    high = jnp.maximum(top[...], jnp.max(scores, axis=0, keepdims=True))
    total[...] = total[...] * jnp.exp(top[...] - high) + jnp.sum(
        jnp.exp(scores - high), axis=0, keepdims=True
    )
    top[...] = high

    @pl.when(step == pl.num_programs(0) - 1)
    def _():
        out_ref[...] = top[...] + jnp.log(total[...])


def inside(place, gathered, queries, temper):
    toks, width = queries.shape
    return call(
        functools.partial(inside_kernel, temper), "inside", 2,
        [pl.BlockSpec((gathered.shape[0] // 2, width), lambda s, _: (s, 0)), full((toks, width))],
        [full((1, toks)), pl.BlockSpec((gathered.shape[0] // 2, toks), lambda s, _: (s, 0))],
        [jax.ShapeDtypeStruct((1, toks), F32),
         jax.ShapeDtypeStruct((gathered.shape[0], toks), F32)],
        [pltpu.VMEM((1, toks), F32), pltpu.VMEM((1, toks), F32)], MIDDLE,
    )(place, gathered, queries)


def asking_rows(first, second, base, cap):
    def piece(ref, s):
        return ref[base + s * cap : base + (s + 1) * cap, :]

    pairs = [(dx, dy) for dx in range(SIDE) for dy in range(SIDE)]
    one = jnp.concatenate([piece(first[dy], dx) for dx, dy in pairs], axis=0)
    two = jnp.concatenate([piece(second[dx], dy) for dx, dy in pairs], axis=0)
    return one, two


def source_mask(place_ref, reps, cap):
    shape = (reps, reps * cap)
    dx = iota(shape, 1) // (SIDE * cap)
    dy = iota(shape, 1) // cap % SIDE
    x = (place_ref[1] + SIDE - dx) % SIDE
    y = (place_ref[2] + SIDE - dy) % SIDE
    return iota(shape, 0) == x * SIDE + y


def hard_kernel(reps, cap, temper, place_ref, *refs):
    first, second, exts = refs[0:4], refs[4:8], refs[8:12]
    p_ref, inside_ref = refs[12:14]
    out_first, out_second = refs[14:18], refs[18:22]
    hs_ref, code_ref, part_ref, top, total = refs[22:]
    step = pl.program_id(0)
    levels = pl.num_programs(0) - 1
    toks = inside_ref.shape[1]
    half_width = p_ref.shape[1] // 2
    slots = reps * cap
    groups = code_ref.shape[0] // 2
    source = source_mask(place_ref, reps, cap)

    @pl.when(step == 0)
    def _():
        top[...] = jnp.full(top.shape, LOW, F32)
        total[...] = jnp.zeros(total.shape, F32)
        table = jnp.concatenate([ext[...] for ext in exts], axis=0)[:, : groups * cap]
        shape = (groups * cap, groups * slots)
        lane, slot = iota(shape, 0), iota(shape, 1)
        to_slot = (lane == slot // slots * cap + slot % cap).astype(BF16)
        laid = mm(table, to_slot)
        row, slot = iota(laid.shape, 0), iota(laid.shape, 1) % slots
        dx, dy = slot // (SIDE * cap), slot // cap % SIDE
        want = dy * 16 + dx
        ids = jnp.sum(jnp.where(row == want, laid, 0.0), axis=0, keepdims=True).astype(I32)
        tok = jnp.sum(jnp.where(row == want + SIDE, laid, 0.0), axis=0, keepdims=True).astype(I32)
        for g in range(groups):
            code_ref[g : g + 1, :] = ids[:, g * slots : (g + 1) * slots]
            code_ref[groups + g : groups + g + 1, :] = tok[:, g * slots : (g + 1) * slots]

    @pl.when(step < levels)
    def _():
        values = []
        for core in range(CORES):
            group = CORES * step + core
            ids = code_ref[pl.ds(group, 1), :]
            tok = code_ref[pl.ds(groups + group, 1), :]
            valid = ids > 0
            base = core * SIDE * cap
            one, two = asking_rows(first, second, base, cap)
            passages = p_ref[core * toks : (core + 1) * toks, :]
            cross = mm(passages, jnp.concatenate([one, two], axis=1), NT)
            hit = iota((toks, slots), 0) + 1 == ids
            hs = temper * jnp.sum(jnp.where(hit, cross, 0.0), axis=0, keepdims=True)
            hs_ref[pl.ds(group, 1), :] = hs
            served = mm(hit.astype(BF16), passages, TN).astype(BF16)
            for dx in range(SIDE):
                for dy in range(SIDE):
                    at = (dx * SIDE + dy) * cap
                    out_first[dy][base + dx * cap : base + (dx + 1) * cap, :] = served[
                        at : at + cap, :half_width
                    ]
                    out_second[dx][base + dy * cap : base + (dy + 1) * cap, :] = served[
                        at : at + cap, half_width:
                    ]
            token = ((iota((toks, slots), 0) == tok) & valid).astype(BF16)
            live = source & valid
            parts = jnp.concatenate(
                [split3(jnp.where(live, hs, 0.0)), live.astype(BF16)], axis=0
            )
            laid = mm(parts, token, NT)
            there = laid[3 * reps :] > 0.5
            value = laid[:reps] + laid[reps : 2 * reps] + laid[2 * reps : 3 * reps]
            values.append((there, jnp.where(there, value, LOW)))
        high = top[...]
        for there, value in values:
            high = jnp.maximum(high, value)
        new = total[...] * jnp.exp(top[...] - high)
        for there, value in values:
            new = new + jnp.where(there, jnp.exp(value - high), 0.0)
        total[...] = new
        top[...] = high

    @pl.when(step == levels)
    def _():
        part = jnp.where(total[...] > 0.0, top[...] + jnp.log(total[...]), LOW)
        within = inside_ref[...]
        high = jnp.maximum(part, within)
        both = high + jnp.log(jnp.exp(part - high) + jnp.exp(within - high))
        own = iota(part.shape, 0) == rep_of(place_ref[1], place_ref[2])
        part_ref[...] = jnp.broadcast_to(jnp.where(own, both, part)[None], part_ref.shape)
        pieces = split3(hs_ref[...]).astype(F32)
        pieces = jnp.concatenate([pieces, jnp.zeros((groups, slots), F32)], axis=0)
        pieces = jnp.concatenate(
            [pieces, jnp.zeros((4 * groups, half_width - slots), F32)], axis=1
        ).astype(BF16)
        for out in (*out_first, *out_second):
            out[: 4 * groups, :] = pieces


def hard(place, first, second, gathered, within, temper, reps, cap):
    rows, half_width = first[0].shape
    toks = within.shape[1]
    groups = gathered.shape[0] // toks
    levels = groups // CORES
    slots = reps * cap
    per = CORES * SIDE * cap
    ins = pl.BlockSpec((per, half_width), lambda s, _: (lax.min(s, levels - 1), 0))
    outs = pl.BlockSpec((per, half_width), lambda s, _: (s, 0))
    ext = pl.BlockSpec((16, half_width), lambda s, _: (groups * SIDE * cap // 16, 0))
    made = call(
        functools.partial(hard_kernel, reps, cap, temper), "hard", levels + 1,
        [ins] * 8 + [ext] * 4
        + [pl.BlockSpec((CORES * toks, CORES * half_width),
                        lambda s, _: (lax.min(s, levels - 1), 0)), full((1, toks))],
        [outs] * 8 + [full((groups, slots)), full((2 * groups, slots)), full((reps, reps, toks))],
        [jax.ShapeDtypeStruct((groups * SIDE * cap + 4 * groups, half_width), BF16)] * 8
        + [jax.ShapeDtypeStruct((groups, slots), F32),
           jax.ShapeDtypeStruct((2 * groups, slots), I32),
           jax.ShapeDtypeStruct((reps, reps, toks), F32)],
        [pltpu.VMEM((reps, toks), F32), pltpu.VMEM((reps, toks), F32)], LIGHT,
    )(place, *first, *second, *first, gathered, within)
    return made[0:4], made[4:8], made[8], made[9], made[10]


def own_row(lt_ref, rep):
    lt = lt_ref[...]
    return jnp.sum(jnp.where(iota(lt.shape, 0) == rep, lt, 0.0), axis=0, keepdims=True)


def column_kernel(reps, cap, temper, place_ref, code_ref, hs_ref, lt_ref, *refs):
    first, second = refs[0:4], refs[4:8]
    p_ref, q_ref, scores_ref, gp_ref, gq_ref, loss_ref, mark_ref, d_ref = refs[8:]
    step = pl.program_id(0)
    toks, width = q_ref.shape
    slots = reps * cap
    groups = code_ref.shape[0] // 2

    @pl.when(step == 0)
    def _():
        log_parts = split3(lt_ref[...])
        source = source_mask(place_ref, reps, cap)
        rows = []
        for g in range(groups):
            valid = code_ref[g : g + 1, :] > 0
            tok = code_ref[groups + g : groups + g + 1, :]
            token = ((iota((toks, slots), 0) == tok) & valid).astype(BF16)
            found = mm(log_parts, token)
            found = found[:reps] + found[reps : 2 * reps] + found[2 * reps :]
            log_slot = jnp.sum(jnp.where(source, found, 0.0), axis=0, keepdims=True)
            rows.append(jnp.where(valid, jnp.exp(hs_ref[g : g + 1, :] - log_slot), 0.0))
        d_ref[...] = jnp.concatenate(rows, axis=0)
        mark_ref[...] = jnp.zeros(mark_ref.shape, F32)
        loss_ref[...] = own_row(lt_ref, rep_of(place_ref[1], place_ref[2]))

    queries = q_ref[...]
    passages = p_ref[...]
    lt_own = own_row(lt_ref, rep_of(place_ref[1], place_ref[2]))
    scores = scores_ref[...]
    row = iota(scores.shape, 0) + CORES * toks * step - toks * place_ref[0]
    eye = row == iota(scores.shape, 1)
    d_scores = (jnp.exp(scores - lt_own) - jnp.where(eye, 1.0, 0.0)).astype(BF16)
    loss_ref[...] -= jnp.sum(jnp.where(eye, scores, 0.0), axis=0, keepdims=True)
    for core in range(CORES):
        group = CORES * step + core
        here = slice(core * toks, (core + 1) * toks)
        ids = code_ref[pl.ds(group, 1), :]
        d_hard = d_ref[pl.ds(group, 1), :]
        hot = jnp.where(iota((toks, slots), 0) + 1 == ids, d_hard, 0.0).astype(BF16)
        both = jnp.concatenate([hot, d_scores[here]], axis=1)
        one, two = asking_rows(first, second, core * SIDE * cap, cap)
        rows = jnp.concatenate([jnp.concatenate([one, two], axis=1), queries], axis=0)
        gp_ref[here, :] = (temper * mm(both, rows)).astype(BF16)
    new = mm(d_scores, passages, TN)

    @pl.when(step == 0)
    def _():
        gq_ref[...] = new

    @pl.when(step > 0)
    def _():
        gq_ref[...] += new


def column(place, codes, hard_scores, log_total, first, second, gathered, queries, scores, temper,
           cap):
    reps = log_total.shape[0]
    toks, width = queries.shape
    slots = pl.BlockSpec((CORES * SIDE * cap, width // 2), lambda s, _: (s, 0))
    block = pl.BlockSpec((CORES * toks, width), lambda s, _: (s, 0))
    return call(
        functools.partial(column_kernel, reps, cap, temper), "column",
        gathered.shape[0] // (CORES * toks),
        [full(codes.shape), full(hard_scores.shape), full(log_total.shape)] + [slots] * 8
        + [block, full((toks, width)),
           pl.BlockSpec((CORES * toks, toks), lambda s, _: (s, 0))],
        [block, full((toks, width)), full((1, toks)), full((8, 128))],
        [jax.ShapeDtypeStruct(gathered.shape, BF16), jax.ShapeDtypeStruct((toks, width), F32),
         jax.ShapeDtypeStruct((1, toks), F32), jax.ShapeDtypeStruct((8, 128), F32)],
        [pltpu.VMEM(hard_scores.shape, F32)], LIGHT,
    )(place, codes, hard_scores, log_total, *first, *second, gathered, queries, scores)


def reduce_kernel(half, cap, groups, place_ref, lt_ref, *refs):
    ranks, rows, outs, weight_ref = refs[0:4], refs[4:8], refs[9:13], refs[13]
    toks = lt_ref.shape[1]
    slots = groups * cap
    reps = lt_ref.shape[0]
    @pl.when(pl.program_id(0) == 0)
    def _():
        shape = (SIDE * slots, 4 * groups)
        group = iota(shape, 0) // cap % groups
        parts = (iota(shape, 1) % groups == group) & (iota(shape, 1) < 3 * groups)
        parts = parts.astype(BF16)
        log_rows = jnp.concatenate(
            [jnp.broadcast_to(own_row(lt_ref, source_of(place_ref, half, s)), (slots, toks))
             for s in range(SIDE)], axis=0
        )
        for line in range(SIDE):
            scores = mm(parts, rows[line][slots * SIDE :, : reps * cap])
            slot, lane = iota(scores.shape, 0), iota(scores.shape, 1)
            s = slot // slots
            block = s * SIDE + line if half == 0 else line * SIDE + s
            hs = jnp.sum(
                jnp.where(lane == block * cap + slot % cap, scores, 0.0), axis=1, keepdims=True
            )
            _, hit = hits_of(ranks[line][...], groups, cap)
            weight_ref[line] = jnp.where(hit, jnp.exp(hs - log_rows), 0.0).astype(BF16)

    for s in range(SIDE):
        values = [
            rows[line][(g * SIDE + s) * cap : (g * SIDE + s + 1) * cap, :]
            for line in range(SIDE) for g in range(groups)
        ]
        weight = jnp.concatenate(
            [weight_ref[line, s * slots : (s + 1) * slots, :] for line in range(SIDE)], axis=0
        )
        outs[s][...] = mm(weight, jnp.concatenate(values, axis=0), TN).astype(outs[s].dtype)


def reduce(place, half, log_total, ranks, rows, mark, groups, cap):
    toks = log_total.shape[1]
    shape = (toks, rows[0].shape[1])
    return call(
        functools.partial(reduce_kernel, half, cap, groups), "reduce", 2,
        [full(log_total.shape)] + [full(ranks[0].shape)] * 4 + [pl.BlockSpec((rows[0].shape[0], shape[1] // 2), lambda s, _: (0, s))] * 4
        + [full(mark.shape)],
        [pl.BlockSpec((toks, shape[1] // 2), lambda s, _: (0, s))] * 4,
        [jax.ShapeDtypeStruct(shape, F32)] + [jax.ShapeDtypeStruct(shape, BF16)] * 3,
        [pltpu.VMEM((SIDE, SIDE * groups * cap, toks), BF16)], HEAVY,
    )(place, log_total, *ranks, *rows, mark)


def final_kernel(temper, place_ref, gq_ref, *refs):
    total = gq_ref[...]
    for ref in refs[0:SIDE]:
        total = total + ref[...].astype(F32)
    refs[-1][...] = (temper * total).astype(BF16)


def final(place, within, parts, half, temper, made=None):
    rows, half_width = parts[0].shape
    lanes = pl.BlockSpec((rows, half_width), lambda *_: (0, half))
    more = [] if made is None else [made]
    return pl.pallas_call(
        functools.partial(final_kernel, temper),
        grid_spec=pltpu.PrefetchScalarGridSpec(
            num_scalar_prefetch=1, grid=(1,),
            in_specs=[lanes] + [full((rows, half_width))] * SIDE + [ANY] * len(more),
            out_specs=lanes, scratch_shapes=[],
        ),
        out_shape=jax.ShapeDtypeStruct(within.shape, BF16),
        compiler_params=pltpu.CompilerParams(
            dimension_semantics=("arbitrary",), vmem_limit_bytes=VMEM_LIMIT
        ),
        input_output_aliases={2 + SIDE: 0} if more else {},
        cost_estimate=pl.CostEstimate(flops=LIGHT, bytes_accessed=1 << 16, transcendentals=0),
        name="final",
    )(place, within, *parts, *more)


def along(x, half, shift):
    pairs = []
    for i in range(SIDE * SIDE):
        a, b = i // SIDE, i % SIDE
        pairs.append((i, rep_of(a + shift, b) if half == 0 else rep_of(a, b + shift)))
    return lax.ppermute(x, "rep", pairs)


def shards(queries, passages, neg_device, neg_row):
    toks, width = queries.shape
    negs = neg_device.shape[1]
    groups = lax.axis_size("grp")
    reps = lax.axis_size("rep")
    cap = 8 * toks // (groups * reps)
    half_width = width // 2
    temper = 3.0 / math.sqrt(width)
    grp, rep = lax.axis_index("grp"), lax.axis_index("rep")
    place = jnp.stack([grp, rep // SIDE, rep % SIDE]).astype(I32)

    lines = jnp.pad(jnp.stack([neg_device.T, neg_row.T]), ((0, 0), (0, 8 - negs), (0, 0)))
    lines = jnp.pad(lines.reshape(16, toks), ((0, 0), (0, half_width - toks))).astype(BF16)
    sources = []
    for half in range(2):
        block = queries[:, half * half_width : (half + 1) * half_width]
        block = jnp.concatenate([block, lines], axis=0)
        sources.append([block] + [along(block, half, s) for s in range(1, SIDE)])
    gathered = lax.all_gather(passages, "grp", axis=0, tiled=True)

    first, second, ranks_first, ranks_second = ([None] * SIDE for _ in range(4))
    earlier = []
    for shift in (2, 1, 3, 0):
        one, two, ranks_first[shift], ranks_second[shift] = mid(
            place, shift, *sources, earlier, groups, reps, cap, negs
        )
        earlier = [ranks_first[shift]]
        first[shift] = along(one, 1, shift) if shift else one
        second[shift] = along(two, 0, shift) if shift else two

    within, scores = inside(place, gathered, queries, temper)
    back_first, back_second, hard_scores, codes, part = hard(
        place, first, second, gathered, within, temper, reps, cap
    )
    parts = lax.all_to_all(part, "rep", split_axis=0, concat_axis=0, tiled=True)
    high = jnp.max(parts, axis=0)
    log_total = high + jnp.log(jnp.sum(jnp.exp(parts - high), axis=0))

    partial_sum, grad_inner, losses, mark = column(
        place, codes, hard_scores, log_total, first, second, gathered, queries, scores, temper, cap
    )
    grad_passages = lax.psum_scatter(partial_sum, "grp", scatter_dimension=0, tiled=True)
    back_first = [along(v, 1, -s) if s else v for s, v in enumerate(back_first)]
    back_second = [along(v, 0, -s) if s else v for s, v in enumerate(back_second)]

    sums = []
    for half, ranks, rows in ((0, ranks_first, back_first), (1, ranks_second, back_second)):
        made = reduce(place, half, log_total, ranks, rows, mark, groups, cap)
        sums.append([along(v, half, -s) if s else v for s, v in enumerate(made)])
    grad_queries = final(place, grad_inner, sums[0], 0, temper)
    grad_queries = final(place, grad_inner, sums[1], 1, temper, grad_queries)
    return (losses.reshape(toks), grad_queries, grad_passages)


def solution(mesh):
    in_specs = (
        P(("grp", "rep"), None),
        P(("grp", "rep"), None),
        P(("grp", "rep"), None),
        P(("grp", "rep"), None),
    )
    out_specs = (P(("grp", "rep")), P(("grp", "rep"), None), P(("grp", "rep"), None))
    return jax.shard_map(shards, mesh=mesh, in_specs=in_specs, out_specs=out_specs, check_vma=False)
```
